32 devices in a mesh: dp: 8 (over z, x), fsdp: 4 (over y, core).
Axes of the slice: x: 2, y: 2, z: 4, core: 2. Of those that a mesh axis runs over, the one named last changes fastest.
Arguments:
- dec_input: bfloat16 [32, 1024, 512], P('dp', 'fsdp'), may hold values from -6 to 6
- enc_output: bfloat16 [32, 1024, 512], P('dp', 'fsdp'), may hold values from -6 to 6
- dec_lengths: int32 [32], P('dp'), may hold values from 256 to 1024, as said below
- enc_lengths: int32 [32], P('dp'), may hold values from 256 to 1024, as said below
- lang_tags: int32 [32], P('dp'), may hold values from 0 to 15
- lang_table: bfloat16 [512, 16], P(('dp', 'fsdp')), may hold values from -3 to 3
- self_in: bfloat16 [512, 1536], P(('dp', 'fsdp')), may hold values from -0.25 to 0.25
- self_out: bfloat16 [512, 512], P(('dp', 'fsdp')), may hold values from -2 to 2
- cross_q: bfloat16 [512, 512], P(('dp', 'fsdp')), may hold values from -0.25 to 0.25
- cross_kv: bfloat16 [512, 1024], P(('dp', 'fsdp')), may hold values from -0.25 to 0.25
- cross_out: bfloat16 [512, 512], P(('dp', 'fsdp')), may hold values from -2 to 2
- ffn_in: bfloat16 [512, 2048], P(('dp', 'fsdp')), may hold values from -0.25 to 0.25
- ffn_out: bfloat16 [2048, 512], P(('dp', 'fsdp')), may hold values from -0.125 to 0.125
- biases: bfloat16 [512, 7], P(('dp', 'fsdp')), may hold values from -2 to 2
- ffn_bias: bfloat16 [2048], P(('dp', 'fsdp')), may hold values from -2 to 2
- norm_gains: bfloat16 [512, 3], P(('dp', 'fsdp')), may hold values from 0.5 to 1.5
- norm_shifts: bfloat16 [512, 3], P(('dp', 'fsdp')), may hold values from -2 to 2
- cotangent: float32 [32, 1024, 512], P('dp', 'fsdp'), may hold values from -6 to 6
Outputs:
- output: bfloat16 [32, 1024, 512], P('dp', 'fsdp')
- grad_input: float32 [32, 1024, 512], P('dp', 'fsdp')
- grad_encoder: float32 [32, 1024, 512], P('dp', 'fsdp')
- grad_lang_table: float32 [512, 16], P(('dp', 'fsdp'))
- grad_self_in: float32 [512, 1536], P(('dp', 'fsdp'))
- grad_self_out: float32 [512, 512], P(('dp', 'fsdp'))
- grad_cross_q: float32 [512, 512], P(('dp', 'fsdp'))
- grad_cross_kv: float32 [512, 1024], P(('dp', 'fsdp'))
- grad_cross_out: float32 [512, 512], P(('dp', 'fsdp'))
- grad_ffn_in: float32 [512, 2048], P(('dp', 'fsdp'))
- grad_ffn_out: float32 [2048, 512], P(('dp', 'fsdp'))
- grad_biases: float32 [512, 7], P(('dp', 'fsdp'))
- grad_ffn_bias: float32 [2048], P(('dp', 'fsdp'))
- grad_norm_gains: float32 [512, 3], P(('dp', 'fsdp'))
- grad_norm_shifts: float32 [512, 3], P(('dp', 'fsdp'))
The draws below stay inside these ranges and needn't reach their ends.
Inputs may be any that keep to these rules, and one draw needn't show every extreme that they name: `dec_lengths`: in each aligned block of 4 sequences one has length 1024. `enc_lengths`: in each aligned block of 4 sequences one has length 1024.
All inputs are finite; a program needn't handle non-finite values.
Results may differ from the reference program's by a relative error of at most 0.022.
The reference program's roundings to bfloat16 on the way count: a program that leaves them out, or rounds other values in their place, can miss the bound.
Values may be sent and summed in bfloat16 or wider, within the bound.
A program may use at most 320 MiB of HBM per device.

```python
import math
import jax
import jax.numpy as jnp
from jax import lax

D = 512
FF = 2048
HEADS = 8
HDIM = 64
LANGS = 16
LEN = 1024
ELEN = 1024
SEQ_GRP = 4
SEQS = 32


def ragged_lengths(key, longest):
    sub_keys = jax.random.split(key, 2)
    drawn_len = jax.random.randint(sub_keys[0], (SEQS,), longest // 4, longest + 1)
    chosen = jax.random.randint(sub_keys[1], (SEQS // SEQ_GRP, 1), 0, SEQ_GRP)
    marked = (jnp.arange(SEQ_GRP)[None, :] == chosen).reshape(SEQS)
    return jnp.where(marked, longest, drawn_len).astype(jnp.int32)


def draw_dec_lengths(key, part):
    key = jax.random.fold_in(key, 11)
    return ragged_lengths(key, LEN)


def draw_enc_lengths(key, part):
    key = jax.random.fold_in(key, 12)
    return ragged_lengths(key, ELEN)


def plant(values, stream_key, low, high):
    spot = [jax.random.randint(jax.random.fold_in(stream_key, axis), (), 0, length) for axis, length in enumerate(values.shape)]
    widest = values.shape.index(max(values.shape))
    beside = spot[:widest] + [(spot[widest] + 1) % values.shape[widest]] + spot[widest + 1:]
    return values.at[tuple(spot)].set(low).at[tuple(beside)].set(high)


def steps_of(stream_key, extent, pieces, least, top_value):
    level, own = 1.0, jax.random.fold_in(stream_key, 6)
    for axis_at, shards_of in pieces:
        heights = jnp.exp(jax.random.uniform(jax.random.fold_in(own, axis_at), (shards_of,), jnp.float32, least / len(pieces), top_value / len(pieces)))
        level = level * jnp.repeat(heights, extent[axis_at] // shards_of).reshape([-1 if axis == axis_at else 1 for axis in range(len(extent))])
    return level


def bell_draw(key, shape, width, most, shards=(), held_as=jnp.bfloat16):
    drawn = width * jax.random.normal(key, shape, jnp.float32)
    if shards:
        drawn = drawn * steps_of(key, shape, shards, -0.22, 0.18)
    return jnp.clip(drawn, -most, most).astype(held_as)


def setup_inputs(seed: int = 0) -> dict:
    arg_keys = jax.random.split(jax.random.key(seed), 19)
    dec_input = bell_draw(arg_keys[0], (SEQS, LEN, D), 1.0, 6.0, ((0, 8), (1, 4)))
    enc_output = bell_draw(arg_keys[1], (SEQS, ELEN, D), 1.0, 6.0, ((0, 8), (1, 4)))
    dec_lengths = draw_dec_lengths(jax.random.fold_in(arg_keys[18], 71), 0)
    enc_lengths = draw_enc_lengths(jax.random.fold_in(arg_keys[18], 71), 0)
    lang_tags = plant(jax.random.randint(arg_keys[4], (SEQS,), 0, LANGS), jax.random.fold_in(arg_keys[4], 1), 0, LANGS - 1).astype(jnp.int32)
    lang_table = bell_draw(arg_keys[5], (D, LANGS), 0.5, 3.0, ((0, 32),))
    self_in = bell_draw(arg_keys[6], (D, 3 * D), D ** -0.5, 0.25, ((0, 32),))
    self_out = bell_draw(arg_keys[7], (D, D), (D // 64) ** -0.5, 2.0, ((0, 32),))
    cross_q = bell_draw(arg_keys[8], (D, D), D ** -0.5, 0.25, ((0, 32),))
    cross_kv = bell_draw(arg_keys[9], (D, 2 * D), D ** -0.5, 0.25, ((0, 32),))
    cross_out = bell_draw(arg_keys[10], (D, D), (D // 64) ** -0.5, 2.0, ((0, 32),))
    ffn_in = bell_draw(arg_keys[11], (D, FF), D ** -0.5, 0.25, ((0, 32),))
    ffn_out = bell_draw(arg_keys[12], (FF, D), FF ** -0.5, 0.125, ((0, 32),))
    biases = bell_draw(arg_keys[13], (D, 7), 0.3, 2.0, ((0, 32),))
    ffn_bias = bell_draw(arg_keys[14], (FF,), 0.3, 2.0, ((0, 32),))
    norm_gains = jnp.clip(1.0 + 0.1 * jax.random.normal(arg_keys[15], (D, 3), jnp.float32), 0.5, 1.5).astype(jnp.bfloat16)
    norm_shifts = bell_draw(arg_keys[16], (D, 3), 0.3, 2.0, ((0, 32),))
    cotangent = bell_draw(arg_keys[17], (SEQS, LEN, D), 1.0, 6.0, ((0, 8), (1, 4)), jnp.float32)
    return {"dec_input": dec_input, "enc_output": enc_output, "dec_lengths": dec_lengths, "enc_lengths": enc_lengths, "lang_tags": lang_tags, "lang_table": lang_table, "self_in": self_in, "self_out": self_out, "cross_q": cross_q, "cross_kv": cross_kv, "cross_out": cross_out, "ffn_in": ffn_in, "ffn_out": ffn_out, "biases": biases, "ffn_bias": ffn_bias, "norm_gains": norm_gains, "norm_shifts": norm_shifts, "cotangent": cotangent}


@jax.custom_vjp
def low(v):
    return lax.optimization_barrier(v.astype(jnp.bfloat16)).astype(jnp.float32)

@jax.custom_vjp
def low_back(v):
    return v

def low_keep(v):
    return (low(v), None)

def low_pass(kept, grad):
    return (grad,)

def back_keep(v):
    return (v, None)

def back_low(kept, grad):
    return (low(grad),)
low.defvjp(low_keep, low_pass)
low_back.defvjp(back_keep, back_low)

def matmul(left, right):
    return jnp.dot(left, right, precision=lax.Precision.HIGHEST, preferred_element_type=jnp.float32)

def smooth_gelu(values):
    return 0.5 * values * (1.0 + jnp.tanh(0.7978845608028654 * (values + 0.044715 * values * values * values)))

def normalize(residual, gain_col, shift_col):
    row_mean = lax.optimization_barrier(jnp.mean(residual, axis=-1, keepdims=True))
    centered = residual - row_mean
    variance = lax.optimization_barrier(jnp.mean(centered * centered, axis=-1, keepdims=True))
    return centered * lax.rsqrt(variance + 1e-05) * gain_col + shift_col

def attend(query, key_rows, value_rows, length):
    row_count = query.shape[0]
    key_count = key_rows.shape[0]
    query_heads = query.reshape(row_count, HEADS, HDIM)
    key_heads = key_rows.reshape(key_count, HEADS, HDIM)
    value_heads = value_rows.reshape(key_count, HEADS, HDIM)
    scores = jnp.einsum('qhd,khd->hqk', query_heads, key_heads, precision=lax.Precision.HIGHEST) * (1.0 / math.sqrt(HDIM))
    key_valid = jnp.arange(key_count) < length
    scores = jnp.where(key_valid[None, None, :], scores, -1000000000.0)
    scores = low_back(scores)
    row_max = lax.optimization_barrier(jnp.max(scores, axis=-1, keepdims=True))
    exp_scores = jnp.exp(scores - row_max)
    attn_probs = low(exp_scores / lax.optimization_barrier(jnp.sum(exp_scores, axis=-1, keepdims=True)))
    attn_mixed = jnp.einsum('hqk,khd->qhd', attn_probs, value_heads, precision=lax.Precision.HIGHEST)
    return low(low_back(attn_mixed.reshape(row_count, HEADS * HDIM)))

def decoder_layer(params, inputs, encoded, length, enc_length, language):
    lang_table, self_in, self_out, cross_q, cross_kv, cross_out, ffn_in, ffn_out, biases, ffn_bias, gains, shifts = params
    zeros_row = jnp.zeros((D,), jnp.float32)
    choose = (jnp.arange(LANGS) == language).astype(jnp.float32)
    shifted = inputs + lax.optimization_barrier(jnp.sum(lang_table * choose[None, :], axis=1))[None, :]
    merged = matmul(low(shifted), self_in) + jnp.concatenate([biases[:, 0], zeros_row, biases[:, 1]])[None, :]
    merged = low(low_back(merged))
    attn_mixed = attend(merged[:, :D], merged[:, D:2 * D], merged[:, 2 * D:], length)
    branch = low_back(matmul(attn_mixed, self_out) + biases[:, 2])
    normed_one = normalize(shifted + branch, gains[:, 0], shifts[:, 0])
    cross_query = low(low_back(matmul(low(normed_one), cross_q) + biases[:, 3]))
    cross_pair = matmul(encoded, cross_kv) + jnp.concatenate([zeros_row, biases[:, 4]])[None, :]
    cross_pair = low(low_back(cross_pair))
    cross_mixed = attend(cross_query, cross_pair[:, :D], cross_pair[:, D:], enc_length)
    cross_branch = low_back(matmul(cross_mixed, cross_out) + biases[:, 5])
    normed_two = normalize(normed_one + cross_branch, gains[:, 1], shifts[:, 1])
    hidden = low_back(matmul(low(normed_two), ffn_in) + ffn_bias)
    activated = low(smooth_gelu(hidden))
    ffn_branch = low_back(matmul(activated, ffn_out) + biases[:, 6])
    normed_three = normalize(normed_two + ffn_branch, gains[:, 2], shifts[:, 2])
    live_rows = (jnp.arange(LEN) < length).astype(jnp.float32)
    return normed_three * live_rows[:, None]

def reference(dec_input, enc_output, dec_lengths, enc_lengths, lang_tags, lang_table, self_in, self_out, cross_q, cross_kv, cross_out, ffn_in, ffn_out, biases, ffn_bias, norm_gains, norm_shifts, cotangent):
    params = tuple((weight.astype(jnp.float32) for weight in (lang_table, self_in, self_out, cross_q, cross_kv, cross_out, ffn_in, ffn_out, biases, ffn_bias, norm_gains, norm_shifts)))

    def forward(weights, inputs, encoded):
        layer_fn = jax.checkpoint(decoder_layer)

        def per_sequence(unused, sliced):
            seq_in, seq_enc, seq_len, seq_elen, seq_tag = sliced
            return (unused, layer_fn(weights, seq_in, seq_enc, seq_len, seq_elen, seq_tag))
        unused, stacked = lax.scan(per_sequence, jnp.zeros((), jnp.float32), (inputs, encoded, dec_lengths, enc_lengths, lang_tags))
        return stacked
    result, pullback = jax.vjp(forward, params, dec_input.astype(jnp.float32), enc_output.astype(jnp.float32))
    gradients = pullback(cotangent)
    weight_grads = gradients[0]
    return (result.astype(jnp.bfloat16), gradients[1], gradients[2], weight_grads[0], weight_grads[1], weight_grads[2], weight_grads[3], weight_grads[4], weight_grads[5], weight_grads[6], weight_grads[7], weight_grads[8], weight_grads[9], weight_grads[10], weight_grads[11])
```

```python
import functools
import math

import jax
import jax.numpy as jnp
from jax import lax
from jax.experimental import pallas as pl
from jax.experimental.pallas import tpu as pltpu
from jax.sharding import PartitionSpec as P

HEADS = 8


def smooth_gelu(values):
    return (
        0.5
        * values
        * (1.0 + jnp.tanh(0.7978845608028654 * (values + 0.044715 * values * values * values)))
    )


def times_t(left, right):
    return lax.dot_general(
        left, right, (((1,), (1,)), ((), ())), preferred_element_type=jnp.float32
    )


def outer_sum(left, right):
    return lax.dot_general(
        left, right, (((0,), (0,)), ((), ())), preferred_element_type=jnp.float32
    )


def normalize_rows(residual, gain_col, shift_col):
    row_mean = jnp.mean(residual, axis=-1, keepdims=True)
    centered = residual - row_mean
    inv_dev = lax.rsqrt(jnp.mean(centered * centered, axis=-1, keepdims=True) + 1e-05)
    unit_rows = centered * inv_dev
    return (unit_rows * gain_col + shift_col, unit_rows, inv_dev)


def normalize_back(grad_above, unit_rows, inv_dev, gain_col):
    grad_unit = grad_above * gain_col
    grad_res = inv_dev * (
        grad_unit
        - jnp.mean(grad_unit, axis=-1, keepdims=True)
        - unit_rows * jnp.mean(grad_unit * unit_rows, axis=-1, keepdims=True)
    )
    return (grad_res, jnp.sum(grad_above * unit_rows, axis=0), jnp.sum(grad_above, axis=0))


def masked_scores(query_bf, key_full, lengths_here):
    groups, rows_here, features = query_bf.shape
    key_count = key_full.shape[1]
    head_size = features // HEADS
    query_heads = query_bf.reshape(groups, rows_here, HEADS, head_size)
    key_heads = key_full.reshape(groups, key_count, HEADS, head_size)
    scores = jnp.einsum(
        "sqhd,skhd->shqk", query_heads, key_heads, preferred_element_type=jnp.float32
    ) * (1.0 / math.sqrt(head_size))
    key_valid = jnp.arange(key_count)[None, :] < lengths_here[:, None]
    return jnp.where(key_valid[:, None, None, :], scores, -1000000000.0)


def attend_forward(query_bf, key_full, value_full, lengths_here):
    groups, rows_here, features = query_bf.shape
    key_count = key_full.shape[1]
    value_heads = value_full.reshape(groups, key_count, HEADS, features // HEADS)
    scores = masked_scores(query_bf, key_full, lengths_here)
    row_max = jnp.max(scores, axis=-1, keepdims=True)
    exp_scores = jnp.exp(scores - row_max)
    row_total = jnp.sum(exp_scores, axis=-1, keepdims=True)
    probs_bf = (exp_scores / row_total).astype(jnp.bfloat16)
    attn_mixed = jnp.einsum(
        "shqk,skhd->sqhd", probs_bf, value_heads, preferred_element_type=jnp.float32
    )
    return (attn_mixed.reshape(groups, rows_here, features), row_max + jnp.log(row_total))


def attend_back(grad_mixed_bf, query_bf, key_full, value_full, lengths_here, log_total):
    groups, rows_here, features = query_bf.shape
    key_count = key_full.shape[1]
    head_size = features // HEADS
    query_heads = query_bf.reshape(groups, rows_here, HEADS, head_size)
    key_heads = key_full.reshape(groups, key_count, HEADS, head_size)
    value_heads = value_full.reshape(groups, key_count, HEADS, head_size)
    grad_heads = grad_mixed_bf.reshape(groups, rows_here, HEADS, head_size)
    attn_probs = jnp.exp(masked_scores(query_bf, key_full, lengths_here) - log_total)
    probs_bf = attn_probs.astype(jnp.bfloat16)
    grad_probs = jnp.einsum(
        "sqhd,skhd->shqk", grad_heads, value_heads, preferred_element_type=jnp.float32
    )
    grad_values = jnp.einsum(
        "shqk,sqhd->skhd", probs_bf, grad_heads, preferred_element_type=jnp.float32
    )
    grad_scores = attn_probs * (
        grad_probs - jnp.sum(attn_probs * grad_probs, axis=-1, keepdims=True)
    )
    grad_scores_bf = grad_scores.astype(jnp.bfloat16)
    score_scale = 1.0 / math.sqrt(head_size)
    grad_query = (
        jnp.einsum("shqk,skhd->sqhd", grad_scores_bf, key_heads, preferred_element_type=jnp.float32)
        * score_scale
    )
    grad_keys = (
        jnp.einsum(
            "shqk,sqhd->skhd", grad_scores_bf, query_heads, preferred_element_type=jnp.float32
        )
        * score_scale
    )
    return (
        grad_query.reshape(groups, rows_here, features),
        grad_keys.reshape(groups, key_count, features),
        grad_values.reshape(groups, key_count, features),
    )


def body(
    dec_input,
    enc_output,
    dec_lengths,
    enc_lengths,
    lang_tags,
    lang_table,
    self_in,
    self_out,
    cross_q,
    cross_kv,
    cross_out,
    ffn_in,
    ffn_out,
    biases,
    ffn_bias,
    norm_gains,
    norm_shifts,
    cotangent,
):
    full_weights = (
        lax.all_gather(lang_table, ("dp", "fsdp"), axis=0, tiled=True),
        lax.all_gather(self_in, ("dp", "fsdp"), axis=0, tiled=True),
        lax.all_gather(self_out, ("dp", "fsdp"), axis=0, tiled=True),
        lax.all_gather(cross_q, ("dp", "fsdp"), axis=0, tiled=True),
        lax.all_gather(cross_kv, ("dp", "fsdp"), axis=0, tiled=True),
        lax.all_gather(cross_out, ("dp", "fsdp"), axis=0, tiled=True),
        lax.all_gather(ffn_in, ("dp", "fsdp"), axis=0, tiled=True),
        lax.all_gather(ffn_out, ("dp", "fsdp"), axis=0, tiled=True),
        lax.all_gather(biases, ("dp", "fsdp"), axis=0, tiled=True),
        lax.all_gather(ffn_bias, ("dp", "fsdp"), axis=0, tiled=True),
        lax.all_gather(norm_gains, ("dp", "fsdp"), axis=0, tiled=True),
        lax.all_gather(norm_shifts, ("dp", "fsdp"), axis=0, tiled=True),
    )
    (
        full_table,
        full_in,
        full_out,
        full_cq,
        full_ckv,
        full_co,
        full_ffn_in,
        full_ffn_out,
        full_biases,
        full_ffn_bias,
        full_gains,
        full_shifts,
    ) = full_weights
    bias_cols = full_biases.astype(jnp.float32)
    gain_cols = full_gains.astype(jnp.float32)
    shift_cols = full_shifts.astype(jnp.float32)
    groups, rows_here, features = dec_input.shape
    enc_rows = enc_output.shape[1]
    tokens = groups * rows_here
    positions = lax.axis_index("fsdp") * rows_here + jnp.arange(rows_here)
    live_rows = (positions[None, :] < dec_lengths[:, None]).astype(jnp.float32)
    live_flat = live_rows.reshape(tokens, 1)
    onehot = (lang_tags[:, None] == jnp.arange(full_table.shape[1])[None, :]).astype(jnp.float32)
    lang_rows = lax.dot_general(
        onehot,
        full_table.astype(jnp.float32),
        (((1,), (1,)), ((), ())),
        precision=lax.Precision.HIGHEST,
        preferred_element_type=jnp.float32,
    )
    flat_start = (dec_input.astype(jnp.float32) + lang_rows[:, None, :]).reshape(tokens, features)
    start_bf = flat_start.astype(jnp.bfloat16)
    zeros_row = jnp.zeros((features,), jnp.float32)
    merged = (
        jnp.dot(start_bf, full_in, preferred_element_type=jnp.float32)
        + jnp.concatenate([bias_cols[:, 0], zeros_row, bias_cols[:, 1]])[None, :]
    )
    merged_bf = merged.astype(jnp.bfloat16).reshape(groups, rows_here, 3 * features)
    query_bf = merged_bf[:, :, :features]
    key_own = merged_bf[:, :, features : 2 * features]
    value_own = merged_bf[:, :, 2 * features :]
    key_full, value_full = (
        lax.all_gather(key_own, "fsdp", axis=1, tiled=True),
        lax.all_gather(value_own, "fsdp", axis=1, tiled=True),
    )
    attn_mixed, self_lse = attend_forward(query_bf, key_full, value_full, dec_lengths)
    mixed_bf = attn_mixed.astype(jnp.bfloat16).reshape(tokens, features)
    branch = jnp.dot(mixed_bf, full_out, preferred_element_type=jnp.float32) + bias_cols[:, 2]
    normed_one, unit_one, inv_one = normalize_rows(
        flat_start + branch, gain_cols[:, 0], shift_cols[:, 0]
    )
    one_bf = normed_one.astype(jnp.bfloat16)
    cross_query = (
        (jnp.dot(one_bf, full_cq, preferred_element_type=jnp.float32) + bias_cols[:, 3])
        .astype(jnp.bfloat16)
        .reshape(groups, rows_here, features)
    )
    enc_flat = enc_output.reshape(groups * enc_rows, features)
    cross_pair = (
        jnp.dot(enc_flat, full_ckv, preferred_element_type=jnp.float32)
        + jnp.concatenate([zeros_row, bias_cols[:, 4]])[None, :]
    )
    pair_bf = cross_pair.astype(jnp.bfloat16).reshape(groups, enc_rows, 2 * features)
    ckey_own = pair_bf[:, :, :features]
    cvalue_own = pair_bf[:, :, features:]
    ckey_full, cvalue_full = (
        lax.all_gather(ckey_own, "fsdp", axis=1, tiled=True),
        lax.all_gather(cvalue_own, "fsdp", axis=1, tiled=True),
    )
    cross_mixed, cross_lse = attend_forward(cross_query, ckey_full, cvalue_full, enc_lengths)
    cmixed_bf = cross_mixed.astype(jnp.bfloat16).reshape(tokens, features)
    cross_branch = jnp.dot(cmixed_bf, full_co, preferred_element_type=jnp.float32) + bias_cols[:, 5]
    normed_two, unit_two, inv_two = normalize_rows(
        normed_one + cross_branch, gain_cols[:, 1], shift_cols[:, 1]
    )
    two_bf = normed_two.astype(jnp.bfloat16)
    hidden = jnp.dot(
        two_bf, full_ffn_in, preferred_element_type=jnp.float32
    ) + full_ffn_bias.astype(jnp.float32)
    activated, gelu_pull = jax.vjp(smooth_gelu, hidden)
    act_bf = activated.astype(jnp.bfloat16)
    ffn_branch = jnp.dot(act_bf, full_ffn_out, preferred_element_type=jnp.float32) + bias_cols[:, 6]
    normed_three, unit_three, inv_three = normalize_rows(
        normed_two + ffn_branch, gain_cols[:, 2], shift_cols[:, 2]
    )
    output = (normed_three * live_flat).astype(jnp.bfloat16).reshape(groups, rows_here, features)
    back_weights = (
        lax.all_gather(lang_table, ("dp", "fsdp"), axis=0, tiled=True),
        lax.all_gather(self_in, ("dp", "fsdp"), axis=0, tiled=True),
        lax.all_gather(self_out, ("dp", "fsdp"), axis=0, tiled=True),
        lax.all_gather(cross_q, ("dp", "fsdp"), axis=0, tiled=True),
        lax.all_gather(cross_kv, ("dp", "fsdp"), axis=0, tiled=True),
        lax.all_gather(cross_out, ("dp", "fsdp"), axis=0, tiled=True),
        lax.all_gather(ffn_in, ("dp", "fsdp"), axis=0, tiled=True),
        lax.all_gather(ffn_out, ("dp", "fsdp"), axis=0, tiled=True),
        lax.all_gather(biases, ("dp", "fsdp"), axis=0, tiled=True),
        lax.all_gather(ffn_bias, ("dp", "fsdp"), axis=0, tiled=True),
        lax.all_gather(norm_gains, ("dp", "fsdp"), axis=0, tiled=True),
        lax.all_gather(norm_shifts, ("dp", "fsdp"), axis=0, tiled=True),
    )
    back_in = back_weights[1]
    back_out = back_weights[2]
    back_cq = back_weights[3]
    back_ckv = back_weights[4]
    back_co = back_weights[5]
    back_ffn_in = back_weights[6]
    back_ffn_out = back_weights[7]
    back_gains = back_weights[10].astype(jnp.float32)
    grad_above = cotangent.reshape(tokens, features) * live_flat
    grad_res3, gain_three, shift_three = normalize_back(
        grad_above, unit_three, inv_three, back_gains[:, 2]
    )
    grad_low3 = grad_res3.astype(jnp.bfloat16)
    grad_ffn_out = outer_sum(act_bf, grad_low3)
    bias_six = jnp.sum(grad_low3.astype(jnp.float32), axis=0)
    grad_act = times_t(grad_low3, back_ffn_out)
    grad_hidden_bf = gelu_pull(grad_act)[0].astype(jnp.bfloat16)
    grad_ffn_in = outer_sum(two_bf, grad_hidden_bf)
    grad_ffn_bias = jnp.sum(grad_hidden_bf.astype(jnp.float32), axis=0)
    grad_two = grad_res3 + times_t(grad_hidden_bf, back_ffn_in)
    grad_res2, gain_two, shift_two = normalize_back(grad_two, unit_two, inv_two, back_gains[:, 1])
    grad_low2 = grad_res2.astype(jnp.bfloat16)
    grad_cross_out = outer_sum(cmixed_bf, grad_low2)
    bias_five = jnp.sum(grad_low2.astype(jnp.float32), axis=0)
    grad_cmixed = (
        times_t(grad_low2, back_co).astype(jnp.bfloat16).reshape(groups, rows_here, features)
    )
    grad_cquery, grad_ckey, grad_cvalue = attend_back(
        grad_cmixed, cross_query, ckey_full, cvalue_full, enc_lengths, cross_lse
    )
    ckey_sum, cvalue_sum = (
        lax.psum_scatter(
            grad_ckey.astype(jnp.bfloat16), "fsdp", scatter_dimension=1, tiled=True
        ).astype(jnp.float32),
        lax.psum_scatter(
            grad_cvalue.astype(jnp.bfloat16), "fsdp", scatter_dimension=1, tiled=True
        ).astype(jnp.float32),
    )
    grad_pair_bf = (
        jnp.concatenate([ckey_sum, cvalue_sum], axis=-1)
        .astype(jnp.bfloat16)
        .reshape(groups * enc_rows, 2 * features)
    )
    grad_cross_kv = outer_sum(enc_flat, grad_pair_bf)
    bias_four = jnp.sum(grad_pair_bf[:, features:].astype(jnp.float32), axis=0)
    grad_encoder = times_t(grad_pair_bf, back_ckv).reshape(groups, enc_rows, features)
    grad_cquery_bf = grad_cquery.astype(jnp.bfloat16).reshape(tokens, features)
    grad_cross_q = outer_sum(one_bf, grad_cquery_bf)
    bias_three = jnp.sum(grad_cquery_bf.astype(jnp.float32), axis=0)
    grad_one = grad_res2 + times_t(grad_cquery_bf, back_cq)
    grad_res1, gain_one, shift_one = normalize_back(grad_one, unit_one, inv_one, back_gains[:, 0])
    grad_low1 = grad_res1.astype(jnp.bfloat16)
    grad_self_out = outer_sum(mixed_bf, grad_low1)
    bias_two = jnp.sum(grad_low1.astype(jnp.float32), axis=0)
    grad_mixed = (
        times_t(grad_low1, back_out).astype(jnp.bfloat16).reshape(groups, rows_here, features)
    )
    grad_query, grad_key, grad_value = attend_back(
        grad_mixed, query_bf, key_full, value_full, dec_lengths, self_lse
    )
    key_sum, value_sum = (
        lax.psum_scatter(
            grad_key.astype(jnp.bfloat16), "fsdp", scatter_dimension=1, tiled=True
        ).astype(jnp.float32),
        lax.psum_scatter(
            grad_value.astype(jnp.bfloat16), "fsdp", scatter_dimension=1, tiled=True
        ).astype(jnp.float32),
    )
    grad_merged_bf = (
        jnp.concatenate([grad_query, key_sum, value_sum], axis=-1)
        .astype(jnp.bfloat16)
        .reshape(tokens, 3 * features)
    )
    grad_self_in = outer_sum(start_bf, grad_merged_bf)
    merged_sums = jnp.sum(grad_merged_bf.astype(jnp.float32), axis=0)
    grad_start = grad_res1 + times_t(grad_merged_bf, back_in)
    grad_input = grad_start.reshape(groups, rows_here, features)
    seq_sums = jnp.sum(grad_input, axis=1)
    grad_table = lax.dot_general(
        seq_sums,
        onehot,
        (((0,), (0,)), ((), ())),
        precision=lax.Precision.HIGHEST,
        preferred_element_type=jnp.float32,
    )
    grad_biases = jnp.stack(
        [
            merged_sums[:features],
            merged_sums[2 * features :],
            bias_two,
            bias_three,
            bias_four,
            bias_five,
            bias_six,
        ],
        axis=1,
    )
    grad_gains = jnp.stack([gain_one, gain_two, gain_three], axis=1)
    grad_shifts = jnp.stack([shift_one, shift_two, shift_three], axis=1)
    reduced = (
        lax.psum_scatter(grad_table, ("dp", "fsdp"), scatter_dimension=0, tiled=True),
        lax.psum_scatter(grad_self_in, ("dp", "fsdp"), scatter_dimension=0, tiled=True),
        lax.psum_scatter(grad_self_out, ("dp", "fsdp"), scatter_dimension=0, tiled=True),
        lax.psum_scatter(grad_cross_q, ("dp", "fsdp"), scatter_dimension=0, tiled=True),
        lax.psum_scatter(grad_cross_kv, ("dp", "fsdp"), scatter_dimension=0, tiled=True),
        lax.psum_scatter(grad_cross_out, ("dp", "fsdp"), scatter_dimension=0, tiled=True),
        lax.psum_scatter(grad_ffn_in, ("dp", "fsdp"), scatter_dimension=0, tiled=True),
        lax.psum_scatter(grad_ffn_out, ("dp", "fsdp"), scatter_dimension=0, tiled=True),
        lax.psum_scatter(grad_biases, ("dp", "fsdp"), scatter_dimension=0, tiled=True),
        lax.psum_scatter(grad_ffn_bias, ("dp", "fsdp"), scatter_dimension=0, tiled=True),
        lax.psum_scatter(grad_gains, ("dp", "fsdp"), scatter_dimension=0, tiled=True),
        lax.psum_scatter(grad_shifts, ("dp", "fsdp"), scatter_dimension=0, tiled=True),
    )
    return (
        output,
        grad_input,
        grad_encoder,
        reduced[0],
        reduced[1],
        reduced[2],
        reduced[3],
        reduced[4],
        reduced[5],
        reduced[6],
        reduced[7],
        reduced[8],
        reduced[9],
        reduced[10],
        reduced[11],
    )


F32 = jnp.float32
BF16 = jnp.bfloat16


def nt_dot(left, right):
    return lax.dot_general(left, right, (((1,), (1,)), ((), ())), preferred_element_type=F32)


def nn_dot(left, right):
    return jnp.dot(left, right, preferred_element_type=F32)


def split_three(value):
    high = value.astype(BF16)
    rest = value - high.astype(F32)
    middle = rest.astype(BF16)
    return high, middle, (rest - middle.astype(F32)).astype(BF16)


def key_extra(tokens, length):
    lane = lax.broadcasted_iota(jnp.int32, (tokens, 128), 1) % 64
    row = lax.broadcasted_iota(jnp.int32, (tokens, 128), 0)
    masked = jnp.where(row < length, 0.0, -1e30)
    return jnp.where(lane == 3, masked, jnp.where(lane < 3, 1.0, 0.0)).astype(BF16)


def row_extra(lane, head, terms, mask_lane):
    base = head * 64
    out = jnp.where(lane == base + 3, mask_lane, 0.0).astype(F32)
    for place, term in enumerate(terms):
        out = jnp.where(lane == base + place, term.astype(F32), out)
    return out.astype(BF16)


def attend_fwd_core(block, length, q_ref, k_ref, v_ref, o_ref, of_ref, lse_ref, kx_ref, va_ref, vb_ref):
    tokens = q_ref.shape[0]
    kx_ref[:, :128] = k_ref[...]
    kx_ref[:, 128:] = key_extra(tokens, length)
    lane_full = lax.broadcasted_iota(jnp.int32, (tokens, 128), 1)
    values = v_ref[...].astype(F32)
    va_ref[...] = jnp.where(lane_full < 64, values, 1.0).astype(BF16)
    vb_ref[...] = jnp.where(lane_full < 64, 1.0, values).astype(BF16)

    def step(index, carry):
        rows = pl.ds(pl.multiple_of(index * block, block), block)
        lane = lax.broadcasted_iota(jnp.int32, (block, 128), 1)
        query = q_ref[rows, :].astype(F32) * 0.125
        halves, tops = [], []
        for head, vx_ref in enumerate((va_ref, vb_ref)):
            inside = (lane < 64) if head == 0 else (lane >= 64)
            own = jnp.where(inside, query, 0.0).astype(BF16)
            extra = row_extra(lane, head, (), 1.0)
            scores = nt_dot(jnp.concatenate([own, extra], axis=1), kx_ref[...])
            top = jnp.max(scores, axis=1, keepdims=True)
            probs = jnp.exp(scores - top).astype(BF16)
            halves.append(nn_dot(probs, vx_ref[...]))
            tops.append(top)
        number = jnp.where(lane < 64, halves[0], halves[1])
        total = pltpu.roll(jnp.where(lane < 64, halves[1], halves[0]), 64, 1)
        out = number / total
        o_ref[rows, :] = out.astype(BF16)
        of_ref[rows, :] = out
        lse_ref[rows, :] = jnp.where(lane < 64, tops[0], tops[1]) + jnp.log(total)
        return carry

    lax.fori_loop(0, tokens // block, step, 0)


def attend_fwd_kernel(block, length_ref, *refs):
    attend_fwd_core(block, length_ref[0], *refs)


def attend_bwd_kernel(
    block, length_ref, q_ref, k_ref, v_ref, do_ref, of_ref, lse_ref, dq_ref, dk_ref, dv_ref,
    kx_ref, vx_ref, kt_ref, dk_acc, dv_acc,
):
    tokens = q_ref.shape[0]
    length = length_ref[0]
    extra_keys = key_extra(tokens, length)
    kx_ref[:, :128] = k_ref[...]
    kx_ref[:, 128:] = extra_keys
    vx_ref[:, :128] = v_ref[...]
    vx_ref[:, 128:] = extra_keys
    turned = k_ref[...].astype(F32).T
    sub = lax.broadcasted_iota(jnp.int32, (128, tokens), 0)
    kt_ref[0] = jnp.where(sub < 64, turned, 0.0).astype(BF16)
    kt_ref[1] = jnp.where(sub < 64, 0.0, turned).astype(BF16)
    dk_acc[...] = jnp.zeros_like(dk_acc)
    dv_acc[...] = jnp.zeros_like(dv_acc)
    same = (
        lax.broadcasted_iota(jnp.int32, (128, 128), 0) // 64
        == lax.broadcasted_iota(jnp.int32, (128, 128), 1) // 64
    ).astype(F32).astype(BF16)

    def step(index, carry):
        rows = pl.ds(pl.multiple_of(index * block, block), block)
        lane = lax.broadcasted_iota(jnp.int32, (block, 128), 1)
        query = q_ref[rows, :].astype(F32) * 0.125
        grad = do_ref[rows, :].astype(F32)
        inner = grad * of_ref[rows, :]
        inner_high = inner.astype(BF16)
        inner_low = (inner - inner_high.astype(F32)).astype(BF16)
        delta = nn_dot(inner_high, same) + nn_dot(inner_low, same)
        lse_terms = split_three(-lse_ref[rows, :])
        delta_terms = split_three(-delta)
        dq_t = jnp.zeros((128, block), F32)
        for head in range(2):
            inside = (lane < 64) if head == 0 else (lane >= 64)
            own_q = jnp.where(inside, query, 0.0).astype(BF16)
            own_g = jnp.where(inside, grad, 0.0).astype(BF16)
            left_q = jnp.concatenate([own_q, row_extra(lane, head, lse_terms, 1.0)], axis=1)
            left_g = jnp.concatenate([own_g, row_extra(lane, head, delta_terms, 0.0)], axis=1)
            probs = jnp.exp(nt_dot(kx_ref[...], left_q))
            dscore = (probs * nt_dot(vx_ref[...], left_g)).astype(BF16)
            dv_acc[...] += nn_dot(probs.astype(BF16), own_g)
            dk_acc[...] += nn_dot(dscore, own_q)
            dq_t = dq_t + nn_dot(kt_ref[head], dscore)
        dq_ref[rows, :] = (dq_t.T * 0.125).astype(BF16)
        return carry

    lax.fori_loop(0, tokens // block, step, 0)
    dk_ref[...] = dk_acc[...].astype(BF16)
    dv_ref[...] = dv_acc[...].astype(BF16)


BIG = pltpu.CompilerParams(vmem_limit_bytes=56 * 1024 * 1024)
SMEM_SPEC = pl.BlockSpec(memory_space=pltpu.SMEM)


def column_block(tokens, offset):
    return pl.BlockSpec((tokens, 128), lambda pair: (0, pair + offset))


def attend_fwd(q_array, q_at, kv_array, k_at, v_at, length):
    tokens = q_array.shape[0]
    features = HEADS * 64
    out_block = column_block(tokens, 0)
    return pl.pallas_call(
        functools.partial(attend_fwd_kernel, 256),
        grid=(HEADS // 2,),
        in_specs=[SMEM_SPEC, column_block(tokens, q_at), column_block(tokens, k_at), column_block(tokens, v_at)],
        out_specs=[out_block] * 3,
        out_shape=[jax.ShapeDtypeStruct((tokens, features), t) for t in (BF16, F32, F32)],
        scratch_shapes=[pltpu.VMEM((tokens, 256), BF16), pltpu.VMEM((tokens, 128), BF16), pltpu.VMEM((tokens, 128), BF16)],
        compiler_params=BIG,
        name="attend_fwd",
    )(length, q_array, kv_array, kv_array)


def attend_bwd(q_array, q_at, kv_array, k_at, v_at, grad, out_f32, lse, length):
    tokens = q_array.shape[0]
    features = HEADS * 64
    own = column_block(tokens, 0)
    return pl.pallas_call(
        functools.partial(attend_bwd_kernel, 256),
        grid=(HEADS // 2,),
        in_specs=[SMEM_SPEC, column_block(tokens, q_at), column_block(tokens, k_at), column_block(tokens, v_at), own, own, own],
        out_specs=[own] * 3,
        out_shape=[jax.ShapeDtypeStruct((tokens, features), BF16)] * 3,
        scratch_shapes=[
            pltpu.VMEM((tokens, 256), BF16),
            pltpu.VMEM((tokens, 256), BF16),
            pltpu.VMEM((2, 128, tokens), BF16),
            pltpu.VMEM((tokens, 128), F32),
            pltpu.VMEM((tokens, 128), F32),
        ],
        compiler_params=BIG,
        name="attend_bwd",
    )(length, q_array, kv_array, kv_array, grad, out_f32, lse)


def row_stats(residual):
    mean = jnp.mean(residual, axis=1, keepdims=True)
    centered = residual - mean
    inv = lax.rsqrt(jnp.mean(centered * centered, axis=1, keepdims=True) + 1e-05)
    return centered * inv, inv


def norm_back(above, unit, inv, gain):
    scaled = above * gain
    return inv * (
        scaled
        - jnp.mean(scaled, axis=1, keepdims=True)
        - unit * jnp.mean(scaled * unit, axis=1, keepdims=True)
    )


def col_sum(value):
    return jnp.sum(value, axis=0, keepdims=True)


def vec(vec_ref, index):
    return vec_ref[pl.ds(index, 1), :]


LANG_ROW = 13


def project_kernel(x_ref, enc_ref, win_ref, wkv_ref, vec_ref, low_ref, merged_ref, pair_ref):
    features = x_ref.shape[1]
    low = (x_ref[...].astype(F32) + vec(vec_ref, LANG_ROW)).astype(BF16)
    low_ref[...] = low
    for part, bias in ((0, 0), (1, None), (2, 1)):
        cols = pl.ds(part * features, features)
        out = nn_dot(low, win_ref[:, cols])
        merged_ref[:, cols] = (out if bias is None else out + vec(vec_ref, bias)).astype(BF16)
    for part, bias in ((0, None), (1, 4)):
        cols = pl.ds(part * features, features)
        out = nn_dot(enc_ref[...], wkv_ref[:, cols])
        pair_ref[:, cols] = (out if bias is None else out + vec(vec_ref, bias)).astype(BF16)


def middle_kernel(x_ref, mixed_ref, wout_ref, wcq_ref, vec_ref, unit_ref, inv_ref, one_ref, cq_ref):
    branch = nn_dot(mixed_ref[...], wout_ref[...]) + vec(vec_ref, 2)
    unit, inv = row_stats(x_ref[...].astype(F32) + vec(vec_ref, LANG_ROW) + branch)
    unit_ref[...] = unit
    inv_ref[...] = jnp.broadcast_to(inv, inv_ref.shape)
    one = (unit * vec(vec_ref, 7) + vec(vec_ref, 10)).astype(BF16)
    one_ref[...] = one
    cq_ref[...] = (nn_dot(one, wcq_ref[...]) + vec(vec_ref, 3)).astype(BF16)


def ffn_kernel(
    length_ref, cmixed_ref, unit_ref, cot_ref, wco_ref, win_ref, wout_ref, vec_ref, fbias_ref,
    out_ref, act_ref, low3_ref, two_ref, ghid_ref, res2_ref, low2_ref, gcm_ref, sums_ref, fsum_ref,
):
    step = pl.program_id(0)
    rows = cmixed_ref.shape[0]

    @pl.when(step == 0)
    def _():
        sums_ref[...] = jnp.zeros_like(sums_ref)
        fsum_ref[...] = jnp.zeros_like(fsum_ref)

    normed_one = unit_ref[...] * vec(vec_ref, 7) + vec(vec_ref, 10)
    branch = nn_dot(cmixed_ref[...], wco_ref[...]) + vec(vec_ref, 5)
    unit2, inv2 = row_stats(normed_one + branch)
    gain2 = vec(vec_ref, 8)
    normed_two = unit2 * gain2 + vec(vec_ref, 11)
    two = normed_two.astype(BF16)
    two_ref[...] = two
    hidden = nn_dot(two, win_ref[...]) + fbias_ref[...]
    square = hidden * hidden
    tanh = jnp.tanh(0.7978845608028654 * (hidden + 0.044715 * square * hidden))
    half = 0.5 * (1.0 + tanh)
    act = (hidden * half).astype(BF16)
    act_ref[...] = act
    slope = half + (0.5 * 0.7978845608028654) * hidden * (1.0 - tanh * tanh) * (1.0 + 3 * 0.044715 * square)
    unit3, inv3 = row_stats(normed_two + nn_dot(act, wout_ref[...]) + vec(vec_ref, 6))
    gain3 = vec(vec_ref, 9)
    live = (lax.broadcasted_iota(jnp.int32, (rows, 1), 0) + step * rows < length_ref[0]).astype(F32)
    out_ref[...] = ((unit3 * gain3 + vec(vec_ref, 12)) * live).astype(BF16)
    above3 = cot_ref[...].astype(F32) * live
    res3 = norm_back(above3, unit3, inv3, gain3)
    low3 = res3.astype(BF16)
    low3_ref[...] = low3
    ghid = (nt_dot(low3, wout_ref[...]) * slope).astype(BF16)
    ghid_ref[...] = ghid
    above2 = res3 + nt_dot(ghid, win_ref[...])
    res2 = norm_back(above2, unit2, inv2, gain2)
    res2_ref[...] = res2
    low2 = res2.astype(BF16)
    low2_ref[...] = low2
    gcm_ref[...] = nt_dot(low2, wco_ref[...]).astype(BF16)
    for index, value in (
        (6, low3.astype(F32)), (5, low2.astype(F32)), (9, above3 * unit3), (12, above3), (8, above2 * unit2), (11, above2),
    ):
        sums_ref[index : index + 1, :] += col_sum(value)
    fsum_ref[...] += col_sum(ghid.astype(F32))


def lower_kernel(
    dq_ref, dck_ref, dcv_ref, res2_ref, unit_ref, inv_ref, wcq_ref, wkv_ref, wout_ref, vec_ref,
    genc_ref, res1_ref, low1_ref, gmix_ref, sums_ref,
):
    features = res2_ref.shape[1]

    @pl.when(pl.program_id(0) == 0)
    def _():
        sums_ref[...] = jnp.zeros_like(sums_ref)

    genc_ref[...] = nt_dot(dck_ref[...], wkv_ref[:, :features]) + nt_dot(dcv_ref[...], wkv_ref[:, features:])
    above = res2_ref[...] + nt_dot(dq_ref[...], wcq_ref[...])
    unit = unit_ref[...]
    res1 = norm_back(above, unit, inv_ref[:, :1], vec(vec_ref, 7))
    res1_ref[...] = res1
    low1 = res1.astype(BF16)
    low1_ref[...] = low1
    gmix_ref[...] = nt_dot(low1, wout_ref[...]).astype(BF16)
    for index, value in (
        (2, low1.astype(F32)), (3, dq_ref[...].astype(F32)), (4, dcv_ref[...].astype(F32)), (7, above * unit), (10, above),
    ):
        sums_ref[index : index + 1, :] += col_sum(value)


def input_kernel(dq_ref, dk_ref, dv_ref, res1_ref, win_ref, gin_ref, sums_ref):
    features = res1_ref.shape[1]

    @pl.when(pl.program_id(0) == 0)
    def _():
        sums_ref[...] = jnp.zeros_like(sums_ref)

    total = res1_ref[...]
    for part, ref in enumerate((dq_ref, dk_ref, dv_ref)):
        total = total + nt_dot(ref[...], win_ref[:, part * features : (part + 1) * features])
    gin_ref[...] = total
    for index, value in ((0, dq_ref[...].astype(F32)), (1, dv_ref[...].astype(F32)), (LANG_ROW, total)):
        sums_ref[index : index + 1, :] += col_sum(value)


def rows_call(kernel, name, tokens, arrays, outs, block=256):
    in_specs, operands = [], []
    for array, kind in arrays:
        operands.append(array)
        if kind == "smem":
            in_specs.append(SMEM_SPEC)
        elif kind == "row":
            in_specs.append(pl.BlockSpec((block, array.shape[1]), lambda i: (i, 0)))
        else:
            in_specs.append(pl.BlockSpec(array.shape, lambda i: (0, 0)))
    out_specs, out_shape = [], []
    for out in outs:
        if len(out) == 2:
            out_specs.append(pl.BlockSpec((block, out[0]), lambda i: (i, 0)))
            out_shape.append(jax.ShapeDtypeStruct((tokens, out[0]), out[1]))
        else:
            out_specs.append(pl.BlockSpec(out[:2], lambda i: (0, 0)))
            out_shape.append(jax.ShapeDtypeStruct(out[:2], out[2]))
    return pl.pallas_call(
        kernel,
        grid=(tokens // block,),
        in_specs=in_specs,
        out_specs=out_specs,
        out_shape=out_shape,
        compiler_params=BIG,
        name=name,
    )(*operands)


MESH = pl.DeviceIdType.MESH
ANY_SPEC = pl.BlockSpec(memory_space=pl.ANY)


class Place:
    def __init__(self, depth):
        dp, fsdp = lax.axis_index("dp"), lax.axis_index("fsdp")
        self.depth = depth
        self.z, self.x = dp // 2, lax.rem(dp, 2)
        self.y, self.c = fsdp // 2, lax.rem(fsdp, 2)
        self.fsdp = fsdp

    def dev(self, z=None, x=None, y=None, c=None):
        z, x = (self.z if z is None else z), (self.x if x is None else x)
        y, c = (self.y if y is None else y), (self.c if c is None else c)
        return (2 * z + x, 2 * y + c)

    def ahead(self, d):
        return lax.rem(self.z + d, self.depth)

    def behind(self, d):
        return lax.rem(self.z + self.depth - d, self.depth)

    def greet(self):
        others = [self.dev(z=self.ahead(d)) for d in range(1, self.depth)]
        others += [self.dev(x=1 - self.x), self.dev(y=1 - self.y), self.dev(c=1 - self.c)]
        others += [self.dev(y=1 - self.y, c=1 - self.c)]
        barrier = pltpu.get_barrier_semaphore()
        for other in others:
            pl.semaphore_signal(barrier, inc=1, device_id=other, device_id_type=MESH)
        pl.semaphore_wait(barrier, len(others))


def remote(src, dst, send, recv, device):
    return pltpu.make_async_remote_copy(
        src_ref=src, dst_ref=dst, send_sem=send, recv_sem=recv, device_id=device, device_id_type=MESH
    )


class Gather:
    def __init__(self, place, src, dst, local, send, recv, cols=None, flip=False):
        self.place, self.src, self.dst, self.flip = place, src, dst, flip
        self.local, self.send, self.recv = local, send, recv
        self.cols = cols
        self.sent = []

    def at(self, z, x, y, c):
        where = (z, x, y, c)
        return self.dst.at[where] if self.cols is None else self.dst.at[(*where, slice(None), self.cols)]

    def push(self, block, index, device):
        copy = remote(block, block, self.send.at[index], self.recv.at[index], device)
        copy.start()
        self.sent.append(copy)

    def heard(self, block, index):
        remote(block, block, self.send.at[index], self.recv.at[index], self.place.dev()).wait_recv()

    def along_z(self):
        p = self.place
        own = self.at(p.z, p.x, p.y, p.c)
        src = self.src if self.cols is None else self.src.at[:, self.cols]
        self.copy = pltpu.make_async_copy(src, own, self.local)
        self.copy.start()
        for d in range(1, p.depth):
            copy = remote(src, own, self.send.at[d - 1], self.recv.at[d - 1], p.dev(z=p.ahead(d)))
            copy.start()
            self.sent.append(copy)

    def across_one(self):
        p = self.place
        self.copy.wait()
        for d in range(1, p.depth):
            self.heard(self.at(p.behind(d), p.x, p.y, p.c), d - 1)
        other = p.dev(x=1 - p.x) if self.flip else p.dev(y=1 - p.y)
        self.push(self.at(slice(None), p.x, p.y, p.c), p.depth - 1, other)

    def plane(self, mine, c):
        p = self.place
        if self.flip:
            return self.at(slice(None), slice(None), p.y if mine else 1 - p.y, c)
        return self.at(slice(None), p.x if mine else 1 - p.x, slice(None), c)

    def across_two(self):
        p = self.place
        missing = (1 - p.x, p.y) if self.flip else (p.x, 1 - p.y)
        self.heard(self.at(slice(None), *missing, p.c), p.depth - 1)
        block = self.plane(True, p.c)
        self.push(block, p.depth, p.dev(y=1 - p.y) if self.flip else p.dev(x=1 - p.x))
        self.push(block, p.depth + 1, p.dev(c=1 - p.c))

    def to_core(self):
        p = self.place
        block = self.plane(False, p.c)
        self.heard(block, p.depth)
        self.push(block, p.depth + 2, p.dev(c=1 - p.c))

    def whole(self):
        p = self.place
        self.heard(self.plane(True, 1 - p.c), p.depth + 1)
        self.heard(self.plane(False, 1 - p.c), p.depth + 2)

    def finish(self):
        for copy in self.sent:
            copy.wait_send()


class Exchange:
    def __init__(self, place, src, dst, local, send, recv):
        self.place, self.src, self.dst = place, src, dst
        self.local, self.send, self.recv = local, send, recv
        self.rows = src.shape[1]

    def block(self, owner):
        return self.dst.at[pl.ds(pl.multiple_of(owner * self.rows, self.rows), self.rows)]

    def start(self):
        me = self.place.fsdp
        self.copy = pltpu.make_async_copy(self.src.at[me], self.block(me), self.local)
        self.copy.start()
        self.sent = []
        for d in range(1, 4):
            to = lax.rem(me + d, 4)
            copy = remote(
                self.src.at[to], self.block(me), self.send.at[d - 1], self.recv.at[d - 1],
                (lax.axis_index("dp"), to),
            )
            copy.start()
            self.sent.append(copy)

    def whole(self):
        self.copy.wait()
        for d in range(1, 4):
            block = self.block(lax.rem(self.place.fsdp + 4 - d, 4))
            remote(block, block, self.send.at[d - 1], self.recv.at[d - 1], self.place.dev()).wait_recv()

    def finish(self):
        for copy in self.sent:
            copy.wait_send()


def flat_cols(ref, cols):
    value = ref[:, :, :, :, :, cols]
    return value.reshape(-1, value.shape[-1])


def first_kernel(
    depth, langs,
    dlen_ref, tag_ref, dec_in, enc_in, cot_in, small_in, in_in, out_in, cq_in, ckv_in, co_in, fin_in, fout_in,
    w_in, w_out, w_cq, w_ckv, w_co, w_fin, w_fout, x_out, enc_out, cot_out, vec_out, fb_out,
    low_out, merged_out, pair_out, mixed_out, mixf_out, lse_out,
    small, win, wkv, x, enc, vecs, fb, low, merged, pair, mixed, mixf, lse, small_cols, kx, va, vb,
    wlocal, wsend, wrecv, elocal, esend, erecv, osem,
):
    p = Place(depth)
    features = x.shape[1]
    tokens = x.shape[0]
    p.greet()
    jobs = []

    def gather(src, dst, cols=None, flip=False):
        n = len(jobs)
        jobs.append(Gather(p, src, dst, wlocal.at[n], wsend.at[n], wrecv.at[n], cols, flip))
        return jobs[-1]

    def part(i):
        return pl.ds(i * features, features)

    def half(i):
        return pl.ds(i * (features // 2), features // 2)

    dec = Exchange(p, dec_in, x, elocal.at[0], esend.at[0], erecv.at[0])
    encode = Exchange(p, enc_in, enc, elocal.at[1], esend.at[1], erecv.at[1])
    cot = Exchange(p, cot_in, cot_out, elocal.at[2], esend.at[2], erecv.at[2])
    g_small = gather(small_in, small)
    g_k, g_v, g_q = gather(in_in, win, part(1)), gather(in_in, win, part(2), True), gather(in_in, win, part(0))
    g_ck, g_cv = gather(ckv_in, wkv, part(0)), gather(ckv_in, wkv, part(1))
    g_out, g_cq, g_co = gather(out_in, w_out), gather(cq_in, w_cq), gather(co_in, w_co)
    g_fi = [gather(fin_in, w_fin, part(i)) for i in range(4)]
    g_fo = [gather(fout_in, w_fout, half(i)) for i in range(2)]
    first = [g_small, g_k, g_v, g_q]
    second = [g_ck, g_cv]
    third = [g_out, g_cq, g_co]
    waves = [first, second, third, g_fi[:2], g_fi[2:], g_fo]

    def move(step, *which):
        for wave in which:
            for job in waves[wave]:
                getattr(job, step)()

    writes = []

    def write(src, dst):
        copy = pltpu.make_async_copy(src, dst, osem.at[len(writes)])
        copy.start()
        writes.append(copy)

    dec.start()
    move("along_z", 0)
    move("along_z", 1)
    move("across_one", 0)
    move("across_two", 0)
    encode.start()
    move("across_one", 1)
    move("along_z", 2)
    move("to_core", 0)
    g_small.whole()
    for r in range(depth * 8):
        where = (r // 8, (r // 4) % 2, (r // 2) % 2, r % 2)
        tile = small[where].astype(F32)
        small_cols[16 * r : 16 * r + 16, :] = tile[:16]
        lanes = slice(128 * (r // 2), 128 * (r // 2) + 128)
        if r % 2 == 0:
            fb[:, lanes] = tile[16:17]
        else:
            fb[:, lanes] += tile[16:17]
    turned = small_cols[...].T
    vecs[...] = turned[:16]
    chosen = lax.broadcasted_iota(jnp.int32, (128, 1), 0) == tag_ref[p.fsdp] + 13
    lang_row = col_sum(jnp.where(chosen, turned, 0.0))
    vecs[LANG_ROW : LANG_ROW + 1, :] = lang_row
    write(vecs, vec_out)
    write(fb, fb_out)
    dec.whole()
    write(x, x_out)
    low[...] = (x[...].astype(F32) + lang_row).astype(BF16)
    write(low, low_out)

    def project(source, weight, cols, bias, dest):
        whole = flat_cols(weight, cols)

        def tile(i, carry):
            rows = pl.ds(pl.multiple_of(i * 256, 256), 256)
            out = nn_dot(source[rows, :], whole)
            dest[rows, cols] = (out if bias is None else out + bias).astype(BF16)
            return carry

        lax.fori_loop(0, tokens // 256, tile, 0)

    g_k.whole()
    project(low, win, part(1), None, merged)
    g_v.whole()
    project(low, win, part(2), vecs[1:2, :], merged)
    move("across_two", 1)
    move("across_one", 2)
    move("along_z", 3)
    g_q.whole()
    project(low, win, part(0), vecs[0:1, :], merged)
    write(win, w_in)
    write(merged, merged_out)
    move("to_core", 1)
    move("across_two", 2)
    move("across_one", 3)
    move("along_z", 4)
    cot.start()
    encode.whole()
    write(enc, enc_out)
    g_ck.whole()
    project(enc, wkv, part(0), None, pair)
    g_cv.whole()
    project(enc, wkv, part(1), vecs[4:5, :], pair)
    write(wkv, w_ckv)
    write(pair, pair_out)
    steps = [
        [("to_core", 2), ("across_two", 3), ("across_one", 4), ("along_z", 5)],
        [("to_core", 3), ("across_two", 4), ("across_one", 5)],
        [("to_core", 4), ("across_two", 5)],
        [("to_core", 5)],
    ]
    length = dlen_ref[p.fsdp]
    for pair_index in range(4):
        cols = pl.ds(128 * pair_index, 128)
        attend_fwd_core(
            256, length, merged.at[:, cols], merged.at[:, pl.ds(features + 128 * pair_index, 128)],
            merged.at[:, pl.ds(2 * features + 128 * pair_index, 128)],
            mixed.at[:, cols], mixf.at[:, cols], lse.at[:, cols], kx, va, vb,
        )
        for step, wave in steps[pair_index]:
            move(step, wave)
    write(mixed, mixed_out)
    write(mixf, mixf_out)
    write(lse, lse_out)
    move("whole", 2, 3, 4, 5)
    cot.whole()
    for job in (*jobs, dec, encode, cot):
        job.finish()
    for copy in writes:
        copy.wait()


def first_call(depth, langs, dlen, tags, dec, enc, cot, small, *weights):
    groups, part_rows, features = dec.shape
    tokens = groups * part_rows
    hidden = weights[5].shape[1]

    def full(w):
        return (depth, 2, 2, 2, *w.shape)

    def sds(shape, dtype):
        return jax.ShapeDtypeStruct(shape, dtype)

    outs = [sds(full(w), BF16) for w in weights]
    outs += [sds((tokens, features), BF16)] * 3 + [sds((16, features), F32), sds((1, hidden), F32)]
    outs += [sds((tokens, n * features), BF16) for n in (1, 3, 2, 1)] + [sds((tokens, features), F32)] * 2
    n_jobs = 15
    return pl.pallas_call(
        functools.partial(first_kernel, depth, langs),
        in_specs=[SMEM_SPEC] * 2 + [ANY_SPEC] * 11,
        out_specs=[ANY_SPEC] * len(outs),
        out_shape=outs,
        scratch_shapes=[
            pltpu.VMEM(full(small), BF16),
            pltpu.VMEM(full(weights[0]), BF16),
            pltpu.VMEM(full(weights[3]), BF16),
            pltpu.VMEM((tokens, features), BF16),
            pltpu.VMEM((tokens, features), BF16),
            pltpu.VMEM((16, features), F32),
            pltpu.VMEM((1, hidden), F32),
            pltpu.VMEM((tokens, features), BF16),
            pltpu.VMEM((tokens, 3 * features), BF16),
            pltpu.VMEM((tokens, 2 * features), BF16),
            pltpu.VMEM((tokens, features), BF16),
            pltpu.VMEM((tokens, features), F32),
            pltpu.VMEM((tokens, features), F32),
            pltpu.VMEM((features, 128), F32),
            pltpu.VMEM((tokens, 256), BF16),
            pltpu.VMEM((tokens, 128), BF16),
            pltpu.VMEM((tokens, 128), BF16),
            pltpu.SemaphoreType.DMA((n_jobs,)),
            pltpu.SemaphoreType.DMA((n_jobs, depth + 3)),
            pltpu.SemaphoreType.DMA((n_jobs, depth + 3)),
            pltpu.SemaphoreType.DMA((3,)),
            pltpu.SemaphoreType.DMA((3, 3)),
            pltpu.SemaphoreType.DMA((3, 3)),
            pltpu.SemaphoreType.DMA((16,)),
        ],
        compiler_params=pltpu.CompilerParams(
            vmem_limit_bytes=56 * 1024 * 1024, collective_id=1, has_side_effects=True
        ),
        name="first",
    )(dlen, tags, dec, enc, cot, small, *weights)


def fast_body(
    dec_input, enc_output, dec_lengths, enc_lengths, lang_tags, lang_table, self_in, self_out, cross_q, cross_kv,
    cross_out, ffn_in, ffn_out, biases, ffn_bias, norm_gains, norm_shifts, cotangent,
):
    both = ("dp", "fsdp")
    groups, part_rows, features = dec_input.shape
    tokens = groups * part_rows
    hidden = ffn_in.shape[1]
    langs = lang_table.shape[1]
    me = lax.axis_index("fsdp")
    depth = lax.axis_size("dp") // 2
    dec_len = lax.dynamic_slice(dec_lengths, (me,), (1,))
    enc_len = lax.dynamic_slice(enc_lengths, (me,), (1,))
    tag = lax.dynamic_slice(lang_tags, (me,), (1,))
    fcols = ffn_bias.shape[0]
    small = jnp.concatenate([biases, norm_gains, norm_shifts, lang_table], axis=1)
    small = jnp.pad(small, ((0, 16), (0, 128 - small.shape[1])))
    small = lax.dynamic_update_slice(small, ffn_bias[None], (16, lax.rem(me, 2) * fcols))
    (
        w_in, w_out, w_cq, w_ckv, w_co, w_fin, w_fout, x, enc, cot, vecs, fbias,
        low, merged, pair, mixed, mixed_f32, self_lse,
    ) = first_call(
        depth, langs, dec_lengths, lang_tags, dec_input, enc_output, cotangent.astype(BF16), small,
        self_in, self_out, cross_q, cross_kv, cross_out, ffn_in, ffn_out,
    )
    w_in, w_out, w_cq, w_ckv, w_co, w_fin, w_fout = [
        w.reshape(-1, w.shape[-1]) for w in (w_in, w_out, w_cq, w_ckv, w_co, w_fin, w_fout)
    ]
    onehot = (tag == jnp.arange(langs)).astype(F32)
    fcols = ffn_bias.shape[0] // biases.shape[0]
    unit1, inv1, one, cquery = rows_call(
        middle_kernel, "middle", tokens,
        [(x, "row"), (mixed, "row"), (w_out, "all"), (w_cq, "all"), (vecs, "all")],
        [(features, F32), (128, F32), (features, BF16), (features, BF16)],
    )
    cmixed, cmixed_f32, cross_lse = attend_fwd(cquery, 0, pair, 0, 4, enc_len)
    output, act, low3, two, ghid, res2, low2, gcm, sums_a, fsum = rows_call(
        ffn_kernel, "ffn", tokens,
        [(dec_len, "smem"), (cmixed, "row"), (unit1, "row"), (cot, "row"), (w_co, "all"), (w_fin, "all"), (w_fout, "all"), (vecs, "all"), (fbias, "all")],
        [(features, BF16), (hidden, BF16), (features, BF16), (features, BF16), (hidden, BF16), (features, F32), (features, BF16), (features, BF16), (16, features, F32), (1, hidden, F32)],
    )
    dcq, dck, dcv = attend_bwd(cquery, 0, pair, 0, 4, gcm, cmixed_f32, cross_lse, enc_len)
    genc, res1, low1, gmix, sums_b = rows_call(
        lower_kernel, "lower", tokens,
        [(dcq, "row"), (dck, "row"), (dcv, "row"), (res2, "row"), (unit1, "row"), (inv1, "row"), (w_cq, "all"), (w_ckv, "all"), (w_out, "all"), (vecs, "all")],
        [(features, F32), (features, F32), (features, BF16), (features, BF16), (16, features, F32)],
    )
    dq, dk, dv = attend_bwd(merged, 0, merged, 4, 8, gmix, mixed_f32, self_lse, dec_len)
    gin, sums_c = rows_call(
        input_kernel, "input", tokens,
        [(dq, "row"), (dk, "row"), (dv, "row"), (res1, "row"), (w_in, "all")],
        [(features, F32), (16, features, F32)],
    )
    g_fout = outer_sum(act, low3)
    g_fin = outer_sum(two, ghid)
    g_co = outer_sum(cmixed, low2)
    g_ckv = jnp.concatenate([outer_sum(enc, dck), outer_sum(enc, dcv)], axis=1)
    g_cq = outer_sum(one, dcq)
    g_out = outer_sum(mixed, low1)
    g_in = jnp.concatenate([outer_sum(low, dq), outer_sum(low, dk), outer_sum(low, dv)], axis=1)
    sums = sums_a + sums_b + sums_c
    g_table = sums[LANG_ROW][:, None] * onehot[None, :]
    g_small = jnp.concatenate([sums[:13].T, g_table, fsum.reshape(features, fcols)], axis=1)
    g_small = jnp.pad(g_small, ((0, 0), (0, 128 - g_small.shape[1])))
    parts = lax.axis_size(both) if hasattr(lax, "axis_size") else lax.psum(1, both)
    packed = jnp.concatenate([g.reshape(parts, -1) for g in (g_fout, g_fin, g_co, g_ckv, g_cq, g_out, g_in, g_small)], axis=1)
    packed = lax.psum_scatter(packed, both, scatter_dimension=0, tiled=True)[0]
    shards, at = [], 0
    for like in (ffn_out, ffn_in, cross_out, cross_kv, cross_q, self_out, self_in, jnp.zeros((biases.shape[0], 128))):
        shards.append(packed[at : at + like.size].reshape(like.shape))
        at += like.size
    r_fout, r_fin, r_co, r_ckv, r_cq, r_out, r_in, r_small = shards
    output = lax.all_to_all(output[None], "fsdp", 1, 0, tiled=True)
    gin = lax.all_to_all(gin[None], "fsdp", 1, 0, tiled=True)
    genc = lax.all_to_all(genc[None], "fsdp", 1, 0, tiled=True)
    return (
        output, gin, genc, r_small[:, 13 : 13 + langs], r_in, r_out, r_cq, r_ckv, r_co, r_fin, r_fout,
        r_small[:, :7], r_small[:, 13 + langs : 13 + langs + fcols].reshape(-1), r_small[:, 7:10], r_small[:, 10:13],
    )


def solution(mesh):
    def either(*args):
        whole_sequences = mesh.shape["fsdp"] == args[0].shape[0] and args[3 + 3].shape[0] % 16 == 0
        return (fast_body if whole_sequences else body)(*args)

    return jax.shard_map(
        either,
        mesh=mesh,
        in_specs=(
            P("dp", "fsdp", None),
            P("dp", "fsdp", None),
            P("dp"),
            P("dp"),
            P("dp"),
            P(("dp", "fsdp"), None),
            P(("dp", "fsdp"), None),
            P(("dp", "fsdp"), None),
            P(("dp", "fsdp"), None),
            P(("dp", "fsdp"), None),
            P(("dp", "fsdp"), None),
            P(("dp", "fsdp"), None),
            P(("dp", "fsdp"), None),
            P(("dp", "fsdp"), None),
            P(("dp", "fsdp")),
            P(("dp", "fsdp"), None),
            P(("dp", "fsdp"), None),
            P("dp", "fsdp", None),
        ),
        out_specs=(
            P("dp", "fsdp", None),
            P("dp", "fsdp", None),
            P("dp", "fsdp", None),
            P(("dp", "fsdp"), None),
            P(("dp", "fsdp"), None),
            P(("dp", "fsdp"), None),
            P(("dp", "fsdp"), None),
            P(("dp", "fsdp"), None),
            P(("dp", "fsdp"), None),
            P(("dp", "fsdp"), None),
            P(("dp", "fsdp"), None),
            P(("dp", "fsdp"), None),
            P(("dp", "fsdp")),
            P(("dp", "fsdp"), None),
            P(("dp", "fsdp"), None),
        ),
        check_vma=False,
    )
```

```python
import functools
import math

import jax
import jax.numpy as jnp
from jax import lax
from jax.experimental import pallas as pl
from jax.experimental.pallas import tpu as pltpu
from jax.sharding import PartitionSpec as P

HEADS = 8
DP, FSDP = AXES = ("dp", "fsdp")


def smooth_gelu(values):
    return (
        0.5
        * values
        * (1.0 + jnp.tanh(0.7978845608028654 * (values + 0.044715 * values * values * values)))
    )


def times_t(left, right):
    return lax.dot_general(
        left, right, (((1,), (1,)), ((), ())), preferred_element_type=jnp.float32
    )


def outer_sum(left, right):
    return lax.dot_general(
        left, right, (((0,), (0,)), ((), ())), preferred_element_type=jnp.float32
    )


def normalize_rows(residual, gain_col, shift_col):
    row_mean = jnp.mean(residual, axis=-1, keepdims=True)
    centered = residual - row_mean
    inv_dev = lax.rsqrt(jnp.mean(centered * centered, axis=-1, keepdims=True) + 1e-05)
    unit_rows = centered * inv_dev
    return (unit_rows * gain_col + shift_col, unit_rows, inv_dev)


def normalize_back(grad_above, unit_rows, inv_dev, gain_col):
    grad_unit = grad_above * gain_col
    grad_res = inv_dev * (
        grad_unit
        - jnp.mean(grad_unit, axis=-1, keepdims=True)
        - unit_rows * jnp.mean(grad_unit * unit_rows, axis=-1, keepdims=True)
    )
    return (grad_res, jnp.sum(grad_above * unit_rows, axis=0), jnp.sum(grad_above, axis=0))


def masked_scores(query_bf, key_full, lengths_here):
    groups, rows_here, features = query_bf.shape
    key_count = key_full.shape[1]
    head_size = features // HEADS
    query_heads = query_bf.reshape(groups, rows_here, HEADS, head_size)
    key_heads = key_full.reshape(groups, key_count, HEADS, head_size)
    scores = jnp.einsum(
        "sqhd,skhd->shqk", query_heads, key_heads, preferred_element_type=jnp.float32
    ) * (1.0 / math.sqrt(head_size))
    key_valid = jnp.arange(key_count)[None, :] < lengths_here[:, None]
    return jnp.where(key_valid[:, None, None, :], scores, -1000000000.0)


def attend_forward(query_bf, key_full, value_full, lengths_here):
    groups, rows_here, features = query_bf.shape
    key_count = key_full.shape[1]
    value_heads = value_full.reshape(groups, key_count, HEADS, features // HEADS)
    scores = masked_scores(query_bf, key_full, lengths_here)
    row_max = jnp.max(scores, axis=-1, keepdims=True)
    exp_scores = jnp.exp(scores - row_max)
    row_total = jnp.sum(exp_scores, axis=-1, keepdims=True)
    probs_bf = (exp_scores / row_total).astype(jnp.bfloat16)
    attn_mixed = jnp.einsum(
        "shqk,skhd->sqhd", probs_bf, value_heads, preferred_element_type=jnp.float32
    )
    return (attn_mixed.reshape(groups, rows_here, features), row_max + jnp.log(row_total))


def attend_back(grad_mixed_bf, query_bf, key_full, value_full, lengths_here, log_total):
    groups, rows_here, features = query_bf.shape
    key_count = key_full.shape[1]
    head_size = features // HEADS
    query_heads = query_bf.reshape(groups, rows_here, HEADS, head_size)
    key_heads = key_full.reshape(groups, key_count, HEADS, head_size)
    value_heads = value_full.reshape(groups, key_count, HEADS, head_size)
    grad_heads = grad_mixed_bf.reshape(groups, rows_here, HEADS, head_size)
    attn_probs = jnp.exp(masked_scores(query_bf, key_full, lengths_here) - log_total)
    probs_bf = attn_probs.astype(jnp.bfloat16)
    grad_probs = jnp.einsum(
        "sqhd,skhd->shqk", grad_heads, value_heads, preferred_element_type=jnp.float32
    )
    grad_values = jnp.einsum(
        "shqk,sqhd->skhd", probs_bf, grad_heads, preferred_element_type=jnp.float32
    )
    grad_scores = attn_probs * (
        grad_probs - jnp.sum(attn_probs * grad_probs, axis=-1, keepdims=True)
    )
    grad_scores_bf = grad_scores.astype(jnp.bfloat16)
    score_scale = 1.0 / math.sqrt(head_size)
    grad_query = (
        jnp.einsum("shqk,skhd->sqhd", grad_scores_bf, key_heads, preferred_element_type=jnp.float32)
        * score_scale
    )
    grad_keys = (
        jnp.einsum(
            "shqk,sqhd->skhd", grad_scores_bf, query_heads, preferred_element_type=jnp.float32
        )
        * score_scale
    )
    return (
        grad_query.reshape(groups, rows_here, features),
        grad_keys.reshape(groups, key_count, features),
        grad_values.reshape(groups, key_count, features),
    )


def body(
    dec_input,
    enc_output,
    dec_lengths,
    enc_lengths,
    lang_tags,
    lang_table,
    self_in,
    self_out,
    cross_q,
    cross_kv,
    cross_out,
    ffn_in,
    ffn_out,
    biases,
    ffn_bias,
    norm_gains,
    norm_shifts,
    cotangent,
):
    full_weights = (
        lax.all_gather(lang_table, AXES, axis=0, tiled=True),
        lax.all_gather(self_in, AXES, axis=0, tiled=True),
        lax.all_gather(self_out, AXES, axis=0, tiled=True),
        lax.all_gather(cross_q, AXES, axis=0, tiled=True),
        lax.all_gather(cross_kv, AXES, axis=0, tiled=True),
        lax.all_gather(cross_out, AXES, axis=0, tiled=True),
        lax.all_gather(ffn_in, AXES, axis=0, tiled=True),
        lax.all_gather(ffn_out, AXES, axis=0, tiled=True),
        lax.all_gather(biases, AXES, axis=0, tiled=True),
        lax.all_gather(ffn_bias, AXES, axis=0, tiled=True),
        lax.all_gather(norm_gains, AXES, axis=0, tiled=True),
        lax.all_gather(norm_shifts, AXES, axis=0, tiled=True),
    )
    (
        full_table,
        full_in,
        full_out,
        full_cq,
        full_ckv,
        full_co,
        full_ffn_in,
        full_ffn_out,
        full_biases,
        full_ffn_bias,
        full_gains,
        full_shifts,
    ) = full_weights
    bias_cols = full_biases.astype(jnp.float32)
    gain_cols = full_gains.astype(jnp.float32)
    shift_cols = full_shifts.astype(jnp.float32)
    groups, rows_here, features = dec_input.shape
    enc_rows = enc_output.shape[1]
    tokens = groups * rows_here
    positions = lax.axis_index(FSDP) * rows_here + jnp.arange(rows_here)
    live_rows = (positions[None, :] < dec_lengths[:, None]).astype(jnp.float32)
    live_flat = live_rows.reshape(tokens, 1)
    onehot = (lang_tags[:, None] == jnp.arange(full_table.shape[1])[None, :]).astype(jnp.float32)
    lang_rows = lax.dot_general(
        onehot,
        full_table.astype(jnp.float32),
        (((1,), (1,)), ((), ())),
        precision=lax.Precision.HIGHEST,
        preferred_element_type=jnp.float32,
    )
    flat_start = (dec_input.astype(jnp.float32) + lang_rows[:, None, :]).reshape(tokens, features)
    start_bf = flat_start.astype(jnp.bfloat16)
    zeros_row = jnp.zeros((features,), jnp.float32)
    merged = (
        jnp.dot(start_bf, full_in, preferred_element_type=jnp.float32)
        + jnp.concatenate([bias_cols[:, 0], zeros_row, bias_cols[:, 1]])[None, :]
    )
    merged_bf = merged.astype(jnp.bfloat16).reshape(groups, rows_here, 3 * features)
    query_bf = merged_bf[:, :, :features]
    key_own = merged_bf[:, :, features : 2 * features]
    value_own = merged_bf[:, :, 2 * features :]
    key_full, value_full = (
        lax.all_gather(key_own, FSDP, axis=1, tiled=True),
        lax.all_gather(value_own, FSDP, axis=1, tiled=True),
    )
    attn_mixed, self_lse = attend_forward(query_bf, key_full, value_full, dec_lengths)
    mixed_bf = attn_mixed.astype(jnp.bfloat16).reshape(tokens, features)
    branch = jnp.dot(mixed_bf, full_out, preferred_element_type=jnp.float32) + bias_cols[:, 2]
    normed_one, unit_one, inv_one = normalize_rows(
        flat_start + branch, gain_cols[:, 0], shift_cols[:, 0]
    )
    one_bf = normed_one.astype(jnp.bfloat16)
    cross_query = (
        (jnp.dot(one_bf, full_cq, preferred_element_type=jnp.float32) + bias_cols[:, 3])
        .astype(jnp.bfloat16)
        .reshape(groups, rows_here, features)
    )
    enc_flat = enc_output.reshape(groups * enc_rows, features)
    cross_pair = (
        jnp.dot(enc_flat, full_ckv, preferred_element_type=jnp.float32)
        + jnp.concatenate([zeros_row, bias_cols[:, 4]])[None, :]
    )
    pair_bf = cross_pair.astype(jnp.bfloat16).reshape(groups, enc_rows, 2 * features)
    ckey_own = pair_bf[:, :, :features]
    cvalue_own = pair_bf[:, :, features:]
    ckey_full, cvalue_full = (
        lax.all_gather(ckey_own, FSDP, axis=1, tiled=True),
        lax.all_gather(cvalue_own, FSDP, axis=1, tiled=True),
    )
    cross_mixed, cross_lse = attend_forward(cross_query, ckey_full, cvalue_full, enc_lengths)
    cmixed_bf = cross_mixed.astype(jnp.bfloat16).reshape(tokens, features)
    cross_branch = jnp.dot(cmixed_bf, full_co, preferred_element_type=jnp.float32) + bias_cols[:, 5]
    normed_two, unit_two, inv_two = normalize_rows(
        normed_one + cross_branch, gain_cols[:, 1], shift_cols[:, 1]
    )
    two_bf = normed_two.astype(jnp.bfloat16)
    hidden = jnp.dot(
        two_bf, full_ffn_in, preferred_element_type=jnp.float32
    ) + full_ffn_bias.astype(jnp.float32)
    activated, gelu_pull = jax.vjp(smooth_gelu, hidden)
    act_bf = activated.astype(jnp.bfloat16)
    ffn_branch = jnp.dot(act_bf, full_ffn_out, preferred_element_type=jnp.float32) + bias_cols[:, 6]
    normed_three, unit_three, inv_three = normalize_rows(
        normed_two + ffn_branch, gain_cols[:, 2], shift_cols[:, 2]
    )
    output = (normed_three * live_flat).astype(jnp.bfloat16).reshape(groups, rows_here, features)
    back_weights = (
        lax.all_gather(lang_table, AXES, axis=0, tiled=True),
        lax.all_gather(self_in, AXES, axis=0, tiled=True),
        lax.all_gather(self_out, AXES, axis=0, tiled=True),
        lax.all_gather(cross_q, AXES, axis=0, tiled=True),
        lax.all_gather(cross_kv, AXES, axis=0, tiled=True),
        lax.all_gather(cross_out, AXES, axis=0, tiled=True),
        lax.all_gather(ffn_in, AXES, axis=0, tiled=True),
        lax.all_gather(ffn_out, AXES, axis=0, tiled=True),
        lax.all_gather(biases, AXES, axis=0, tiled=True),
        lax.all_gather(ffn_bias, AXES, axis=0, tiled=True),
        lax.all_gather(norm_gains, AXES, axis=0, tiled=True),
        lax.all_gather(norm_shifts, AXES, axis=0, tiled=True),
    )
    back_in = back_weights[1]
    back_out = back_weights[2]
    back_cq = back_weights[3]
    back_ckv = back_weights[4]
    back_co = back_weights[5]
    back_ffn_in = back_weights[6]
    back_ffn_out = back_weights[7]
    back_gains = back_weights[10].astype(jnp.float32)
    grad_above = cotangent.reshape(tokens, features) * live_flat
    grad_res3, gain_three, shift_three = normalize_back(
        grad_above, unit_three, inv_three, back_gains[:, 2]
    )
    grad_low3 = grad_res3.astype(jnp.bfloat16)
    grad_ffn_out = outer_sum(act_bf, grad_low3)
    bias_six = jnp.sum(grad_low3.astype(jnp.float32), axis=0)
    grad_act = times_t(grad_low3, back_ffn_out)
    grad_hidden_bf = gelu_pull(grad_act)[0].astype(jnp.bfloat16)
    grad_ffn_in = outer_sum(two_bf, grad_hidden_bf)
    grad_ffn_bias = jnp.sum(grad_hidden_bf.astype(jnp.float32), axis=0)
    grad_two = grad_res3 + times_t(grad_hidden_bf, back_ffn_in)
    grad_res2, gain_two, shift_two = normalize_back(grad_two, unit_two, inv_two, back_gains[:, 1])
    grad_low2 = grad_res2.astype(jnp.bfloat16)
    grad_cross_out = outer_sum(cmixed_bf, grad_low2)
    bias_five = jnp.sum(grad_low2.astype(jnp.float32), axis=0)
    grad_cmixed = (
        times_t(grad_low2, back_co).astype(jnp.bfloat16).reshape(groups, rows_here, features)
    )
    grad_cquery, grad_ckey, grad_cvalue = attend_back(
        grad_cmixed, cross_query, ckey_full, cvalue_full, enc_lengths, cross_lse
    )
    ckey_sum, cvalue_sum = (
        lax.psum_scatter(
            grad_ckey.astype(jnp.bfloat16), FSDP, scatter_dimension=1, tiled=True
        ).astype(jnp.float32),
        lax.psum_scatter(
            grad_cvalue.astype(jnp.bfloat16), FSDP, scatter_dimension=1, tiled=True
        ).astype(jnp.float32),
    )
    grad_pair_bf = (
        jnp.concatenate([ckey_sum, cvalue_sum], axis=-1)
        .astype(jnp.bfloat16)
        .reshape(groups * enc_rows, 2 * features)
    )
    grad_cross_kv = outer_sum(enc_flat, grad_pair_bf)
    bias_four = jnp.sum(grad_pair_bf[:, features:].astype(jnp.float32), axis=0)
    grad_encoder = times_t(grad_pair_bf, back_ckv).reshape(groups, enc_rows, features)
    grad_cquery_bf = grad_cquery.astype(jnp.bfloat16).reshape(tokens, features)
    grad_cross_q = outer_sum(one_bf, grad_cquery_bf)
    bias_three = jnp.sum(grad_cquery_bf.astype(jnp.float32), axis=0)
    grad_one = grad_res2 + times_t(grad_cquery_bf, back_cq)
    grad_res1, gain_one, shift_one = normalize_back(grad_one, unit_one, inv_one, back_gains[:, 0])
    grad_low1 = grad_res1.astype(jnp.bfloat16)
    grad_self_out = outer_sum(mixed_bf, grad_low1)
    bias_two = jnp.sum(grad_low1.astype(jnp.float32), axis=0)
    grad_mixed = (
        times_t(grad_low1, back_out).astype(jnp.bfloat16).reshape(groups, rows_here, features)
    )
    grad_query, grad_key, grad_value = attend_back(
        grad_mixed, query_bf, key_full, value_full, dec_lengths, self_lse
    )
    key_sum, value_sum = (
        lax.psum_scatter(
            grad_key.astype(jnp.bfloat16), FSDP, scatter_dimension=1, tiled=True
        ).astype(jnp.float32),
        lax.psum_scatter(
            grad_value.astype(jnp.bfloat16), FSDP, scatter_dimension=1, tiled=True
        ).astype(jnp.float32),
    )
    grad_merged_bf = (
        jnp.concatenate([grad_query, key_sum, value_sum], axis=-1)
        .astype(jnp.bfloat16)
        .reshape(tokens, 3 * features)
    )
    grad_self_in = outer_sum(start_bf, grad_merged_bf)
    merged_sums = jnp.sum(grad_merged_bf.astype(jnp.float32), axis=0)
    grad_start = grad_res1 + times_t(grad_merged_bf, back_in)
    grad_input = grad_start.reshape(groups, rows_here, features)
    seq_sums = jnp.sum(grad_input, axis=1)
    grad_table = lax.dot_general(
        seq_sums,
        onehot,
        (((0,), (0,)), ((), ())),
        precision=lax.Precision.HIGHEST,
        preferred_element_type=jnp.float32,
    )
    grad_biases = jnp.stack(
        [
            merged_sums[:features],
            merged_sums[2 * features :],
            bias_two,
            bias_three,
            bias_four,
            bias_five,
            bias_six,
        ],
        axis=1,
    )
    grad_gains = jnp.stack([gain_one, gain_two, gain_three], axis=1)
    grad_shifts = jnp.stack([shift_one, shift_two, shift_three], axis=1)
    reduced = (
        lax.psum_scatter(grad_table, AXES, scatter_dimension=0, tiled=True),
        lax.psum_scatter(grad_self_in, AXES, scatter_dimension=0, tiled=True),
        lax.psum_scatter(grad_self_out, AXES, scatter_dimension=0, tiled=True),
        lax.psum_scatter(grad_cross_q, AXES, scatter_dimension=0, tiled=True),
        lax.psum_scatter(grad_cross_kv, AXES, scatter_dimension=0, tiled=True),
        lax.psum_scatter(grad_cross_out, AXES, scatter_dimension=0, tiled=True),
        lax.psum_scatter(grad_ffn_in, AXES, scatter_dimension=0, tiled=True),
        lax.psum_scatter(grad_ffn_out, AXES, scatter_dimension=0, tiled=True),
        lax.psum_scatter(grad_biases, AXES, scatter_dimension=0, tiled=True),
        lax.psum_scatter(grad_ffn_bias, AXES, scatter_dimension=0, tiled=True),
        lax.psum_scatter(grad_gains, AXES, scatter_dimension=0, tiled=True),
        lax.psum_scatter(grad_shifts, AXES, scatter_dimension=0, tiled=True),
    )
    return (
        output,
        grad_input,
        grad_encoder,
        reduced[0],
        reduced[1],
        reduced[2],
        reduced[3],
        reduced[4],
        reduced[5],
        reduced[6],
        reduced[7],
        reduced[8],
        reduced[9],
        reduced[10],
        reduced[11],
    )


F32 = jnp.float32
BF16 = jnp.bfloat16


def nt_dot(left, right):
    return lax.dot_general(left, right, (((1,), (1,)), ((), ())), preferred_element_type=F32)


def nn_dot(left, right):
    return jnp.dot(left, right, preferred_element_type=F32)


def split_three(value):
    high = value.astype(BF16)
    rest = value - high.astype(F32)
    middle = rest.astype(BF16)
    return high, middle, (rest - middle.astype(F32)).astype(BF16)


def key_extra(tokens, length):
    lane = lax.broadcasted_iota(jnp.int32, (tokens, 128), 1) % 64
    row = lax.broadcasted_iota(jnp.int32, (tokens, 128), 0)
    masked = jnp.where(row < length, 0.0, -1e30)
    return jnp.where(lane == 3, masked, jnp.where(lane < 3, 1.0, 0.0)).astype(BF16)


def row_extra(lane, head, terms, mask_lane):
    base = head * 64
    out = jnp.where(lane == base + 3, mask_lane, 0.0).astype(F32)
    for place, term in enumerate(terms):
        out = jnp.where(lane == base + place, term.astype(F32), out)
    return out.astype(BF16)


def attend_fwd_core(block, length, q_ref, k_ref, v_ref, o_ref, of_ref, lse_ref, kx_ref, va_ref, vb_ref, between):
    tokens = q_ref.shape[0]
    kx_ref[:, :128] = k_ref[...]
    kx_ref[:, 128:] = key_extra(tokens, length)
    lane_full = lax.broadcasted_iota(jnp.int32, (tokens, 128), 1)
    values = v_ref[...].astype(F32)
    va_ref[...] = jnp.where(lane_full < 64, values, 1.0).astype(BF16)
    vb_ref[...] = jnp.where(lane_full < 64, 1.0, values).astype(BF16)

    for index in range(tokens // block):
        rows = pl.ds(index * block, block)
        lane = lax.broadcasted_iota(jnp.int32, (block, 128), 1)
        query = q_ref[rows, :].astype(F32) * 0.125
        halves, tops, both = [], [], []
        for head in range(2):
            inside = (lane < 64) if head == 0 else (lane >= 64)
            own = jnp.where(inside, query, 0.0).astype(BF16)
            extra = row_extra(lane, head, (), 1.0)
            both.append(nt_dot(jnp.concatenate([own, extra], axis=1), kx_ref[...]))
        for scores, vx_ref in zip(both, (va_ref, vb_ref)):
            top = jnp.max(scores, axis=1, keepdims=True)
            probs = jnp.exp(scores - top).astype(BF16)
            halves.append(nn_dot(probs, vx_ref[...]))
            tops.append(top)
        number = jnp.where(lane < 64, halves[0], halves[1])
        total = pltpu.roll(jnp.where(lane < 64, halves[1], halves[0]), 64, 1)
        out = number / total
        o_ref[rows, :] = out.astype(BF16)
        of_ref[rows, :] = out
        lse_ref[rows, :] = jnp.where(lane < 64, tops[0], tops[1]) + jnp.log(total)
        if index + 1 < tokens // block:
            between()


def attend_bwd_core(
    block, length, q_ref, k_ref, v_ref, do_ref, of_ref, lse_ref, dq_ref, dk_ref, dv_ref,
    kx_ref, vx_ref, kt_ref, dk_acc, dv_acc,
):
    tokens = q_ref.shape[0]
    extra_keys = key_extra(tokens, length)
    kx_ref[:, :128] = k_ref[...]
    kx_ref[:, 128:] = extra_keys
    vx_ref[:, :128] = v_ref[...]
    vx_ref[:, 128:] = extra_keys
    turned = k_ref[...].astype(F32).T
    sub = lax.broadcasted_iota(jnp.int32, (128, tokens), 0)
    kt_ref[0] = jnp.where(sub < 64, turned, 0.0).astype(BF16)
    kt_ref[1] = jnp.where(sub < 64, 0.0, turned).astype(BF16)
    dk_acc[...] = jnp.zeros_like(dk_acc)
    dv_acc[...] = jnp.zeros_like(dv_acc)
    same = (
        lax.broadcasted_iota(jnp.int32, (128, 128), 0) // 64
        == lax.broadcasted_iota(jnp.int32, (128, 128), 1) // 64
    ).astype(F32).astype(BF16)

    def step(index, carry):
        rows = pl.ds(pl.multiple_of(index * block, block), block)
        lane = lax.broadcasted_iota(jnp.int32, (block, 128), 1)
        query = q_ref[rows, :].astype(F32) * 0.125
        grad = do_ref[rows, :].astype(F32)
        inner = grad * of_ref[rows, :]
        inner_high = inner.astype(BF16)
        inner_low = (inner - inner_high.astype(F32)).astype(BF16)
        delta = nn_dot(inner_high, same) + nn_dot(inner_low, same)
        lse_terms = split_three(-lse_ref[rows, :])
        delta_terms = split_three(-delta)
        dq_t = jnp.zeros((128, block), F32)
        own_q, own_g, logits, grads = [], [], [], []
        for head in range(2):
            inside = (lane < 64) if head == 0 else (lane >= 64)
            own_q.append(jnp.where(inside, query, 0.0).astype(BF16))
            own_g.append(jnp.where(inside, grad, 0.0).astype(BF16))
            left_q = jnp.concatenate([own_q[head], row_extra(lane, head, lse_terms, 1.0)], axis=1)
            left_g = jnp.concatenate([own_g[head], row_extra(lane, head, delta_terms, 0.0)], axis=1)
            logits.append(nt_dot(kx_ref[...], left_q))
            grads.append(nt_dot(vx_ref[...], left_g))
        for head in range(2):
            probs = jnp.exp(logits[head])
            dscore = (probs * grads[head]).astype(BF16)
            dv_acc[...] += nn_dot(probs.astype(BF16), own_g[head])
            dk_acc[...] += nn_dot(dscore, own_q[head])
            dq_t = dq_t + nn_dot(kt_ref[head], dscore)
        dq_ref[rows, :] = (dq_t.T * 0.125).astype(BF16)
        return carry

    lax.fori_loop(0, tokens // block, step, 0)
    dk_ref[...] = dk_acc[...].astype(BF16)
    dv_ref[...] = dv_acc[...].astype(BF16)


BIG = pltpu.CompilerParams(vmem_limit_bytes=56 * 1024 * 1024)
SMEM_SPEC = pl.BlockSpec(memory_space=pltpu.SMEM)


def row_stats(residual):
    mean = jnp.mean(residual, axis=1, keepdims=True)
    centered = residual - mean
    inv = lax.rsqrt(jnp.mean(centered * centered, axis=1, keepdims=True) + 1e-05)
    return centered * inv, inv


def norm_back(above, unit, inv, gain):
    scaled = above * gain
    return inv * (
        scaled
        - jnp.mean(scaled, axis=1, keepdims=True)
        - unit * jnp.mean(scaled * unit, axis=1, keepdims=True)
    )


def col_sum(value):
    return jnp.sum(value, axis=0, keepdims=True)


def vec(vec_ref, index):
    return vec_ref[pl.ds(index, 1), :]


LANG_ROW = 13


def ffn_kernel(
    length_ref, cmixed_ref, unit_ref, cot_ref, wco_ref, win_ref, wout_ref, vec_ref, fbias_ref,
    out_ref, res2_ref, gcm_ref, sums_ref, fsum_ref, gfo_ref, gfi_ref, gco_ref,
    act_all, low3_all, two_all, ghid_all, low2_all, cmix_all,
):
    step = pl.program_id(0)
    rows = cmixed_ref.shape[0]
    here = pl.ds(pl.multiple_of(step * rows, rows), rows)
    act_ref, low3_ref, two_ref, ghid_ref, low2_ref = [
        ref.at[here] for ref in (act_all, low3_all, two_all, ghid_all, low2_all)
    ]
    cmix_all[here, :] = cmixed_ref[...]

    @pl.when(step == 0)
    def _():
        sums_ref[...] = jnp.zeros_like(sums_ref)
        fsum_ref[...] = jnp.zeros_like(fsum_ref)

    normed_one = unit_ref[...] * vec(vec_ref, 7) + vec(vec_ref, 10)
    branch = nn_dot(cmixed_ref[...], wco_ref[...]) + vec(vec_ref, 5)
    unit2, inv2 = row_stats(normed_one + branch)
    gain2 = vec(vec_ref, 8)
    normed_two = unit2 * gain2 + vec(vec_ref, 11)
    two = normed_two.astype(BF16)
    two_ref[...] = two
    hidden = nn_dot(two, win_ref[...]) + fbias_ref[...]
    square = hidden * hidden
    tanh = jnp.tanh(0.7978845608028654 * (hidden + 0.044715 * square * hidden))
    half = 0.5 * (1.0 + tanh)
    act = (hidden * half).astype(BF16)
    act_ref[...] = act
    slope = half + (0.5 * 0.7978845608028654) * hidden * (1.0 - tanh * tanh) * (1.0 + 3 * 0.044715 * square)
    unit3, inv3 = row_stats(normed_two + nn_dot(act, wout_ref[...]) + vec(vec_ref, 6))
    gain3 = vec(vec_ref, 9)
    live = (lax.broadcasted_iota(jnp.int32, (rows, 1), 0) + step * rows < length_ref[lax.axis_index(FSDP)]).astype(F32)
    out_ref[...] = ((unit3 * gain3 + vec(vec_ref, 12)) * live).astype(BF16)
    above3 = cot_ref[...].astype(F32) * live
    res3 = norm_back(above3, unit3, inv3, gain3)
    low3 = res3.astype(BF16)
    low3_ref[...] = low3
    ghid = (nt_dot(low3, wout_ref[...]) * slope).astype(BF16)
    ghid_ref[...] = ghid
    above2 = res3 + nt_dot(ghid, win_ref[...])
    res2 = norm_back(above2, unit2, inv2, gain2)
    res2_ref[...] = res2
    low2 = res2.astype(BF16)
    low2_ref[...] = low2
    gcm_ref[...] = nt_dot(low2, wco_ref[...]).astype(BF16)
    for index, value in (
        (6, low3.astype(F32)), (5, low2.astype(F32)), (9, above3 * unit3), (12, above3), (8, above2 * unit2), (11, above2),
    ):
        sums_ref[index : index + 1, :] += col_sum(value)
    fsum_ref[...] += col_sum(ghid.astype(F32))

    @pl.when(step == pl.num_programs(0) - 1)
    def _():
        features = low3_all.shape[1]
        for part in range(act_all.shape[1] // features):
            cols = slice(part * features, part * features + features)
            gfo_ref[cols, :] = turned_dot(act_all[:, cols], low3_all[...]).astype(BF16)
            gfi_ref[:, cols] = turned_dot(two_all[...], ghid_all[:, cols]).astype(BF16)
        gco_ref[...] = turned_dot(cmix_all[...], low2_all[...]).astype(BF16)


def rows_call(kernel, name, tokens, arrays, outs, block=256, scratch=()):
    in_specs, operands = [], []
    for array, kind in arrays:
        operands.append(array)
        if kind == "smem":
            in_specs.append(SMEM_SPEC)
        elif kind == "row":
            in_specs.append(pl.BlockSpec((block, array.shape[1]), lambda i: (i, 0)))
        else:
            in_specs.append(pl.BlockSpec(array.shape, lambda i: (0, 0)))
    out_specs, out_shape = [], []
    for out in outs:
        if len(out) == 2:
            out_specs.append(pl.BlockSpec((block, out[0]), lambda i: (i, 0)))
            out_shape.append(jax.ShapeDtypeStruct((tokens, out[0]), out[1]))
        else:
            out_specs.append(pl.BlockSpec(out[:2], lambda i: (0, 0)))
            out_shape.append(jax.ShapeDtypeStruct(out[:2], out[2]))
    return pl.pallas_call(
        kernel,
        grid=(tokens // block,),
        in_specs=in_specs,
        out_specs=out_specs,
        out_shape=out_shape,
        scratch_shapes=list(scratch),
        compiler_params=BIG,
        name=name,
    )(*operands)


MESH = pl.DeviceIdType.MESH
ANY_SPEC = pl.BlockSpec(memory_space=pl.ANY)
VMEM_SPEC = pl.BlockSpec(memory_space=pltpu.VMEM)
ALONG_Z, ALONG_X, ALONG_Y = 0, 1, 2
EVERY = slice(None)


class Place:
    def __init__(self, depth):
        dp, fsdp = lax.axis_index(DP), lax.axis_index(FSDP)
        self.depth = depth
        self.z, self.x = dp // 2, lax.rem(dp, 2)
        self.y, self.c = fsdp // 2, lax.rem(fsdp, 2)
        self.fsdp = fsdp

    def dev(self, z=None, x=None, y=None, c=None):
        z, x = (self.z if z is None else z), (self.x if x is None else x)
        y, c = (self.y if y is None else y), (self.c if c is None else c)
        return (2 * z + x, 2 * y + c)

    def ahead(self, d):
        return lax.rem(self.z + d, self.depth)

    def behind(self, d):
        return lax.rem(self.z + self.depth - d, self.depth)

    def greet(self):
        others = [self.dev(z=self.ahead(d)) for d in range(1, self.depth)]
        others += [self.dev(x=1 - self.x), self.dev(y=1 - self.y), self.dev(c=1 - self.c)]
        others += [self.dev(y=1 - self.y, c=1 - self.c)]
        barrier = pltpu.get_barrier_semaphore()
        for other in others:
            pl.semaphore_signal(barrier, inc=1, device_id=other, device_id_type=MESH)
        pl.semaphore_wait(barrier, len(others))


def remote(src, dst, send, recv, device):
    return pltpu.make_async_remote_copy(
        src_ref=src, dst_ref=dst, send_sem=send, recv_sem=recv, device_id=device, device_id_type=MESH
    )


class Gather:
    def __init__(self, place, order, src, dst, local, send, recv, cols=None):
        self.place, self.order, self.src, self.dst = place, order, src, dst
        self.local, self.send, self.recv = local, send, recv
        self.cols = cols
        self.sent = []
        self.have = [place.z, place.x, place.y]

    def at(self, zxy, c):
        where = (*zxy, c)
        return self.dst.at[where] if self.cols is None else self.dst.at[(*where, EVERY, self.cols)]

    def instead(self, axis, index):
        return [index if a == axis else h for a, h in enumerate(self.have)]

    def push(self, src, dst, index, device):
        copy = remote(src, dst, self.send.at[index], self.recv.at[index], device)
        copy.start()
        self.sent.append(copy)

    def heard(self, block, index):
        remote(block, block, self.send.at[index], self.recv.at[index], self.place.dev()).wait_recv()

    def to_core(self, zxy, index):
        block = self.at(zxy, self.place.c)
        self.push(block, block, index, self.place.dev(c=1 - self.place.c))

    def start(self, stage, src=None):
        p, axis = self.place, self.order[stage]
        block = self.at(self.have, p.c)
        src = block if src is None else src
        if axis == ALONG_Z:
            for d in range(1, p.depth):
                self.push(src, block, d - 1, p.dev(z=p.ahead(d)))
        else:
            self.push(src, block, p.depth - 2 + axis, p.dev(x=1 - p.x) if axis == ALONG_X else p.dev(y=1 - p.y))

    def parts(self, stage):
        p, axis = self.place, self.order[stage]
        if axis == ALONG_Z:
            return [(self.instead(axis, p.behind(d)), d - 1) for d in range(1, p.depth)]
        other = 1 - (p.x if axis == ALONG_X else p.y)
        return [(self.instead(axis, other), p.depth - 2 + axis)]

    def arrive(self, stage):
        for zxy, index in self.parts(stage):
            self.heard(self.at(zxy, self.place.c), index)
        self.have = self.instead(self.order[stage], EVERY)

    def s0(self):
        p = self.place
        if self.src is None:
            self.start(0)
            return
        src = self.src if self.cols is None else self.src.at[:, self.cols]
        self.copy = pltpu.make_async_copy(src, self.at(self.have, p.c), self.local)
        self.copy.start()
        self.start(0, src)

    def s1(self):
        if self.src is not None:
            self.copy.wait()
        self.arrive(0)
        self.start(1)

    def s2(self):
        self.arrive(1)
        self.start(2)
        self.halfway = list(self.have)
        self.to_core(self.halfway, self.place.depth + 1)

    def s3(self):
        self.rest = [zxy for zxy, _ in self.parts(2)]
        self.arrive(2)
        for i, zxy in enumerate(self.rest):
            self.to_core(zxy, self.place.depth + 2 + i)

    def whole(self):
        p = self.place
        for i, zxy in enumerate((self.halfway, *self.rest)):
            self.heard(self.at(zxy, 1 - p.c), p.depth + 1 + i)

    def finish(self):
        for copy in self.sent:
            copy.wait_send()


class Exchange:
    def __init__(self, place, src, dst, local, send, recv):
        self.place, self.src, self.dst = place, src, dst
        self.local, self.send, self.recv = local, send, recv
        self.rows = src.shape[1]

    def block(self, owner):
        return self.dst.at[pl.ds(pl.multiple_of(owner * self.rows, self.rows), self.rows)]

    def start(self):
        me = self.place.fsdp
        self.copy = pltpu.make_async_copy(self.src.at[me], self.block(me), self.local)
        self.copy.start()
        self.sent = []
        for d in range(1, 4):
            to = lax.rem(me + d, 4)
            copy = remote(
                self.src.at[to], self.block(me), self.send.at[d - 1], self.recv.at[d - 1],
                (lax.axis_index(DP), to),
            )
            copy.start()
            self.sent.append(copy)

    def whole(self):
        self.copy.wait()
        for d in range(1, 4):
            block = self.block(lax.rem(self.place.fsdp + 4 - d, 4))
            remote(block, block, self.send.at[d - 1], self.recv.at[d - 1], self.place.dev()).wait_recv()

    def finish(self):
        for copy in self.sent:
            copy.wait_send()


def flat_cols(ref, cols):
    value = ref[:, :, :, :, :, cols]
    return value.reshape(-1, value.shape[-1])


FFN_ROW = 29


def first_kernel(
    depth,
    dlen_ref, elen_ref, tag_ref, bias_ref, gain_ref, shift_ref, table_ref, fbias_ref,
    in_ref, dec_in, enc_in, cot_in, out_in, cq_in, ckv_in, co_in, fin_in, fout_in,
    w_in, w_out, w_cq, w_ckv, w_co, w_fin, w_fout, enc_out, cot_out, vec_out, fb_out,
    low_out, merged_out, pair_out, mixed_out, mixf_out, lse_out, unit_out, inv_out, one_out, cq_out, cmixed_out, cmixf_out, clse_out,
    small_own, small, win, wkv, wout, wcq, x, enc, cot_wide, cot_low, vecs, fb, low, merged, pair, mixed, mixf, lse,
    unit1, inv1, one, cquery, cmixed, cmixf, clse, kx, va, vb,
    wlocal, wsend, wrecv, elocal, esend, erecv, osem, csem,
):
    p = Place(depth)
    tokens, features = x.shape
    langs = table_ref.shape[1]
    pairs = features // 128
    cot_load = pltpu.make_async_copy(cot_in, cot_wide, csem.at[0])
    cot_load.start()
    tile = small_own
    tile[...] = jnp.zeros_like(tile)
    tile[0:7, :16] = bias_ref[...].astype(F32)
    tile[7:10, :16] = gain_ref[...].astype(F32)
    tile[10:13, :16] = shift_ref[...].astype(F32)
    eye = lax.broadcasted_iota(jnp.int32, (langs, langs), 0) == lax.broadcasted_iota(jnp.int32, (langs, langs), 1)
    tile[LANG_ROW : LANG_ROW + langs, :16] = nt_dot(eye.astype(F32).astype(BF16), table_ref[...])
    tile[FFN_ROW : FFN_ROW + 1, :64] = fbias_ref[...].astype(F32)
    shifted = pltpu.roll(tile[...], 16 * (4 * p.x + 2 * p.y + p.c), 1)
    ffn_row = lax.broadcasted_iota(jnp.int32, tile.shape, 0) == FFN_ROW
    small_tile = jnp.where(ffn_row, pltpu.roll(tile[...], 64 * p.c, 1), shifted).astype(BF16)
    small[p.z, p.x, p.y, p.c] = small_tile
    for i in range(pairs):
        for k in range(3):
            win[i, p.z, p.x, p.y, p.c, :, 128 * k : 128 * k + 128] = in_ref[:, features * k + 128 * i : features * k + 128 * i + 128]
    p.greet()
    jobs = []

    def gather(order, src, dst, cols=None):
        n = len(jobs)
        jobs.append(Gather(p, order, src, dst, wlocal.at[n], wsend.at[n], wrecv.at[n], cols))
        return jobs[-1]

    def part(i):
        return pl.ds(i * features, features)

    def half(i):
        return pl.ds(i * (features // 2), features // 2)

    yzx = (ALONG_Y, ALONG_Z, ALONG_X)
    dec = Exchange(p, dec_in, x, elocal.at[0], esend.at[0], erecv.at[0])
    encode = Exchange(p, enc_in, enc, elocal.at[1], esend.at[1], erecv.at[1])
    cot = Exchange(p, cot_low, cot_out, elocal.at[2], esend.at[2], erecv.at[2])
    g_small = gather(yzx, None, small)
    g_in = [gather(yzx, None, win.at[i]) for i in range(pairs)]
    kv = [gather(yzx, ckv_in, wkv, part(i)) for i in range(2)]
    g_out, g_cq, g_co = gather(yzx, out_in, wout), gather(yzx, cq_in, wcq), gather(yzx, co_in, w_co)
    fi = [gather(yzx, fin_in, w_fin, part(i)) for i in range(4)]
    fo = [gather(yzx, fout_in, w_fout, half(i)) for i in range(2)]

    def move(step, which):
        for job in which:
            step(job)

    writes = []

    def write(src, dst):
        copy = pltpu.make_async_copy(src, dst, osem.at[len(writes)])
        copy.start()
        writes.append(copy)

    queue = [g_small, *g_in, *kv, g_out, g_cq, g_co, *fi, *fo]
    clock = [0]

    def tick(n=1):
        for _ in range(n):
            t = clock[0]
            clock[0] += 1
            for lag, step in ((4, Gather.s3), (2, Gather.s2), (0, Gather.s1)):
                if 0 <= t - lag < len(queue):
                    step(queue[t - lag])

    move(Gather.s0, queue[:10])
    dec.start()
    move(Gather.s0, queue[10:])
    tick(6)
    encode.start()
    g_small.whole()
    spread = []
    for z in range(depth):
        total = None
        for r in range(8):
            where = (z, r // 4, (r // 2) % 2, r % 2)
            tile_r = small[where].astype(F32)
            total = tile_r if total is None else total + tile_r
            at = 128 * (4 * z + r // 2)
            if r % 2 == 0:
                fb[:, at : at + 128] = tile_r[FFN_ROW : FFN_ROW + 1]
            else:
                fb[:, at : at + 128] += tile_r[FFN_ROW : FFN_ROW + 1]
        spread.append(total)
    rows_all = jnp.concatenate(spread, axis=1)
    vecs[...] = rows_all[:16]
    chosen = lax.broadcasted_iota(jnp.int32, (rows_all.shape[0], 1), 0) == tag_ref[p.fsdp] + LANG_ROW
    lang_row = col_sum(jnp.where(chosen, rows_all, 0.0))
    vecs[LANG_ROW : LANG_ROW + 1, :] = lang_row
    write(vecs, vec_out)
    write(fb, fb_out)
    dec.whole()
    low[...] = (x[...].astype(F32) + lang_row).astype(BF16)
    write(low, low_out)

    def project(source, weight, cols, bias, dest):
        whole = flat_cols(weight, cols)

        def tile(i, carry):
            rows = pl.ds(pl.multiple_of(i * 512, 512), 512)
            out = nn_dot(source[rows, :], whole)
            dest[rows, cols] = (out if bias is None else out + bias).astype(BF16)
            return carry

        lax.fori_loop(0, tokens // 512, tile, 0)

    cot_load.wait()
    for j in range(4):
        cot_low[j] = cot_wide[j].astype(BF16)

    def attend(length, q, q_at, kv_ref, k_at, v_at, out, out_wide, out_lse, at, between):
        attend_fwd_core(
            512, length, q.at[:, pl.ds(q_at, 128)], kv_ref.at[:, pl.ds(k_at, 128)], kv_ref.at[:, pl.ds(v_at, 128)],
            out.at[:, pl.ds(at, 128)], out_wide.at[:, pl.ds(at, 128)], out_lse.at[:, pl.ds(at, 128)], kx, va, vb, between,
        )

    dec_len = dlen_ref[p.fsdp]
    for i in range(pairs):
        g_in[i].whole()
        at, wide = 128 * i, 384 * i
        w_pair = flat_cols(win.at[i], EVERY)

        def project_pair(j, carry, at=at, wide=wide, w_pair=w_pair):
            rows = pl.ds(pl.multiple_of(j * 512, 512), 512)
            out = nn_dot(low[rows, :], w_pair)
            merged[rows, wide : wide + 128] = (out[:, :128] + vecs[0:1, at : at + 128]).astype(BF16)
            merged[rows, wide + 128 : wide + 256] = out[:, 128:256].astype(BF16)
            merged[rows, wide + 256 : wide + 384] = (out[:, 256:] + vecs[1:2, at : at + 128]).astype(BF16)
            return carry

        lax.fori_loop(0, tokens // 512, project_pair, 0)
        if i == 1:
            cot.start()
        attend(dec_len, merged, wide, merged, wide + 128, wide + 256, mixed, mixf, lse, at, tick)
        tick()
    for a, b in ((win, w_in), (merged, merged_out), (mixed, mixed_out), (mixf, mixf_out), (lse, lse_out)):
        write(a, b)
    encode.whole()
    write(enc, enc_out)
    kv[0].whole()
    project(enc, wkv, part(0), None, pair)
    kv[1].whole()
    project(enc, wkv, part(1), vecs[4:5, :], pair)
    write(wkv, w_ckv)
    write(pair, pair_out)
    tick()
    move(Gather.whole, (g_out, g_cq))
    write(wout, w_out)
    write(wcq, w_cq)
    out_matrix = flat_cols(wout, EVERY)
    cq_matrix = flat_cols(wcq, EVERY)

    def middle(i, carry):
        rows = pl.ds(pl.multiple_of(i * 256, 256), 256)
        branch = nn_dot(mixed[rows, :], out_matrix) + vecs[2:3, :]
        unit, inv = row_stats(x[rows, :].astype(F32) + lang_row + branch)
        unit1[rows, :] = unit
        inv1[rows, :] = jnp.broadcast_to(inv, (256, 128))
        one_low = (unit * vecs[7:8, :] + vecs[10:11, :]).astype(BF16)
        one[rows, :] = one_low
        cquery[rows, :] = (nn_dot(one_low, cq_matrix) + vecs[3:4, :]).astype(BF16)
        return carry

    lax.fori_loop(0, tokens // 256, middle, 0)
    for a, b in ((unit1, unit_out), (inv1, inv_out), (one, one_out), (cquery, cq_out)):
        write(a, b)
    enc_len = elen_ref[p.fsdp]
    tick()
    for i in range(pairs):
        at = 128 * i
        attend(enc_len, cquery, at, pair, at, features + at, cmixed, cmixf, clse, at, tick)
        tick()
    for a, b in ((cmixed, cmixed_out), (cmixf, cmixf_out), (clse, clse_out)):
        write(a, b)
    move(Gather.whole, (g_co, *fi, *fo))
    cot.whole()
    for job in (*jobs, dec, encode, cot):
        job.finish()
    for copy in writes:
        copy.wait()


def first_call(depth, dlen, elen, tags, biases, gains, shifts, table, fbias, dec, enc, cot, *weights):
    groups, part_rows, features = dec.shape
    tokens = groups * part_rows
    hidden = weights[5].shape[1]

    def full(shape):
        return (depth, 2, 2, 2, *shape)

    def sds(shape, dtype):
        return jax.ShapeDtypeStruct(shape, dtype)

    tf = (tokens, features)
    pairs = features // 128
    packed = (pairs, *full((weights[0].shape[0], 384)))
    outs = [sds(packed, BF16)] + [sds(full(w.shape), BF16) for w in weights[1:]]
    outs += [sds(tf, BF16)] * 2 + [sds((16, features), F32), sds((1, hidden), F32)]
    outs += [sds((tokens, n * features), BF16) for n in (1, 3, 2, 1)] + [sds(tf, F32)] * 2
    outs += [sds(tf, F32), sds((tokens, 128), F32), sds(tf, BF16), sds(tf, BF16), sds(tf, BF16), sds(tf, F32), sds(tf, F32)]
    n_jobs = 16
    dma = pltpu.SemaphoreType.DMA
    shapes = [
        ((32, 128), F32), (full((32, 128)), BF16), (packed, BF16), (full(weights[3].shape), BF16),
        (full(weights[1].shape), BF16), (full(weights[2].shape), BF16),
        (tf, BF16), (tf, BF16), (cot.shape, F32), (cot.shape, BF16), ((16, features), F32), ((1, hidden), F32),
        (tf, BF16), ((tokens, 3 * features), BF16), ((tokens, 2 * features), BF16), (tf, BF16), (tf, F32), (tf, F32),
        (tf, F32), ((tokens, 128), F32), (tf, BF16), (tf, BF16), (tf, BF16), (tf, F32), (tf, F32),
        ((tokens, 256), BF16), ((tokens, 128), BF16), ((tokens, 128), BF16),
    ]
    return pl.pallas_call(
        functools.partial(first_kernel, depth),
        in_specs=[SMEM_SPEC] * 3 + [VMEM_SPEC] * 6 + [ANY_SPEC] * 9,
        out_specs=[ANY_SPEC] * len(outs),
        out_shape=outs,
        scratch_shapes=[pltpu.VMEM(*s) for s in shapes]
        + [dma((n_jobs,)), dma((n_jobs, depth + 5)), dma((n_jobs, depth + 5))]
        + [dma((3,)), dma((3, 3)), dma((3, 3)), dma((24,)), dma((1,))],
        compiler_params=pltpu.CompilerParams(
            vmem_limit_bytes=60 * 1024 * 1024, collective_id=1, has_side_effects=True
        ),
        name="first",
    )(dlen, elen, tags, biases, gains, shifts, table, fbias, weights[0], dec, enc, cot, *weights[1:])


class Scatter:
    def __init__(self, place, full, own, core_buf, x_buf, z_buf, y_buf, send, recv):
        self.place, self.full, self.own = place, full, own
        self.core_buf, self.x_buf, self.z_buf, self.y_buf = core_buf, x_buf, z_buf, y_buf
        self.send, self.recv = send, recv
        self.sent = []

    def push(self, src, dst, index, device):
        copy = remote(src, dst, self.send.at[index], self.recv.at[index], device)
        copy.start()
        self.sent.append(copy)

    def heard(self, block, index):
        remote(block, block, self.send.at[index], self.recv.at[index], self.place.dev()).wait_recv()

    def to_core(self):
        p = self.place
        self.push(self.full.at[:, :, :, 1 - p.c], self.core_buf, 0, p.dev(c=1 - p.c))

    def across_x(self):
        p = self.place
        self.heard(self.core_buf, 0)
        away = 1 - p.x
        for z in range(p.depth):
            total = self.core_buf[z, away].astype(F32) + self.own[z, away].astype(F32)
            self.core_buf[z, away] = total.astype(BF16)
        self.push(self.core_buf.at[:, away], self.x_buf, 1, p.dev(x=away))

    def along_z(self):
        p = self.place
        self.heard(self.x_buf, 1)
        for d in range(1, p.depth):
            z = p.ahead(d)
            total = self.x_buf[z].astype(F32) + self.core_buf[z, p.x].astype(F32) + self.own[z, p.x].astype(F32)
            self.x_buf[z] = total.astype(BF16)
            self.push(self.x_buf.at[z], self.z_buf.at[d - 1], 1 + d, p.dev(z=z))

    def here(self, y):
        p = self.place
        total = self.x_buf[p.z, y].astype(F32) + self.core_buf[p.z, p.x, y].astype(F32)
        total = total + self.own[p.z, p.x, y].astype(F32)
        for d in range(1, p.depth):
            total = total + self.z_buf[d - 1, y].astype(F32)
        return total

    def across_y(self):
        p = self.place
        for d in range(1, p.depth):
            self.heard(self.z_buf.at[d - 1], 1 + d)
        away = 1 - p.y
        self.x_buf[p.z, away] = self.here(away).astype(BF16)
        self.push(self.x_buf.at[p.z, away], self.y_buf, p.depth + 1, p.dev(y=away))

    def result(self):
        self.heard(self.y_buf, self.place.depth + 1)
        return self.here(self.place.y) + self.y_buf[...].astype(F32)

    def finish(self):
        for copy in self.sent:
            copy.wait_send()


class Return:
    def __init__(self, place, src, dst, local, send, recv):
        self.place, self.src, self.dst = place, src, dst
        self.local, self.send, self.recv = local, send, recv
        self.rows = dst.shape[1]
        self.sent = []

    def block(self, owner):
        return self.src.at[pl.ds(pl.multiple_of(owner * self.rows, self.rows), self.rows)]

    def start_one(self, d):
        me = self.place.fsdp
        if d == 0:
            self.copy = pltpu.make_async_copy(self.block(me), self.dst.at[me], self.local)
            self.copy.start()
            return
        to = lax.rem(me + d, 4)
        copy = remote(
            self.block(to), self.dst.at[me], self.send.at[d - 1], self.recv.at[d - 1], (lax.axis_index(DP), to)
        )
        copy.start()
        self.sent.append(copy)

    def start(self):
        for d in (2, 3, 1, 0):
            self.start_one(d)

    def finish(self):
        self.copy.wait()
        for d in range(1, 4):
            block = self.dst.at[lax.rem(self.place.fsdp + 4 - d, 4)]
            remote(block, block, self.send.at[d - 1], self.recv.at[d - 1], self.place.dev()).wait_recv()
        for copy in self.sent:
            copy.wait_send()


def turned_dot(left, right):
    return lax.dot_general(left, right, (((0,), (0,)), ((), ())), preferred_element_type=F32)


def last_kernel(
    depth, langs,
    dlen_ref, elen_ref, tag_ref, sums_in, fsum_in, vec_ref,
    gfo_in, gfi_in, gco_in, output_in, cq_in, pair_in, gcm_in, cmixf_in, clse_in,
    res2_in, unit_in, inv_in, wcq_in, wckv_in, wout_in, enc_in, one_in,
    merged_in, mixf_in, lse_in, mixed_in, low_in, win_in,
    out_ret, gin_ret, genc_ret, r_small, r_in, r_out, r_cq, r_ckv, r_co, r_fi, r_fo,
    cq, pair, gcm, cmixf, clse, res2, unit, inv, wcq, wckv, wout, enc, one, merged, mixed, low, win,
    dcq, dpair, gmix, dmerged, low1, genc_low, gin_low, sums,
    own_fo, own_fi, own_co, full_ckv, full_cq, full_out, full_in, full_small, small_t,
    c_fo, x_fo, z_fo, y_fo, c_fi, x_fi, z_fi, y_fi, c_co, x_co, z_co, y_co, c_ckv, x_ckv, z_ckv, y_ckv,
    c_cq, x_cq, z_cq, y_cq, c_out, x_out, z_out, y_out, c_in, x_in, z_in, y_in, c_sm, x_sm, z_sm, y_sm,
    kx, vx, kt, dk_acc, dv_acc,
    send, recv, rlocal, rsend, rrecv, isem,
):
    p = Place(depth)
    tokens, features = cq.shape
    p_pairs = features // 128
    loads = []

    def load(src, dst):
        copy = pltpu.make_async_copy(src, dst, isem.at[len(loads)])
        copy.start()
        loads.append(copy)
        return copy

    by_pair = []
    for i in range(p_pairs):
        cols = pl.ds(128 * i, 128)
        some = [load(a.at[:, cols], b.at[:, cols]) for a, b in ((cq_in, cq), (gcm_in, gcm), (cmixf_in, cmixf), (clse_in, clse), (pair_in, pair))]
        high = pl.ds(features + 128 * i, 128)
        some.append(load(pair_in.at[:, high], pair.at[:, high]))
        by_pair.append(some)
    early = [load(gfo_in.at[:, :, :, p.c], own_fo), load(gfi_in.at[:, :, :, p.c], own_fi), load(gco_in.at[:, :, :, p.c], own_co)]
    mid = [load(a, b) for a, b in ((wcq_in, wcq), (wckv_in, wckv), (wout_in, wout), (res2_in, res2), (unit_in, unit), (inv_in, inv), (enc_in, enc), (one_in, one))]
    late = [load(a, b) for a, b in ((merged_in, merged), (mixed_in, mixed), (low_in, low), (win_in, win))]
    mixf, lse, total_in = cmixf, clse, res2

    p.greet()
    count = [0]

    def scatter(full, own, *bufs):
        n = count[0]
        count[0] += 1
        return Scatter(p, full, own, *bufs, send.at[n], recv.at[n])

    def inner(full):
        return full.at[:, :, :, p.c]

    fo_rows, fi_cols = own_fo.shape[3] // 2, own_fi.shape[4] // 2
    s_fo = [
        scatter(gfo_in.at[:, :, :, :, rows], own_fo.at[:, :, :, rows], c_fo.at[i], x_fo.at[i], z_fo.at[i], y_fo.at[i])
        for i, rows in ((i, pl.ds(i * fo_rows, fo_rows)) for i in range(2))
    ]
    s_fi = [
        scatter(gfi_in.at[:, :, :, :, :, cols], own_fi.at[:, :, :, :, cols], c_fi.at[i], x_fi.at[i], z_fi.at[i], y_fi.at[i])
        for i, cols in ((i, pl.ds(i * fi_cols, fi_cols)) for i in range(2))
    ]
    s_co = scatter(gco_in, own_co, c_co, x_co, z_co, y_co)
    s_ckv = scatter(full_ckv, inner(full_ckv), c_ckv, x_ckv, z_ckv, y_ckv)
    s_cq = scatter(full_cq, inner(full_cq), c_cq, x_cq, z_cq, y_cq)
    s_out = scatter(full_out, inner(full_out), c_out, x_out, z_out, y_out)
    s_in = [
        scatter(full_in.at[i], inner(full_in.at[i]), c_in.at[i], x_in.at[i], z_in.at[i], y_in.at[i])
        for i in range(p_pairs)
    ]
    s_small = scatter(full_small, inner(full_small), c_sm, x_sm, z_sm, y_sm)
    b_out = Return(p, output_in, out_ret, rlocal.at[0], rsend.at[0], rrecv.at[0])
    b_enc = Return(p, genc_low, genc_ret, rlocal.at[1], rsend.at[1], rrecv.at[1])
    b_in = Return(p, gin_low, gin_ret, rlocal.at[2], rsend.at[2], rrecv.at[2])

    for job in (s_fo[0], s_fi[0], s_fo[1], s_fi[1], s_co):
        job.to_core()
    sums[...] = sums_in[...]

    def backward(length, q, k, v, do, of, ls, dq, dk, dv):
        attend_bwd_core(512, length, q, k, v, do, of, ls, dq, dk, dv, kx, vx, kt, dk_acc, dv_acc)

    def cut(ref, at):
        return ref.at[:, pl.ds(at, 128)]

    plan = [
        [s_fi[0].across_x, s_fo[1].across_x],
        [s_fi[1].across_x, s_co.across_x, s_fo[0].along_z, b_out.start],
        [s_fi[0].along_z, s_fo[1].along_z],
        [s_fi[1].along_z, s_co.along_z, s_fo[0].across_y, s_fi[0].across_y],
    ]

    def move(steps):
        for step in steps:
            step()

    enc_len = elen_ref[p.fsdp]
    for i in range(p_pairs):
        for copy in by_pair[i]:
            copy.wait()
        if i == 0:
            for copy in early:
                copy.wait()
            s_fo[0].across_x()
        at = 128 * i
        backward(
            enc_len, cut(cq, at), cut(pair, at), cut(pair, features + at), cut(gcm, at), cut(cmixf, at), cut(clse, at),
            cut(dcq, at), cut(dpair, at), cut(dpair, features + at),
        )
        move(plan[i])
    late += [load(a, b) for a, b in ((mixf_in, mixf), (lse_in, lse))]
    for copy in mid:
        copy.wait()

    def weight_sum(left, right, full, cols, lead=()):
        value = turned_dot(left, right)
        shape = (depth, 2, 2, 2, value.shape[0] // (8 * depth), value.shape[1])
        full[(*lead, slice(None), slice(None), slice(None), slice(None), slice(None), cols)] = value.astype(BF16).reshape(shape)

    for part in range(2):
        cols = pl.ds(part * features, features)
        weight_sum(enc[...], dpair[:, cols], full_ckv, cols)
    s_ckv.to_core()
    weight_sum(one[...], dcq[...], full_cq, pl.ds(0, features))
    s_cq.to_core()

    def lower(i, carry):
        rows = pl.ds(pl.multiple_of(i * 256, 256), 256)
        genc = nt_dot(dpair[rows, :], wckv[...])
        genc_low[rows, :] = genc.astype(BF16)
        dq = dcq[rows, :]
        above = res2[rows, :] + nt_dot(dq, wcq[...])
        units = unit[rows, :]
        res1 = norm_back(above, units, inv[rows, :1], vec(vec_ref, 7))
        total_in[rows, :] = res1
        low_one = res1.astype(BF16)
        low1[rows, :] = low_one
        gmix[rows, :] = nt_dot(low_one, wout[...]).astype(BF16)
        for index, value in (
            (2, low_one.astype(F32)), (3, dq.astype(F32)), (4, dpair[rows, features:].astype(F32)), (7, above * units), (10, above),
        ):
            sums[index : index + 1, :] += col_sum(value)
        return carry

    lax.fori_loop(0, tokens // 256, lower, 0)
    b_enc.start()
    move([s_ckv.across_x, s_cq.across_x, s_fo[1].across_y, s_fi[1].across_y, s_co.across_y])
    for copy in late:
        copy.wait()
    weight_sum(mixed[...], low1[...], full_out, pl.ds(0, features))
    s_out.to_core()
    plan = [
        [s_out.across_x, s_ckv.along_z, s_cq.along_z],
        [s_in[0].across_x, s_out.along_z, s_ckv.across_y, s_cq.across_y],
        [s_in[1].across_x, s_in[0].along_z, s_out.across_y],
        [s_in[2].across_x, s_in[1].along_z, s_in[0].across_y],
    ]
    dec_len = dlen_ref[p.fsdp]
    for i in range(p_pairs):
        at = 128 * i
        wide = 384 * i
        backward(
            dec_len, cut(merged, wide), cut(merged, wide + 128), cut(merged, wide + 256), cut(gmix, at), cut(mixf, at), cut(lse, at),
            cut(dmerged, wide), cut(dmerged, wide + 128), cut(dmerged, wide + 256),
        )
        move(plan[i])
        weight_sum(low[...], dmerged[:, wide : wide + 384], full_in, slice(None), (i,))
        s_in[i].to_core()
        w_pair = win[i]

        def add_input(j, carry, wide=wide, w_pair=w_pair, last=i == p_pairs - 1):
            rows = pl.ds(pl.multiple_of(j * 256, 256), 256)
            total = total_in[rows, :] + nt_dot(dmerged[rows, wide : wide + 384], w_pair)
            total_in[rows, :] = total
            if last:
                gin_low[rows, :] = total.astype(BF16)
                sums[LANG_ROW : LANG_ROW + 1, :] += col_sum(total)
            return carry

        lax.fori_loop(0, tokens // 256, add_input, 0)
        for part, index in ((0, 0), (2, 1)):
            block = dmerged[:, wide + 128 * part : wide + 128 * part + 128].astype(F32)
            sums[index : index + 1, at : at + 128] = col_sum(block)
    b_in.start()
    move([s_in[3].across_x, s_in[2].along_z, s_in[1].across_y])
    small_t[...] = jnp.zeros_like(small_t)
    small_t[:16, :] = sums[...]
    place_tag = lax.broadcasted_iota(jnp.int32, (langs + 3, 1), 0) == tag_ref[p.fsdp]
    small_t[LANG_ROW : LANG_ROW + langs + 3, :] = jnp.where(place_tag, sums[LANG_ROW : LANG_ROW + 1, :], 0.0)
    columns = small_t[...].T.astype(BF16)
    full_small[:, :, :, :, :16, :] = columns.reshape(depth, 2, 2, 2, 16, 128)
    top = lax.broadcasted_iota(jnp.int32, (16, 128), 0) == 0
    for r in range(depth * 8):
        lanes = slice(128 * (r // 2), 128 * (r // 2) + 128)
        tile = jnp.where(top, fsum_in[:, lanes], 0.0)
        full_small[r // 8, (r // 4) % 2, (r // 2) % 2, r % 2, 16:32, :] = tile.astype(BF16)
    s_small.to_core()
    for i in range(2):
        r_fo[i * fo_rows : (i + 1) * fo_rows, :] = s_fo[i].result()
        r_fi[:, i * fi_cols : (i + 1) * fi_cols] = s_fi[i].result()
    r_co[...] = s_co.result()
    r_ckv[...] = s_ckv.result()
    move([s_small.across_x, s_in[3].along_z])
    r_cq[...] = s_cq.result()
    r_out[...] = s_out.result()
    move([s_in[2].across_y, s_small.along_z, s_in[3].across_y, s_small.across_y])
    for i in range(p_pairs):
        value = s_in[i].result()
        for part in range(3):
            at = part * features + 128 * i
            r_in[:, at : at + 128] = value[:, 128 * part : 128 * part + 128]
    r_small[...] = s_small.result()
    for job in (*s_fo, *s_fi, s_co, s_ckv, s_cq, s_out, *s_in, s_small, b_out, b_enc, b_in):
        job.finish()


def last_call(depth, langs, hidden, part_rows, dlen, elen, tags, sums, fsum, vecs, *arrays):
    tokens, features = arrays[4].shape
    pairs = features // 128
    groups = tokens // part_rows

    def sds(shape, dtype):
        return jax.ShapeDtypeStruct(shape, dtype)

    rows = features // (8 * depth)
    frows = hidden // (8 * depth)
    outs = [sds((groups, part_rows, features), BF16)] * 3
    outs += [
        sds((32, 128), F32), sds((rows, 3 * features), F32), sds((rows, features), F32), sds((rows, features), F32),
        sds((rows, 2 * features), F32), sds((rows, features), F32), sds((rows, hidden), F32), sds((frows, features), F32),
    ]

    def bufs(r, c, lead=()):
        return [
            pltpu.VMEM((*lead, depth, 2, 2, r, c), BF16), pltpu.VMEM((*lead, depth, 2, r, c), BF16),
            pltpu.VMEM((*lead, depth - 1, 2, r, c), BF16), pltpu.VMEM((*lead, r, c), BF16),
        ]

    def like(a):
        return pltpu.VMEM(a.shape, a.dtype)

    scratch = [like(a) for i, a in enumerate(arrays[4:]) if i not in (14, 15)]
    scratch += [
        pltpu.VMEM((tokens, features), BF16), pltpu.VMEM((tokens, 2 * features), BF16), pltpu.VMEM((tokens, features), BF16),
        pltpu.VMEM((tokens, 3 * features), BF16), pltpu.VMEM((tokens, features), BF16),
        pltpu.VMEM((tokens, features), BF16), pltpu.VMEM((tokens, features), BF16), pltpu.VMEM((16, features), F32),
        pltpu.VMEM((depth, 2, 2, frows, features), BF16), pltpu.VMEM((depth, 2, 2, rows, hidden), BF16), pltpu.VMEM((depth, 2, 2, rows, features), BF16),
        pltpu.VMEM((depth, 2, 2, 2, rows, 2 * features), BF16), pltpu.VMEM((depth, 2, 2, 2, rows, features), BF16), pltpu.VMEM((depth, 2, 2, 2, rows, features), BF16),
        pltpu.VMEM((pairs, depth, 2, 2, 2, rows, 384), BF16), pltpu.VMEM((depth, 2, 2, 2, 32, 128), BF16), pltpu.VMEM((128, features), F32),
    ]
    scratch += bufs(frows // 2, features, (2,)) + bufs(rows, hidden // 2, (2,)) + bufs(rows, features) + bufs(rows, 2 * features)
    scratch += bufs(rows, features) + bufs(rows, features) + bufs(rows, 384, (pairs,)) + bufs(32, 128)
    scratch += [
        pltpu.VMEM((tokens, 256), BF16), pltpu.VMEM((tokens, 256), BF16), pltpu.VMEM((2, 128, tokens), BF16),
        pltpu.VMEM((tokens, 128), F32), pltpu.VMEM((tokens, 128), F32),
        pltpu.SemaphoreType.DMA((pairs + 9, depth + 2)), pltpu.SemaphoreType.DMA((pairs + 9, depth + 2)),
        pltpu.SemaphoreType.DMA((3,)), pltpu.SemaphoreType.DMA((3, 3)), pltpu.SemaphoreType.DMA((3, 3)),
        pltpu.SemaphoreType.DMA((6 * pairs + 17,)),
    ]
    return pl.pallas_call(
        functools.partial(last_kernel, depth, langs),
        in_specs=[SMEM_SPEC] * 3 + [VMEM_SPEC] * 3 + [ANY_SPEC] * len(arrays),
        out_specs=[ANY_SPEC] * 3 + [VMEM_SPEC] * 8,
        out_shape=outs,
        scratch_shapes=scratch,
        compiler_params=pltpu.CompilerParams(
            vmem_limit_bytes=60 * 1024 * 1024, collective_id=2, has_side_effects=True
        ),
        name="last",
    )(dlen, elen, tags, sums, fsum, vecs, *arrays)


def finish_kernel(
    out_in, gin_in, genc_in, small_in, in_in, wout_in, cq_in, ckv_in, co_in, fi_in, fo_in,
    out, gin, genc, bias, gain, shift, table, fbias, r_in, r_out, r_cq, r_ckv, r_co, r_fi, r_fo, square,
):
    out[...] = out_in[...]
    gin[...] = gin_in[...].astype(F32)
    genc[...] = genc_in[...].astype(F32)

    @pl.when(pl.program_id(0) == 0)
    def _():
        for src, dst in (
            (in_in, r_in), (wout_in, r_out), (cq_in, r_cq), (ckv_in, r_ckv), (co_in, r_co), (fi_in, r_fi), (fo_in, r_fo),
        ):
            dst[...] = src[...]
        square[...] = jnp.zeros_like(square)
        square[:32, :] = small_in[...]
        turned = square[...].T
        bias[...] = turned[0:7, :16]
        gain[...] = turned[7:10, :16]
        shift[...] = turned[10:13, :16]
        table[...] = pltpu.roll(small_in[:16, :], 128 - LANG_ROW, 1)[:, : table.shape[1]]
        core = lax.rem(lax.axis_index(FSDP), 2)
        row = small_in[16:24, :]
        fbias[...] = jnp.where(core == 0, row, pltpu.roll(row, 64, 1))[0:1, :64]


def finish_call(langs, output, gin, genc, small, *sums):
    groups, part_rows, features = output.shape

    def block(a):
        return pl.BlockSpec((1, part_rows, features), lambda i: (i, 0, 0))

    def whole(a):
        return pl.BlockSpec(a.shape, lambda i: (0, 0))

    def sds(*shape):
        return jax.ShapeDtypeStruct(shape, F32)

    smalls = [sds(7, 16), sds(3, 16), sds(3, 16), sds(16, langs), sds(1, 64)]
    outs = [jax.ShapeDtypeStruct(output.shape, BF16), sds(*gin.shape), sds(*genc.shape), *smalls]
    outs += [sds(*a.shape) for a in sums]
    return pl.pallas_call(
        finish_kernel,
        grid=(groups,),
        in_specs=[block(a) for a in (output, gin, genc)] + [whole(a) for a in (small, *sums)],
        out_specs=[block(a) for a in (output, gin, genc)] + [whole(a) for a in (*smalls, *sums)],
        out_shape=outs,
        scratch_shapes=[pltpu.VMEM((128, 128), F32)],
        compiler_params=BIG,
        name="finish",
    )(output, gin, genc, small, *sums)


def fast_body(
    dec_input, enc_output, dec_lengths, enc_lengths, lang_tags, lang_table, self_in, self_out, cross_q, cross_kv,
    cross_out, ffn_in, ffn_out, biases, ffn_bias, norm_gains, norm_shifts, cotangent,
):
    groups, part_rows, features = dec_input.shape
    tokens = groups * part_rows
    hidden = ffn_in.shape[1]
    langs = lang_table.shape[1]
    depth = lax.axis_size(DP) // 2
    (
        w_in, w_out, w_cq, w_ckv, w_co, w_fin, w_fout, enc, cot, vecs, fbias, low, merged, pair, mixed, mixed_f32, self_lse,
        unit1, inv1, one, cquery, cmixed, cmixed_f32, cross_lse,
    ) = first_call(
        depth, dec_lengths, enc_lengths, lang_tags, biases.T, norm_gains.T, norm_shifts.T, lang_table, ffn_bias[None],
        dec_input, enc_output, cotangent, self_in, self_out, cross_q, cross_kv, cross_out, ffn_in, ffn_out,
    )
    w_in = w_in.reshape(w_in.shape[0], -1, w_in.shape[-1])
    w_out, w_cq, w_ckv, w_co, w_fin, w_fout = [
        w.reshape(-1, w.shape[-1]) for w in (w_out, w_cq, w_ckv, w_co, w_fin, w_fout)
    ]
    output, res2, gcm, sums, fsum, g_fout, g_fin, g_co = rows_call(
        ffn_kernel, "ffn", tokens,
        [(dec_lengths, "smem"), (cmixed, "row"), (unit1, "row"), (cot, "row"), (w_co, "all"), (w_fin, "all"), (w_fout, "all"), (vecs, "all"), (fbias, "all")],
        [(features, BF16), (features, F32), (features, BF16), (16, features, F32), (1, hidden, F32), (hidden, features, BF16), (features, hidden, BF16), (features, features, BF16)],
        scratch=[pltpu.VMEM((tokens, n), BF16) for n in (hidden, features, features, hidden, features, features)],
    )
    full = (depth, 2, 2, 2)
    g_fout, g_fin, g_co = [g.reshape(*full, g.shape[0] // (8 * depth), g.shape[1]) for g in (g_fout, g_fin, g_co)]
    moved = last_call(
        depth, langs, hidden, part_rows, dec_lengths, enc_lengths, lang_tags, sums, fsum, vecs,
        g_fout, g_fin, g_co, output, cquery, pair, gcm, cmixed_f32, cross_lse, res2, unit1, inv1, w_cq, w_ckv, w_out, enc, one,
        merged, mixed_f32, self_lse, mixed, low, w_in,
    )
    output, gin, genc, bias, gain, shift, table, g_fbias, *sums = finish_call(langs, *moved)
    return (output, gin, genc, table, *sums, bias.T, g_fbias.reshape(-1), gain.T, shift.T)


def solution(mesh):
    def either(*args):
        whole_sequences = mesh.shape[FSDP] == args[0].shape[0] == 4 and mesh.shape[DP] % 2 == 0
        whole_sequences = whole_sequences and args[6].shape[0] == 16
        return (fast_body if whole_sequences else body)(*args)

    return jax.shard_map(
        either,
        mesh=mesh,
        in_specs=(
            P(DP, FSDP, None),
            P(DP, FSDP, None),
            P(DP),
            P(DP),
            P(DP),
            P(AXES, None),
            P(AXES, None),
            P(AXES, None),
            P(AXES, None),
            P(AXES, None),
            P(AXES, None),
            P(AXES, None),
            P(AXES, None),
            P(AXES, None),
            P(AXES),
            P(AXES, None),
            P(AXES, None),
            P(DP, FSDP, None),
        ),
        out_specs=(
            P(DP, FSDP, None),
            P(DP, FSDP, None),
            P(DP, FSDP, None),
            P(AXES, None),
            P(AXES, None),
            P(AXES, None),
            P(AXES, None),
            P(AXES, None),
            P(AXES, None),
            P(AXES, None),
            P(AXES, None),
            P(AXES, None),
            P(AXES),
            P(AXES, None),
            P(AXES, None),
        ),
        check_vma=False,
    )
```

```python
import functools
import math

import jax
import jax.numpy as jnp
from jax import lax
from jax.experimental import pallas as pl
from jax.experimental.pallas import tpu as pltpu
from jax.sharding import PartitionSpec as P

HEADS = 8
DP, FSDP = AXES = ("dp", "fsdp")


def smooth_gelu(values):
    return (
        0.5
        * values
        * (1.0 + jnp.tanh(0.7978845608028654 * (values + 0.044715 * values * values * values)))
    )


def times_t(left, right):
    return lax.dot_general(
        left, right, (((1,), (1,)), ((), ())), preferred_element_type=jnp.float32
    )


def outer_sum(left, right):
    return lax.dot_general(
        left, right, (((0,), (0,)), ((), ())), preferred_element_type=jnp.float32
    )


def normalize_rows(residual, gain_col, shift_col):
    row_mean = jnp.mean(residual, axis=-1, keepdims=True)
    centered = residual - row_mean
    inv_dev = lax.rsqrt(jnp.mean(centered * centered, axis=-1, keepdims=True) + 1e-05)
    unit_rows = centered * inv_dev
    return (unit_rows * gain_col + shift_col, unit_rows, inv_dev)


def normalize_back(grad_above, unit_rows, inv_dev, gain_col):
    grad_unit = grad_above * gain_col
    grad_res = inv_dev * (
        grad_unit
        - jnp.mean(grad_unit, axis=-1, keepdims=True)
        - unit_rows * jnp.mean(grad_unit * unit_rows, axis=-1, keepdims=True)
    )
    return (grad_res, jnp.sum(grad_above * unit_rows, axis=0), jnp.sum(grad_above, axis=0))


def masked_scores(query_bf, key_full, lengths_here):
    groups, rows_here, features = query_bf.shape
    key_count = key_full.shape[1]
    head_size = features // HEADS
    query_heads = query_bf.reshape(groups, rows_here, HEADS, head_size)
    key_heads = key_full.reshape(groups, key_count, HEADS, head_size)
    scores = jnp.einsum(
        "sqhd,skhd->shqk", query_heads, key_heads, preferred_element_type=jnp.float32
    ) * (1.0 / math.sqrt(head_size))
    key_valid = jnp.arange(key_count)[None, :] < lengths_here[:, None]
    return jnp.where(key_valid[:, None, None, :], scores, -1000000000.0)


def attend_forward(query_bf, key_full, value_full, lengths_here):
    groups, rows_here, features = query_bf.shape
    key_count = key_full.shape[1]
    value_heads = value_full.reshape(groups, key_count, HEADS, features // HEADS)
    scores = masked_scores(query_bf, key_full, lengths_here)
    row_max = jnp.max(scores, axis=-1, keepdims=True)
    exp_scores = jnp.exp(scores - row_max)
    row_total = jnp.sum(exp_scores, axis=-1, keepdims=True)
    probs_bf = (exp_scores / row_total).astype(jnp.bfloat16)
    attn_mixed = jnp.einsum(
        "shqk,skhd->sqhd", probs_bf, value_heads, preferred_element_type=jnp.float32
    )
    return (attn_mixed.reshape(groups, rows_here, features), row_max + jnp.log(row_total))


def attend_back(grad_mixed_bf, query_bf, key_full, value_full, lengths_here, log_total):
    groups, rows_here, features = query_bf.shape
    key_count = key_full.shape[1]
    head_size = features // HEADS
    query_heads = query_bf.reshape(groups, rows_here, HEADS, head_size)
    key_heads = key_full.reshape(groups, key_count, HEADS, head_size)
    value_heads = value_full.reshape(groups, key_count, HEADS, head_size)
    grad_heads = grad_mixed_bf.reshape(groups, rows_here, HEADS, head_size)
    attn_probs = jnp.exp(masked_scores(query_bf, key_full, lengths_here) - log_total)
    probs_bf = attn_probs.astype(jnp.bfloat16)
    grad_probs = jnp.einsum(
        "sqhd,skhd->shqk", grad_heads, value_heads, preferred_element_type=jnp.float32
    )
    grad_values = jnp.einsum(
        "shqk,sqhd->skhd", probs_bf, grad_heads, preferred_element_type=jnp.float32
    )
    grad_scores = attn_probs * (
        grad_probs - jnp.sum(attn_probs * grad_probs, axis=-1, keepdims=True)
    )
    grad_scores_bf = grad_scores.astype(jnp.bfloat16)
    score_scale = 1.0 / math.sqrt(head_size)
    grad_query = (
        jnp.einsum("shqk,skhd->sqhd", grad_scores_bf, key_heads, preferred_element_type=jnp.float32)
        * score_scale
    )
    grad_keys = (
        jnp.einsum(
            "shqk,sqhd->skhd", grad_scores_bf, query_heads, preferred_element_type=jnp.float32
        )
        * score_scale
    )
    return (
        grad_query.reshape(groups, rows_here, features),
        grad_keys.reshape(groups, key_count, features),
        grad_values.reshape(groups, key_count, features),
    )


def body(
    dec_input,
    enc_output,
    dec_lengths,
    enc_lengths,
    lang_tags,
    lang_table,
    self_in,
    self_out,
    cross_q,
    cross_kv,
    cross_out,
    ffn_in,
    ffn_out,
    biases,
    ffn_bias,
    norm_gains,
    norm_shifts,
    cotangent,
):
    full_weights = (
        lax.all_gather(lang_table, AXES, axis=0, tiled=True),
        lax.all_gather(self_in, AXES, axis=0, tiled=True),
        lax.all_gather(self_out, AXES, axis=0, tiled=True),
        lax.all_gather(cross_q, AXES, axis=0, tiled=True),
        lax.all_gather(cross_kv, AXES, axis=0, tiled=True),
        lax.all_gather(cross_out, AXES, axis=0, tiled=True),
        lax.all_gather(ffn_in, AXES, axis=0, tiled=True),
        lax.all_gather(ffn_out, AXES, axis=0, tiled=True),
        lax.all_gather(biases, AXES, axis=0, tiled=True),
        lax.all_gather(ffn_bias, AXES, axis=0, tiled=True),
        lax.all_gather(norm_gains, AXES, axis=0, tiled=True),
        lax.all_gather(norm_shifts, AXES, axis=0, tiled=True),
    )
    (
        full_table,
        full_in,
        full_out,
        full_cq,
        full_ckv,
        full_co,
        full_ffn_in,
        full_ffn_out,
        full_biases,
        full_ffn_bias,
        full_gains,
        full_shifts,
    ) = full_weights
    bias_cols = full_biases.astype(jnp.float32)
    gain_cols = full_gains.astype(jnp.float32)
    shift_cols = full_shifts.astype(jnp.float32)
    groups, rows_here, features = dec_input.shape
    enc_rows = enc_output.shape[1]
    tokens = groups * rows_here
    positions = lax.axis_index(FSDP) * rows_here + jnp.arange(rows_here)
    live_rows = (positions[None, :] < dec_lengths[:, None]).astype(jnp.float32)
    live_flat = live_rows.reshape(tokens, 1)
    onehot = (lang_tags[:, None] == jnp.arange(full_table.shape[1])[None, :]).astype(jnp.float32)
    lang_rows = lax.dot_general(
        onehot,
        full_table.astype(jnp.float32),
        (((1,), (1,)), ((), ())),
        precision=lax.Precision.HIGHEST,
        preferred_element_type=jnp.float32,
    )
    flat_start = (dec_input.astype(jnp.float32) + lang_rows[:, None, :]).reshape(tokens, features)
    start_bf = flat_start.astype(jnp.bfloat16)
    zeros_row = jnp.zeros((features,), jnp.float32)
    merged = (
        jnp.dot(start_bf, full_in, preferred_element_type=jnp.float32)
        + jnp.concatenate([bias_cols[:, 0], zeros_row, bias_cols[:, 1]])[None, :]
    )
    merged_bf = merged.astype(jnp.bfloat16).reshape(groups, rows_here, 3 * features)
    query_bf = merged_bf[:, :, :features]
    key_own = merged_bf[:, :, features : 2 * features]
    value_own = merged_bf[:, :, 2 * features :]
    key_full, value_full = (
        lax.all_gather(key_own, FSDP, axis=1, tiled=True),
        lax.all_gather(value_own, FSDP, axis=1, tiled=True),
    )
    attn_mixed, self_lse = attend_forward(query_bf, key_full, value_full, dec_lengths)
    mixed_bf = attn_mixed.astype(jnp.bfloat16).reshape(tokens, features)
    branch = jnp.dot(mixed_bf, full_out, preferred_element_type=jnp.float32) + bias_cols[:, 2]
    normed_one, unit_one, inv_one = normalize_rows(
        flat_start + branch, gain_cols[:, 0], shift_cols[:, 0]
    )
    one_bf = normed_one.astype(jnp.bfloat16)
    cross_query = (
        (jnp.dot(one_bf, full_cq, preferred_element_type=jnp.float32) + bias_cols[:, 3])
        .astype(jnp.bfloat16)
        .reshape(groups, rows_here, features)
    )
    enc_flat = enc_output.reshape(groups * enc_rows, features)
    cross_pair = (
        jnp.dot(enc_flat, full_ckv, preferred_element_type=jnp.float32)
        + jnp.concatenate([zeros_row, bias_cols[:, 4]])[None, :]
    )
    pair_bf = cross_pair.astype(jnp.bfloat16).reshape(groups, enc_rows, 2 * features)
    ckey_own = pair_bf[:, :, :features]
    cvalue_own = pair_bf[:, :, features:]
    ckey_full, cvalue_full = (
        lax.all_gather(ckey_own, FSDP, axis=1, tiled=True),
        lax.all_gather(cvalue_own, FSDP, axis=1, tiled=True),
    )
    cross_mixed, cross_lse = attend_forward(cross_query, ckey_full, cvalue_full, enc_lengths)
    cmixed_bf = cross_mixed.astype(jnp.bfloat16).reshape(tokens, features)
    cross_branch = jnp.dot(cmixed_bf, full_co, preferred_element_type=jnp.float32) + bias_cols[:, 5]
    normed_two, unit_two, inv_two = normalize_rows(
        normed_one + cross_branch, gain_cols[:, 1], shift_cols[:, 1]
    )
    two_bf = normed_two.astype(jnp.bfloat16)
    hidden = jnp.dot(
        two_bf, full_ffn_in, preferred_element_type=jnp.float32
    ) + full_ffn_bias.astype(jnp.float32)
    activated, gelu_pull = jax.vjp(smooth_gelu, hidden)
    act_bf = activated.astype(jnp.bfloat16)
    ffn_branch = jnp.dot(act_bf, full_ffn_out, preferred_element_type=jnp.float32) + bias_cols[:, 6]
    normed_three, unit_three, inv_three = normalize_rows(
        normed_two + ffn_branch, gain_cols[:, 2], shift_cols[:, 2]
    )
    output = (normed_three * live_flat).astype(jnp.bfloat16).reshape(groups, rows_here, features)
    back_weights = (
        lax.all_gather(lang_table, AXES, axis=0, tiled=True),
        lax.all_gather(self_in, AXES, axis=0, tiled=True),
        lax.all_gather(self_out, AXES, axis=0, tiled=True),
        lax.all_gather(cross_q, AXES, axis=0, tiled=True),
        lax.all_gather(cross_kv, AXES, axis=0, tiled=True),
        lax.all_gather(cross_out, AXES, axis=0, tiled=True),
        lax.all_gather(ffn_in, AXES, axis=0, tiled=True),
        lax.all_gather(ffn_out, AXES, axis=0, tiled=True),
        lax.all_gather(biases, AXES, axis=0, tiled=True),
        lax.all_gather(ffn_bias, AXES, axis=0, tiled=True),
        lax.all_gather(norm_gains, AXES, axis=0, tiled=True),
        lax.all_gather(norm_shifts, AXES, axis=0, tiled=True),
    )
    back_in = back_weights[1]
    back_out = back_weights[2]
    back_cq = back_weights[3]
    back_ckv = back_weights[4]
    back_co = back_weights[5]
    back_ffn_in = back_weights[6]
    back_ffn_out = back_weights[7]
    back_gains = back_weights[10].astype(jnp.float32)
    grad_above = cotangent.reshape(tokens, features) * live_flat
    grad_res3, gain_three, shift_three = normalize_back(
        grad_above, unit_three, inv_three, back_gains[:, 2]
    )
    grad_low3 = grad_res3.astype(jnp.bfloat16)
    grad_ffn_out = outer_sum(act_bf, grad_low3)
    bias_six = jnp.sum(grad_low3.astype(jnp.float32), axis=0)
    grad_act = times_t(grad_low3, back_ffn_out)
    grad_hidden_bf = gelu_pull(grad_act)[0].astype(jnp.bfloat16)
    grad_ffn_in = outer_sum(two_bf, grad_hidden_bf)
    grad_ffn_bias = jnp.sum(grad_hidden_bf.astype(jnp.float32), axis=0)
    grad_two = grad_res3 + times_t(grad_hidden_bf, back_ffn_in)
    grad_res2, gain_two, shift_two = normalize_back(grad_two, unit_two, inv_two, back_gains[:, 1])
    grad_low2 = grad_res2.astype(jnp.bfloat16)
    grad_cross_out = outer_sum(cmixed_bf, grad_low2)
    bias_five = jnp.sum(grad_low2.astype(jnp.float32), axis=0)
    grad_cmixed = (
        times_t(grad_low2, back_co).astype(jnp.bfloat16).reshape(groups, rows_here, features)
    )
    grad_cquery, grad_ckey, grad_cvalue = attend_back(
        grad_cmixed, cross_query, ckey_full, cvalue_full, enc_lengths, cross_lse
    )
    ckey_sum, cvalue_sum = (
        lax.psum_scatter(
            grad_ckey.astype(jnp.bfloat16), FSDP, scatter_dimension=1, tiled=True
        ).astype(jnp.float32),
        lax.psum_scatter(
            grad_cvalue.astype(jnp.bfloat16), FSDP, scatter_dimension=1, tiled=True
        ).astype(jnp.float32),
    )
    grad_pair_bf = (
        jnp.concatenate([ckey_sum, cvalue_sum], axis=-1)
        .astype(jnp.bfloat16)
        .reshape(groups * enc_rows, 2 * features)
    )
    grad_cross_kv = outer_sum(enc_flat, grad_pair_bf)
    bias_four = jnp.sum(grad_pair_bf[:, features:].astype(jnp.float32), axis=0)
    grad_encoder = times_t(grad_pair_bf, back_ckv).reshape(groups, enc_rows, features)
    grad_cquery_bf = grad_cquery.astype(jnp.bfloat16).reshape(tokens, features)
    grad_cross_q = outer_sum(one_bf, grad_cquery_bf)
    bias_three = jnp.sum(grad_cquery_bf.astype(jnp.float32), axis=0)
    grad_one = grad_res2 + times_t(grad_cquery_bf, back_cq)
    grad_res1, gain_one, shift_one = normalize_back(grad_one, unit_one, inv_one, back_gains[:, 0])
    grad_low1 = grad_res1.astype(jnp.bfloat16)
    grad_self_out = outer_sum(mixed_bf, grad_low1)
    bias_two = jnp.sum(grad_low1.astype(jnp.float32), axis=0)
    grad_mixed = (
        times_t(grad_low1, back_out).astype(jnp.bfloat16).reshape(groups, rows_here, features)
    )
    grad_query, grad_key, grad_value = attend_back(
        grad_mixed, query_bf, key_full, value_full, dec_lengths, self_lse
    )
    key_sum, value_sum = (
        lax.psum_scatter(
            grad_key.astype(jnp.bfloat16), FSDP, scatter_dimension=1, tiled=True
        ).astype(jnp.float32),
        lax.psum_scatter(
            grad_value.astype(jnp.bfloat16), FSDP, scatter_dimension=1, tiled=True
        ).astype(jnp.float32),
    )
    grad_merged_bf = (
        jnp.concatenate([grad_query, key_sum, value_sum], axis=-1)
        .astype(jnp.bfloat16)
        .reshape(tokens, 3 * features)
    )
    grad_self_in = outer_sum(start_bf, grad_merged_bf)
    merged_sums = jnp.sum(grad_merged_bf.astype(jnp.float32), axis=0)
    grad_start = grad_res1 + times_t(grad_merged_bf, back_in)
    grad_input = grad_start.reshape(groups, rows_here, features)
    seq_sums = jnp.sum(grad_input, axis=1)
    grad_table = lax.dot_general(
        seq_sums,
        onehot,
        (((0,), (0,)), ((), ())),
        precision=lax.Precision.HIGHEST,
        preferred_element_type=jnp.float32,
    )
    grad_biases = jnp.stack(
        [
            merged_sums[:features],
            merged_sums[2 * features :],
            bias_two,
            bias_three,
            bias_four,
            bias_five,
            bias_six,
        ],
        axis=1,
    )
    grad_gains = jnp.stack([gain_one, gain_two, gain_three], axis=1)
    grad_shifts = jnp.stack([shift_one, shift_two, shift_three], axis=1)
    reduced = (
        lax.psum_scatter(grad_table, AXES, scatter_dimension=0, tiled=True),
        lax.psum_scatter(grad_self_in, AXES, scatter_dimension=0, tiled=True),
        lax.psum_scatter(grad_self_out, AXES, scatter_dimension=0, tiled=True),
        lax.psum_scatter(grad_cross_q, AXES, scatter_dimension=0, tiled=True),
        lax.psum_scatter(grad_cross_kv, AXES, scatter_dimension=0, tiled=True),
        lax.psum_scatter(grad_cross_out, AXES, scatter_dimension=0, tiled=True),
        lax.psum_scatter(grad_ffn_in, AXES, scatter_dimension=0, tiled=True),
        lax.psum_scatter(grad_ffn_out, AXES, scatter_dimension=0, tiled=True),
        lax.psum_scatter(grad_biases, AXES, scatter_dimension=0, tiled=True),
        lax.psum_scatter(grad_ffn_bias, AXES, scatter_dimension=0, tiled=True),
        lax.psum_scatter(grad_gains, AXES, scatter_dimension=0, tiled=True),
        lax.psum_scatter(grad_shifts, AXES, scatter_dimension=0, tiled=True),
    )
    return (
        output,
        grad_input,
        grad_encoder,
        reduced[0],
        reduced[1],
        reduced[2],
        reduced[3],
        reduced[4],
        reduced[5],
        reduced[6],
        reduced[7],
        reduced[8],
        reduced[9],
        reduced[10],
        reduced[11],
    )


F32 = jnp.float32
BF16 = jnp.bfloat16


def nt_dot(left, right):
    return lax.dot_general(left, right, (((1,), (1,)), ((), ())), preferred_element_type=F32)


def nn_dot(left, right):
    return jnp.dot(left, right, preferred_element_type=F32)


def split_three(value):
    high = value.astype(BF16)
    rest = value - high.astype(F32)
    middle = rest.astype(BF16)
    return high, middle, (rest - middle.astype(F32)).astype(BF16)


def key_extra(tokens, length):
    lane = lax.broadcasted_iota(jnp.int32, (tokens, 128), 1) % 64
    row = lax.broadcasted_iota(jnp.int32, (tokens, 128), 0)
    masked = jnp.where(row < length, 0.0, -1e30)
    return jnp.where(lane == 3, masked, jnp.where(lane < 3, 1.0, 0.0)).astype(BF16)


def row_extra(lane, head, terms, mask_lane):
    base = head * 64
    out = jnp.where(lane == base + 3, mask_lane, 0.0).astype(F32)
    for place, term in enumerate(terms):
        out = jnp.where(lane == base + place, term.astype(F32), out)
    return out.astype(BF16)


def attend_fwd_core(block, length, q_ref, k_ref, v_ref, o_ref, of_ref, lse_ref, kx_ref, va_ref, vb_ref, between):
    tokens = q_ref.shape[0]
    kx_ref[:, :128] = k_ref[...]
    kx_ref[:, 128:] = key_extra(tokens, length)
    lane_full = lax.broadcasted_iota(jnp.int32, (tokens, 128), 1)
    values = v_ref[...].astype(F32)
    va_ref[...] = jnp.where(lane_full < 64, values, 1.0).astype(BF16)
    vb_ref[...] = jnp.where(lane_full < 64, 1.0, values).astype(BF16)

    for index in range(tokens // block):
        rows = pl.ds(index * block, block)
        lane = lax.broadcasted_iota(jnp.int32, (block, 128), 1)
        query = q_ref[rows, :].astype(F32) * 0.125
        halves, tops, both = [], [], []
        for head in range(2):
            inside = (lane < 64) if head == 0 else (lane >= 64)
            own = jnp.where(inside, query, 0.0).astype(BF16)
            extra = row_extra(lane, head, (), 1.0)
            both.append(nt_dot(jnp.concatenate([own, extra], axis=1), kx_ref[...]))
        for scores, vx_ref in zip(both, (va_ref, vb_ref)):
            top = jnp.max(scores, axis=1, keepdims=True)
            probs = jnp.exp(scores - top).astype(BF16)
            halves.append(nn_dot(probs, vx_ref[...]))
            tops.append(top)
        number = jnp.where(lane < 64, halves[0], halves[1])
        total = pltpu.roll(jnp.where(lane < 64, halves[1], halves[0]), 64, 1)
        out = number / total
        o_ref[rows, :] = out.astype(BF16)
        of_ref[rows, :] = out
        lse_ref[rows, :] = jnp.where(lane < 64, tops[0], tops[1]) + jnp.log(total)
        if index + 1 < tokens // block:
            between()


def attend_bwd_core(
    chunk, length, q_ref, k_ref, v_ref, do_ref, of_ref, lse_ref, dq_ref, dk_ref, dv_ref, kx_ref, vx_ref, kt_ref, dk_acc, dv_acc, between,
):
    tokens = q_ref.shape[0]
    extra_keys = key_extra(tokens, length)
    kx_ref[:, :128] = k_ref[...]
    kx_ref[:, 128:] = extra_keys
    vx_ref[:, :128] = v_ref[...]
    vx_ref[:, 128:] = extra_keys
    turned = k_ref[...].astype(F32).T
    sub = lax.broadcasted_iota(jnp.int32, (128, tokens), 0)
    kt_ref[0] = jnp.where(sub < 64, turned, 0.0).astype(BF16)
    kt_ref[1] = jnp.where(sub < 64, 0.0, turned).astype(BF16)
    dk_acc[...] = jnp.zeros_like(dk_acc)
    dv_acc[...] = jnp.zeros_like(dv_acc)
    same = (
        lax.broadcasted_iota(jnp.int32, (128, 128), 0) // 64
        == lax.broadcasted_iota(jnp.int32, (128, 128), 1) // 64
    ).astype(F32).astype(BF16)
    lane = lax.broadcasted_iota(jnp.int32, (tokens, 128), 1)
    query = q_ref[...].astype(F32) * 0.125
    grad = do_ref[...].astype(F32)
    inner = grad * of_ref[...]
    inner_high = inner.astype(BF16)
    inner_low = (inner - inner_high.astype(F32)).astype(BF16)
    delta = nn_dot(inner_high, same) + nn_dot(inner_low, same)
    lse_terms = split_three(-lse_ref[...])
    delta_terms = split_three(-delta)
    own_q, own_g, left_q, left_g = [], [], [], []
    for head in range(2):
        inside = (lane < 64) if head == 0 else (lane >= 64)
        own_q.append(jnp.where(inside, query, 0.0).astype(BF16))
        own_g.append(jnp.where(inside, grad, 0.0).astype(BF16))
        left_q.append(jnp.concatenate([own_q[head], row_extra(lane, head, lse_terms, 1.0)], axis=1))
        left_g.append(jnp.concatenate([own_g[head], row_extra(lane, head, delta_terms, 0.0)], axis=1))
    dq_t = jnp.zeros((128, tokens), F32)

    def front(keys, head):
        return nt_dot(kx_ref[keys, :], left_q[head]), nt_dot(vx_ref[keys, :], left_g[head])

    units = [(pl.ds(start, chunk), head) for start in range(0, tokens, chunk) for head in range(2)]
    following = front(*units[0])
    for index, (keys, head) in enumerate(units):
        logits, grads = following
        if index + 1 < len(units):
            following = front(*units[index + 1])
        probs = jnp.exp(logits)
        dscore = (probs * grads).astype(BF16)
        dv_acc[keys, :] += nn_dot(probs.astype(BF16), own_g[head])
        dk_acc[keys, :] += nn_dot(dscore, own_q[head])
        dq_t = dq_t + nn_dot(kt_ref[head, :, keys], dscore)
        between()
    dq_ref[...] = (dq_t.T * 0.125).astype(BF16)
    dk_ref[...] = dk_acc[...].astype(BF16)
    dv_ref[...] = dv_acc[...].astype(BF16)


BIG = pltpu.CompilerParams(vmem_limit_bytes=56 * 1024 * 1024)
SMEM_SPEC = pl.BlockSpec(memory_space=pltpu.SMEM)


def row_stats(residual):
    mean = jnp.mean(residual, axis=1, keepdims=True)
    centered = residual - mean
    inv = lax.rsqrt(jnp.mean(centered * centered, axis=1, keepdims=True) + 1e-05)
    return centered * inv, inv


def norm_back(above, unit, inv, gain):
    scaled = above * gain
    return inv * (
        scaled
        - jnp.mean(scaled, axis=1, keepdims=True)
        - unit * jnp.mean(scaled * unit, axis=1, keepdims=True)
    )


def col_sum(value):
    return jnp.sum(value, axis=0, keepdims=True)


def vec(vec_ref, index):
    return vec_ref[pl.ds(index, 1), :]


LANG_ROW = 13


def turned_dot(left, right):
    return lax.dot_general(left, right, (((0,), (0,)), ((), ())), preferred_element_type=F32)


def ffn_rows(
    rows, live, cmixed_ref, unit_ref, cot_ref, wco, win, wout, vec_ref, fbias_ref,
    out_ref, act_refs, low3_ref, two_ref, ghid_refs, res2_ref, low2_ref, gcm_ref, sums_ref, fsum_ref,
):
    normed_one = unit_ref[rows, :] * vec(vec_ref, 7) + vec(vec_ref, 10)
    branch = nn_dot(cmixed_ref[rows, :], wco) + vec(vec_ref, 5)
    unit2, inv2 = row_stats(normed_one + branch)
    gain2 = vec(vec_ref, 8)
    normed_two = unit2 * gain2 + vec(vec_ref, 11)
    two = normed_two.astype(BF16)
    two_ref[rows, :] = two
    hidden = nn_dot(two, win) + fbias_ref[...]
    square = hidden * hidden
    tanh = jnp.tanh(0.7978845608028654 * (hidden + 0.044715 * square * hidden))
    half = 0.5 * (1.0 + tanh)
    act = (hidden * half).astype(BF16)
    width = out_ref.shape[1]
    for i, ref in enumerate(act_refs):
        ref[rows, :] = act[:, i * width : (i + 1) * width]
    slope = half + (0.5 * 0.7978845608028654) * hidden * (1.0 - tanh * tanh) * (1.0 + 3 * 0.044715 * square)
    unit3, inv3 = row_stats(normed_two + nn_dot(act, wout) + vec(vec_ref, 6))
    gain3 = vec(vec_ref, 9)
    out_ref[rows, :] = ((unit3 * gain3 + vec(vec_ref, 12)) * live).astype(BF16)
    above3 = cot_ref[rows, :].astype(F32) * live
    res3 = norm_back(above3, unit3, inv3, gain3)
    low3 = res3.astype(BF16)
    low3_ref[rows, :] = low3
    ghid = (nt_dot(low3, wout) * slope).astype(BF16)
    for i, ref in enumerate(ghid_refs):
        ref[rows, :] = ghid[:, i * width : (i + 1) * width]
    above2 = res3 + nt_dot(ghid, win)
    res2 = norm_back(above2, unit2, inv2, gain2)
    res2_ref[rows, :] = res2
    low2 = res2.astype(BF16)
    low2_ref[rows, :] = low2
    gcm_ref[rows, :] = nt_dot(low2, wco).astype(BF16)
    for index, value in (
        (6, low3.astype(F32)), (5, low2.astype(F32)), (9, above3 * unit3), (12, above3), (8, above2 * unit2), (11, above2),
    ):
        sums_ref[index : index + 1, :] += col_sum(value)
    fsum_ref[...] += col_sum(ghid.astype(F32))


MESH = pl.DeviceIdType.MESH
ANY_SPEC = pl.BlockSpec(memory_space=pl.ANY)
VMEM_SPEC = pl.BlockSpec(memory_space=pltpu.VMEM)
ALONG_Z, ALONG_X, ALONG_Y = 0, 1, 2
EVERY = slice(None)


class Place:
    def __init__(self, depth):
        dp, fsdp = lax.axis_index(DP), lax.axis_index(FSDP)
        self.depth = depth
        self.z, self.x = dp // 2, lax.rem(dp, 2)
        self.y, self.c = fsdp // 2, lax.rem(fsdp, 2)
        self.fsdp = fsdp

    def dev(self, z=None, x=None, y=None, c=None):
        z, x = (self.z if z is None else z), (self.x if x is None else x)
        y, c = (self.y if y is None else y), (self.c if c is None else c)
        return (2 * z + x, 2 * y + c)

    def ahead(self, d):
        return lax.rem(self.z + d, self.depth)

    def behind(self, d):
        return lax.rem(self.z + self.depth - d, self.depth)

    def greet(self):
        others = [self.dev(z=self.ahead(d)) for d in range(1, self.depth)]
        others += [self.dev(x=1 - self.x), self.dev(y=1 - self.y), self.dev(c=1 - self.c)]
        others += [self.dev(y=1 - self.y, c=1 - self.c)]
        barrier = pltpu.get_barrier_semaphore()
        for other in others:
            pl.semaphore_signal(barrier, inc=1, device_id=other, device_id_type=MESH)

    def meet(self):
        pl.semaphore_wait(pltpu.get_barrier_semaphore(), self.depth + 3)


def remote(src, dst, send, recv, device):
    return pltpu.make_async_remote_copy(
        src_ref=src, dst_ref=dst, send_sem=send, recv_sem=recv, device_id=device, device_id_type=MESH
    )


class Gather:
    def __init__(self, place, order, src, dst, local, send, recv, cols=None):
        self.place, self.order, self.src, self.dst = place, order, src, dst
        self.local, self.send, self.recv = local, send, recv
        self.cols = cols
        self.sent = []
        self.have = [place.z, place.x, place.y]

    def at(self, zxy, c):
        where = (*zxy, c)
        return self.dst.at[where] if self.cols is None else self.dst.at[(*where, EVERY, self.cols)]

    def instead(self, axis, index):
        return [index if a == axis else h for a, h in enumerate(self.have)]

    def push(self, src, dst, index, device):
        copy = remote(src, dst, self.send.at[index], self.recv.at[index], device)
        copy.start()
        self.sent.append(copy)

    def heard(self, block, index):
        remote(block, block, self.send.at[index], self.recv.at[index], self.place.dev()).wait_recv()

    def to_core(self, zxy, index):
        block = self.at(zxy, self.place.c)
        self.push(block, block, index, self.place.dev(c=1 - self.place.c))

    def start(self, stage, src=None):
        p, axis = self.place, self.order[stage]
        block = self.at(self.have, p.c)
        src = block if src is None else src
        if axis == ALONG_Z:
            for d in range(1, p.depth):
                self.push(src, block, d - 1, p.dev(z=p.ahead(d)))
        else:
            self.push(src, block, p.depth - 2 + axis, p.dev(x=1 - p.x) if axis == ALONG_X else p.dev(y=1 - p.y))

    def parts(self, stage):
        p, axis = self.place, self.order[stage]
        if axis == ALONG_Z:
            return [(self.instead(axis, p.behind(d)), d - 1) for d in range(1, p.depth)]
        other = 1 - (p.x if axis == ALONG_X else p.y)
        return [(self.instead(axis, other), p.depth - 2 + axis)]

    def arrive(self, stage):
        for zxy, index in self.parts(stage):
            self.heard(self.at(zxy, self.place.c), index)
        self.have = self.instead(self.order[stage], EVERY)

    def s0(self):
        p = self.place
        if self.src is None:
            self.start(0)
            return
        src = self.src if self.cols is None else self.src.at[:, self.cols]
        self.copy = pltpu.make_async_copy(src, self.at(self.have, p.c), self.local)
        self.copy.start()
        self.start(0, src)

    def s1(self):
        if self.src is not None:
            self.copy.wait()
        self.arrive(0)
        self.start(1)

    def s2(self):
        self.arrive(1)
        self.start(2)
        self.halfway = list(self.have)
        self.to_core(self.halfway, self.place.depth + 1)

    def s3(self):
        self.rest = [zxy for zxy, _ in self.parts(2)]
        self.arrive(2)
        for i, zxy in enumerate(self.rest):
            self.to_core(zxy, self.place.depth + 2 + i)

    def whole(self):
        p = self.place
        for i, zxy in enumerate((self.halfway, *self.rest)):
            self.heard(self.at(zxy, 1 - p.c), p.depth + 1 + i)

    def finish(self):
        for copy in self.sent:
            copy.wait_send()


class Exchange:
    def __init__(self, place, src, dst, local, send, recv):
        self.place, self.src, self.dst = place, src, dst
        self.local, self.send, self.recv = local, send, recv
        self.rows = src.shape[1]

    def block(self, owner):
        return self.dst.at[pl.ds(pl.multiple_of(owner * self.rows, self.rows), self.rows)]

    def start(self):
        me = self.place.fsdp
        self.copy = pltpu.make_async_copy(self.src.at[me], self.block(me), self.local)
        self.copy.start()
        self.sent = []
        for d in range(1, 4):
            to = lax.rem(me + d, 4)
            copy = remote(
                self.src.at[to], self.block(me), self.send.at[d - 1], self.recv.at[d - 1],
                (lax.axis_index(DP), to),
            )
            copy.start()
            self.sent.append(copy)

    def whole(self):
        self.copy.wait()
        for d in range(1, 4):
            block = self.block(lax.rem(self.place.fsdp + 4 - d, 4))
            remote(block, block, self.send.at[d - 1], self.recv.at[d - 1], self.place.dev()).wait_recv()

    def finish(self):
        for copy in self.sent:
            copy.wait_send()


def flat_cols(ref, cols):
    value = ref[:, :, :, :, :, cols]
    return value.reshape(-1, value.shape[-1])


FFN_ROW = 29


def first_kernel(
    depth,
    dlen_ref, elen_ref, tag_ref, bias_ref, gain_ref, shift_ref, table_ref, fbias_ref,
    in_ref, dec_in, enc_in, cot_in, out_in, cq_in, ckv_in, co_in, fin_in, fout_in,
    w_in, w_out, w_cq, w_ckv, enc_out, vec_out, low_out, merged_out, pair_out, mixed_out, mixf_out, lse_out, unit_out, inv_out, one_out, cq_out,
    cmixf_out, clse_out, out_out, res2_out, gcm_out, sums_out, fsum_out, gfo_out, gfi_out, gco_out,
    small_own, small, win, wkv, wout, wcq, w_co, w_fin, w_fout, cot_seq, x, enc, cot_low, vecs, fb, low, merged, pair, mixed, mixf, lse,
    unit1, inv1, one, cquery, cmixed, cmixf, clse, ghid_two, ghid_three, sums, fsum, kx, va, vb,
    wlocal, wsend, wrecv, elocal, esend, erecv, osem, csem,
):
    p = Place(depth)
    p.greet()
    tokens, features = x.shape
    langs = table_ref.shape[1]
    pairs = features // 128
    cot_loads = [
        pltpu.make_async_copy(cot_in.at[j], unit1.at[pl.ds(256 * j, 256)], csem.at[j]) for j in range(4)
    ]
    for copy in cot_loads:
        copy.start()
    tile = small_own
    tile[...] = jnp.zeros_like(tile)
    tile[0:7, :16] = bias_ref[...].astype(F32)
    tile[7:10, :16] = gain_ref[...].astype(F32)
    tile[10:13, :16] = shift_ref[...].astype(F32)
    eye = lax.broadcasted_iota(jnp.int32, (langs, langs), 0) == lax.broadcasted_iota(jnp.int32, (langs, langs), 1)
    tile[LANG_ROW : LANG_ROW + langs, :16] = nt_dot(eye.astype(F32).astype(BF16), table_ref[...])
    tile[FFN_ROW : FFN_ROW + 1, :64] = fbias_ref[...].astype(F32)
    shifted = pltpu.roll(tile[...], 16 * (4 * p.x + 2 * p.y + p.c), 1)
    ffn_row = lax.broadcasted_iota(jnp.int32, tile.shape, 0) == FFN_ROW
    small_tile = jnp.where(ffn_row, pltpu.roll(tile[...], 64 * p.c, 1), shifted).astype(BF16)
    small[p.z, p.x, p.y, p.c] = small_tile
    for i in range(pairs):
        for k in range(3):
            win[i, p.z, p.x, p.y, p.c, :, 128 * k : 128 * k + 128] = in_ref[:, features * k + 128 * i : features * k + 128 * i + 128]
    p.meet()
    jobs = []

    def gather(order, src, dst, cols=None):
        n = len(jobs)
        jobs.append(Gather(p, order, src, dst, wlocal.at[n], wsend.at[n], wrecv.at[n], cols))
        return jobs[-1]

    def part(i):
        return pl.ds(i * features, features)

    def half(i):
        return pl.ds(i * (features // 2), features // 2)

    yzx = (ALONG_Y, ALONG_Z, ALONG_X)
    dec = Exchange(p, dec_in, x, elocal.at[0], esend.at[0], erecv.at[0])
    encode = Exchange(p, enc_in, enc, elocal.at[1], esend.at[1], erecv.at[1])
    cot = Exchange(p, cot_low, cot_seq, elocal.at[2], esend.at[2], erecv.at[2])
    g_small = gather(yzx, None, small)
    g_in = [gather(yzx, None, win.at[i]) for i in range(pairs)]
    kv = [gather(yzx, ckv_in, wkv, part(i)) for i in range(2)]
    g_out, g_cq, g_co = gather(yzx, out_in, wout), gather(yzx, cq_in, wcq), gather(yzx, co_in, w_co)
    fi = [gather(yzx, fin_in, w_fin, part(i)) for i in range(4)]
    fo = [gather(yzx, fout_in, w_fout, half(i)) for i in range(2)]

    def move(step, which):
        for job in which:
            step(job)

    writes, done = [], [0]

    def write(src, dst):
        copy = pltpu.make_async_copy(src, dst, osem.at[len(writes)])
        copy.start()
        writes.append(copy)

    def written():
        for copy in writes[done[0] :]:
            copy.wait()
        done[0] = len(writes)

    queue = [g_small, *g_in, *kv, g_out, g_cq, g_co, *fi, *fo]
    clock = [0]

    def tick(n=1):
        for _ in range(n):
            t = clock[0]
            clock[0] += 1
            for lag, step in ((4, Gather.s3), (2, Gather.s2), (0, Gather.s1)):
                if 0 <= t - lag < len(queue):
                    step(queue[t - lag])

    move(Gather.s0, queue[:10])
    dec.start()
    move(Gather.s0, queue[10:])
    tick(6)
    encode.start()
    g_small.whole()
    spread = []
    for z in range(depth):
        total = None
        for r in range(8):
            where = (z, r // 4, (r // 2) % 2, r % 2)
            tile_r = small[where].astype(F32)
            total = tile_r if total is None else total + tile_r
            at = 128 * (4 * z + r // 2)
            if r % 2 == 0:
                fb[:, at : at + 128] = tile_r[FFN_ROW : FFN_ROW + 1]
            else:
                fb[:, at : at + 128] += tile_r[FFN_ROW : FFN_ROW + 1]
        spread.append(total)
    rows_all = jnp.concatenate(spread, axis=1)
    vecs[...] = rows_all[:16]
    chosen = lax.broadcasted_iota(jnp.int32, (rows_all.shape[0], 1), 0) == tag_ref[p.fsdp] + LANG_ROW
    lang_row = col_sum(jnp.where(chosen, rows_all, 0.0))
    vecs[LANG_ROW : LANG_ROW + 1, :] = lang_row
    write(vecs, vec_out)
    dec.whole()
    low[...] = (x[...].astype(F32) + lang_row).astype(BF16)
    write(low, low_out)

    def project(source, weight, cols, bias, dest):
        whole = flat_cols(weight, cols)

        def tile(i, carry):
            rows = pl.ds(pl.multiple_of(i * 512, 512), 512)
            out = nn_dot(source[rows, :], whole)
            dest[rows, cols] = (out if bias is None else out + bias).astype(BF16)
            return carry

        lax.fori_loop(0, tokens // 512, tile, 0)

    for j in range(4):
        cot_loads[j].wait()
        cot_low[j] = unit1[256 * j : 256 * j + 256, :].astype(BF16)

    def attend(length, q, q_at, kv_ref, k_at, v_at, out, out_wide, out_lse, at, between):
        attend_fwd_core(
            512, length, q.at[:, pl.ds(q_at, 128)], kv_ref.at[:, pl.ds(k_at, 128)], kv_ref.at[:, pl.ds(v_at, 128)],
            out.at[:, pl.ds(at, 128)], out_wide.at[:, pl.ds(at, 128)], out_lse.at[:, pl.ds(at, 128)], kx, va, vb, between,
        )

    dec_len = dlen_ref[p.fsdp]
    for i in range(pairs):
        g_in[i].whole()
        at, wide = 128 * i, 384 * i
        w_pair = flat_cols(win.at[i], EVERY)

        def project_pair(j, carry, at=at, wide=wide, w_pair=w_pair):
            rows = pl.ds(pl.multiple_of(j * 512, 512), 512)
            out = nn_dot(low[rows, :], w_pair)
            merged[rows, wide : wide + 128] = (out[:, :128] + vecs[0:1, at : at + 128]).astype(BF16)
            merged[rows, wide + 128 : wide + 256] = out[:, 128:256].astype(BF16)
            merged[rows, wide + 256 : wide + 384] = (out[:, 256:] + vecs[1:2, at : at + 128]).astype(BF16)
            return carry

        lax.fori_loop(0, tokens // 512, project_pair, 0)
        if i == 1:
            cot.start()
        attend(dec_len, merged, wide, merged, wide + 128, wide + 256, mixed, mixf, lse, at, tick)
        tick()
    for a, b in ((win, w_in), (merged, merged_out), (mixed, mixed_out), (mixf, mixf_out), (lse, lse_out)):
        write(a, b)
    encode.whole()
    write(enc, enc_out)
    kv[0].whole()
    project(enc, wkv, part(0), None, pair)
    kv[1].whole()
    project(enc, wkv, part(1), vecs[4:5, :], pair)
    write(wkv, w_ckv)
    write(pair, pair_out)
    tick()
    move(Gather.whole, (g_out, g_cq))
    write(wout, w_out)
    write(wcq, w_cq)
    out_matrix = flat_cols(wout, EVERY)
    cq_matrix = flat_cols(wcq, EVERY)

    def middle(i, carry):
        rows = pl.ds(pl.multiple_of(i * 256, 256), 256)
        branch = nn_dot(mixed[rows, :], out_matrix) + vecs[2:3, :]
        unit, inv = row_stats(x[rows, :].astype(F32) + lang_row + branch)
        unit1[rows, :] = unit
        inv1[rows, :] = jnp.broadcast_to(inv, (256, 128))
        one_low = (unit * vecs[7:8, :] + vecs[10:11, :]).astype(BF16)
        one[rows, :] = one_low
        cquery[rows, :] = (nn_dot(one_low, cq_matrix) + vecs[3:4, :]).astype(BF16)
        return carry

    lax.fori_loop(0, tokens // 256, middle, 0)
    for a, b in ((unit1, unit_out), (inv1, inv_out), (one, one_out), (cquery, cq_out)):
        write(a, b)
    enc_len = elen_ref[p.fsdp]
    tick()
    for i in range(pairs):
        at = 128 * i
        attend(enc_len, cquery, at, pair, at, features + at, cmixed, cmixf, clse, at, tick)
        tick()
    written()
    for a, b in ((cmixf, cmixf_out), (clse, clse_out)):
        write(a, b)
    low3, two, low2 = [merged.at[:, part(i)] for i in range(3)]
    gcm, output = [pair.at[:, part(i)] for i in range(2)]
    res2 = mixf
    act, ghid = (x, enc, low, mixed), (one, cquery, ghid_two, ghid_three)
    sums[...] = jnp.zeros_like(sums)
    fsum[...] = jnp.zeros_like(fsum)
    cot.whole()
    move(Gather.whole, (g_co, *fi, *fo))
    co_matrix, fin_matrix, fout_matrix = [flat_cols(w, EVERY) for w in (w_co, w_fin, w_fout)]

    def ffn(i, carry):
        start = pl.multiple_of(i * 256, 256)
        live = (lax.broadcasted_iota(jnp.int32, (256, 1), 0) + start < dec_len).astype(F32)
        ffn_rows(
            pl.ds(start, 256), live, cmixed, unit1, cot_seq, co_matrix, fin_matrix, fout_matrix, vecs, fb,
            output, act, low3, two, ghid, res2, low2, gcm, sums, fsum,
        )
        return carry

    lax.fori_loop(0, tokens // 256, ffn, 0)
    for a, b in ((output, out_out), (res2, res2_out), (gcm, gcm_out), (sums, sums_out), (fsum, fsum_out)):
        write(a, b)
    for job in (*jobs, dec, encode, cot):
        job.finish()
    gco, gfi, gfo = w_co, w_fin, w_fout
    per_slab = gfo.shape[1] * gfo.shape[2] * gfo.shape[3] * gfo.shape[4]
    for i in range(len(act)):
        value = turned_dot(act[i][...], low3[...]).astype(BF16)
        for j in range(features // per_slab):
            slab = value[j * per_slab : (j + 1) * per_slab]
            gfo[i * (features // per_slab) + j] = slab.reshape(gfo.shape[1:])
    write(gfo, gfo_out)
    for i in range(len(ghid)):
        value = turned_dot(two[...], ghid[i][...]).astype(BF16)
        gfi[:, :, :, :, :, i * features : (i + 1) * features] = value.reshape(gco.shape)
    write(gfi, gfi_out)
    gco[...] = turned_dot(cmixed[...], low2[...]).astype(BF16).reshape(gco.shape)
    write(gco, gco_out)
    written()


def first_call(depth, dlen, elen, tags, biases, gains, shifts, table, fbias, dec, enc, cot, *weights):
    groups, part_rows, features = dec.shape
    tokens = groups * part_rows
    hidden = weights[5].shape[1]

    def full(shape):
        return (depth, 2, 2, 2, *shape)

    def sds(shape, dtype):
        return jax.ShapeDtypeStruct(shape, dtype)

    tf = (tokens, features)
    pairs = features // 128
    packed = (pairs, *full((weights[0].shape[0], 384)))
    full_of = [full(w.shape) for w in weights]
    outs = [sds(packed, BF16)] + [sds(s, BF16) for s in full_of[1:4]]
    outs += [sds(tf, BF16), sds((16, features), F32)]
    outs += [sds((tokens, n * features), BF16) for n in (1, 3, 2, 1)] + [sds(tf, F32)] * 2
    outs += [sds(tf, F32), sds((tokens, 128), F32), sds(tf, BF16), sds(tf, BF16), sds(tf, F32), sds(tf, F32)]
    outs += [sds(tf, BF16), sds(tf, F32), sds(tf, BF16), sds((16, features), F32), sds((1, hidden), F32)]
    outs += [sds(full_of[6], BF16), sds(full_of[5], BF16), sds(full_of[4], BF16)]
    n_jobs = 16
    dma = pltpu.SemaphoreType.DMA
    shapes = [
        ((32, 128), F32), (full((32, 128)), BF16), (packed, BF16), (full(weights[3].shape), BF16),
        (full_of[1], BF16), (full_of[2], BF16), (full_of[4], BF16), (full_of[5], BF16), (full_of[6], BF16), (tf, BF16),
        (tf, BF16), (tf, BF16), (cot.shape, BF16), ((16, features), F32), ((1, hidden), F32),
        (tf, BF16), ((tokens, 3 * features), BF16), ((tokens, 2 * features), BF16), (tf, BF16), (tf, F32), (tf, F32),
        (tf, F32), ((tokens, 128), F32), (tf, BF16), (tf, BF16), (tf, BF16), (tf, F32), (tf, F32),
        (tf, BF16), (tf, BF16),
        ((16, features), F32), ((1, hidden), F32), ((tokens, 256), BF16), ((tokens, 128), BF16), ((tokens, 128), BF16),
    ]
    return pl.pallas_call(
        functools.partial(first_kernel, depth),
        in_specs=[SMEM_SPEC] * 3 + [VMEM_SPEC] * 6 + [ANY_SPEC] * 9,
        out_specs=[ANY_SPEC] * len(outs),
        out_shape=outs,
        scratch_shapes=[pltpu.VMEM(*s) for s in shapes]
        + [dma((n_jobs,)), dma((n_jobs, depth + 5)), dma((n_jobs, depth + 5))]
        + [dma((3,)), dma((3, 3)), dma((3, 3)), dma((32,)), dma((4,))],
        compiler_params=pltpu.CompilerParams(
            vmem_limit_bytes=60 * 1024 * 1024, collective_id=1, has_side_effects=True
        ),
        name="first",
    )(dlen, elen, tags, biases, gains, shifts, table, fbias, weights[0], dec, enc, cot, *weights[1:])


class Scatter:
    def __init__(self, place, full, own, core_buf, x_buf, z_buf, y_buf, send, recv):
        self.place, self.full, self.own = place, full, own
        self.core_buf, self.x_buf, self.z_buf, self.y_buf = core_buf, x_buf, z_buf, y_buf
        self.send, self.recv = send, recv
        self.sent = []

    def push(self, src, dst, index, device):
        copy = remote(src, dst, self.send.at[index], self.recv.at[index], device)
        copy.start()
        self.sent.append(copy)

    def heard(self, block, index):
        remote(block, block, self.send.at[index], self.recv.at[index], self.place.dev()).wait_recv()

    def to_core(self):
        p = self.place
        self.push(self.full.at[:, :, :, 1 - p.c], self.core_buf, 0, p.dev(c=1 - p.c))

    def across_x(self):
        p = self.place
        self.heard(self.core_buf, 0)
        away = 1 - p.x
        for z in range(p.depth):
            total = self.core_buf[z, away].astype(F32) + self.own[z, away].astype(F32)
            self.core_buf[z, away] = total.astype(BF16)
        self.push(self.core_buf.at[:, away], self.x_buf, 1, p.dev(x=away))

    def along_z(self):
        p = self.place
        self.heard(self.x_buf, 1)
        for d in range(1, p.depth):
            z = p.ahead(d)
            total = self.x_buf[z].astype(F32) + self.core_buf[z, p.x].astype(F32) + self.own[z, p.x].astype(F32)
            self.x_buf[z] = total.astype(BF16)
            self.push(self.x_buf.at[z], self.z_buf.at[d - 1], 1 + d, p.dev(z=z))

    def here(self, y):
        p = self.place
        total = self.x_buf[p.z, y].astype(F32) + self.core_buf[p.z, p.x, y].astype(F32)
        total = total + self.own[p.z, p.x, y].astype(F32)
        for d in range(1, p.depth):
            total = total + self.z_buf[d - 1, y].astype(F32)
        return total

    def across_y(self):
        p = self.place
        for d in range(1, p.depth):
            self.heard(self.z_buf.at[d - 1], 1 + d)
        away = 1 - p.y
        self.x_buf[p.z, away] = self.here(away).astype(BF16)
        self.push(self.x_buf.at[p.z, away], self.y_buf, p.depth + 1, p.dev(y=away))

    def result(self):
        self.heard(self.y_buf, self.place.depth + 1)
        return self.here(self.place.y) + self.y_buf[...].astype(F32)

    def finish(self):
        for copy in self.sent:
            copy.wait_send()


class Return:
    def __init__(self, place, src, dst, local, send, recv):
        self.place, self.src, self.dst = place, src, dst
        self.local, self.send, self.recv = local, send, recv
        self.rows = dst.shape[1]
        self.sent = []

    def block(self, owner):
        return self.src.at[pl.ds(pl.multiple_of(owner * self.rows, self.rows), self.rows)]

    def start_one(self, d):
        me = self.place.fsdp
        if d == 0:
            self.copy = pltpu.make_async_copy(self.block(me), self.dst.at[me], self.local)
            self.copy.start()
            return
        to = lax.rem(me + d, 4)
        copy = remote(
            self.block(to), self.dst.at[me], self.send.at[d - 1], self.recv.at[d - 1], (lax.axis_index(DP), to)
        )
        copy.start()
        self.sent.append(copy)

    def start(self):
        for d in (2, 3, 1, 0):
            self.start_one(d)

    def finish(self):
        self.copy.wait()
        for d in range(1, 4):
            block = self.dst.at[lax.rem(self.place.fsdp + 4 - d, 4)]
            remote(block, block, self.send.at[d - 1], self.recv.at[d - 1], self.place.dev()).wait_recv()
        for copy in self.sent:
            copy.wait_send()


def last_kernel(
    depth, langs,
    dlen_ref, elen_ref, tag_ref, sums_in, fsum_in, vec_ref,
    gfo_in, gfi_in, gco_in, output_in, cq_in, pair_in, gcm_in, cmixf_in, clse_in,
    res2_in, unit_in, inv_in, wcq_in, wckv_in, wout_in, enc_in, one_in,
    merged_in, mixf_in, lse_in, mixed_in, low_in, win_in,
    out_ret, gin_ret, genc_ret, r_small, r_in, r_out, r_cq, r_ckv, r_co, r_fi, r_fo,
    cq, pair, gcm, cmixf, clse, res2, unit, inv, wcq, wckv, wout, enc, one, merged, mixed, low, win,
    dcq, dpair, gmix, dmerged, low1, genc_low, gin_low, sums,
    own_fo, own_fi, own_co, full_ckv, full_cq, full_out, full_in, full_small, small_t,
    c_fo, x_fo, z_fo, y_fo, c_fi, x_fi, z_fi, y_fi, c_co, x_co, z_co, y_co, c_ckv, x_ckv, z_ckv, y_ckv,
    c_cq, x_cq, z_cq, y_cq, c_out, x_out, z_out, y_out, c_in, x_in, z_in, y_in, c_sm, x_sm, z_sm, y_sm,
    kx, vx, kt, dk_acc, dv_acc,
    send, recv, rlocal, rsend, rrecv, isem,
):
    p = Place(depth)
    p.greet()
    tokens, features = cq.shape
    p_pairs = features // 128
    loads = []

    def load(src, dst):
        copy = pltpu.make_async_copy(src, dst, isem.at[len(loads)])
        copy.start()
        loads.append(copy)
        return copy

    by_pair = []
    for i in range(p_pairs):
        cols = pl.ds(128 * i, 128)
        some = [load(a.at[:, cols], b.at[:, cols]) for a, b in ((cq_in, cq), (gcm_in, gcm), (cmixf_in, cmixf), (clse_in, clse), (pair_in, pair))]
        high = pl.ds(features + 128 * i, 128)
        some.append(load(pair_in.at[:, high], pair.at[:, high]))
        by_pair.append(some)
    early = [load(gfo_in.at[:, :, :, p.c], own_fo), load(gfi_in.at[:, :, :, p.c], own_fi), load(gco_in.at[:, :, :, p.c], own_co)]
    mid = [load(a, b) for a, b in ((wcq_in, wcq), (wckv_in, wckv), (wout_in, wout), (res2_in, res2), (unit_in, unit), (inv_in, inv), (enc_in, enc), (one_in, one))]
    late = [load(a, b) for a, b in ((merged_in, merged), (mixed_in, mixed), (low_in, low), (win_in, win))]
    mixf, lse, total_in = cmixf, clse, res2

    count = [0]

    def scatter(full, own, *bufs):
        n = count[0]
        count[0] += 1
        return Scatter(p, full, own, *bufs, send.at[n], recv.at[n])

    def inner(full):
        return full.at[:, :, :, p.c]

    fo_rows, fi_cols = own_fo.shape[3] // 2, own_fi.shape[4] // 2
    s_fo = [
        scatter(gfo_in.at[:, :, :, :, rows], own_fo.at[:, :, :, rows], c_fo.at[i], x_fo.at[i], z_fo.at[i], y_fo.at[i])
        for i, rows in ((i, pl.ds(i * fo_rows, fo_rows)) for i in range(2))
    ]
    s_fi = [
        scatter(gfi_in.at[:, :, :, :, :, cols], own_fi.at[:, :, :, :, cols], c_fi.at[i], x_fi.at[i], z_fi.at[i], y_fi.at[i])
        for i, cols in ((i, pl.ds(i * fi_cols, fi_cols)) for i in range(2))
    ]
    s_co = scatter(gco_in, own_co, c_co, x_co, z_co, y_co)
    s_ckv = scatter(full_ckv, inner(full_ckv), c_ckv, x_ckv, z_ckv, y_ckv)
    s_cq = scatter(full_cq, inner(full_cq), c_cq, x_cq, z_cq, y_cq)
    s_out = scatter(full_out, inner(full_out), c_out, x_out, z_out, y_out)
    s_in = [
        scatter(full_in.at[i], inner(full_in.at[i]), c_in.at[i], x_in.at[i], z_in.at[i], y_in.at[i])
        for i in range(p_pairs)
    ]
    s_small = scatter(full_small, inner(full_small), c_sm, x_sm, z_sm, y_sm)
    b_out = Return(p, output_in, out_ret, rlocal.at[0], rsend.at[0], rrecv.at[0])
    b_enc = Return(p, genc_low, genc_ret, rlocal.at[1], rsend.at[1], rrecv.at[1])
    b_in = Return(p, gin_low, gin_ret, rlocal.at[2], rsend.at[2], rrecv.at[2])

    sums[...] = sums_in[...]

    def backward(length, q, k, v, do, of, ls, dq, dk, dv):
        attend_bwd_core(512, length, q, k, v, do, of, ls, dq, dk, dv, kx, vx, kt, dk_acc, dv_acc, between)

    def cut(ref, at):
        return ref.at[:, pl.ds(at, 128)]

    slots = [
        [], [], [], [],
        [b_out.start], [s_fo[0].across_x], [s_fi[0].across_x], [],
        [s_fo[1].across_x], [s_fi[1].across_x, s_co.across_x], [], [s_fo[0].along_z],
        [], [], [], [s_fi[0].along_z],
        [s_fo[1].along_z], [], [s_fo[0].across_y], [s_fi[0].across_y, s_fi[1].along_z],
        [], [s_out.across_x, s_co.along_z], [], [],
        [s_ckv.along_z, s_in[0].across_x], [s_cq.along_z, s_fo[1].across_y], [], [s_fi[1].across_y, s_out.along_z],
        [s_in[1].across_x, s_co.across_y], [s_in[0].along_z], [s_ckv.across_y], [s_cq.across_y],
        [s_in[2].across_x], [s_in[1].along_z], [s_out.across_y, s_in[0].across_y], [],
    ]
    slot = [0]

    def move(steps):
        for step in steps:
            step()

    def between():
        move(slots[slot[0]])
        slot[0] += 1

    enc_len = elen_ref[p.fsdp]
    for i in range(p_pairs):
        for copy in by_pair[i]:
            copy.wait()
        if i == 0:
            for copy in early:
                copy.wait()
        at = 128 * i
        backward(
            enc_len, cut(cq, at), cut(pair, at), cut(pair, features + at), cut(gcm, at), cut(cmixf, at), cut(clse, at),
            cut(dcq, at), cut(dpair, at), cut(dpair, features + at),
        )
        if i == 0:
            p.meet()
            for job in (s_fo[0], s_fi[0], s_fo[1], s_fi[1], s_co):
                job.to_core()
    late += [load(a, b) for a, b in ((mixf_in, mixf), (lse_in, lse))]
    for copy in mid:
        copy.wait()

    def weight_sum(left, right, full, cols, lead=()):
        value = turned_dot(left, right)
        shape = (depth, 2, 2, 2, value.shape[0] // (8 * depth), value.shape[1])
        full[(*lead, slice(None), slice(None), slice(None), slice(None), slice(None), cols)] = value.astype(BF16).reshape(shape)

    for part in range(2):
        cols = pl.ds(part * features, features)
        weight_sum(enc[...], dpair[:, cols], full_ckv, cols)
    s_ckv.to_core()
    weight_sum(one[...], dcq[...], full_cq, pl.ds(0, features))
    s_cq.to_core()

    for i in range(tokens // 256):
        rows = pl.ds(i * 256, 256)
        genc = nt_dot(dpair[rows, :], wckv[...])
        genc_low[rows, :] = genc.astype(BF16)
        dq = dcq[rows, :]
        above = res2[rows, :] + nt_dot(dq, wcq[...])
        units = unit[rows, :]
        res1 = norm_back(above, units, inv[rows, :1], vec(vec_ref, 7))
        total_in[rows, :] = res1
        low_one = res1.astype(BF16)
        low1[rows, :] = low_one
        gmix[rows, :] = nt_dot(low_one, wout[...]).astype(BF16)
        for index, value in (
            (2, low_one.astype(F32)), (3, dq.astype(F32)), (4, dpair[rows, features:].astype(F32)), (7, above * units), (10, above),
        ):
            sums[index : index + 1, :] += col_sum(value)
        between()
    b_enc.start()
    move([s_ckv.across_x, s_cq.across_x])
    for copy in late:
        copy.wait()
    weight_sum(mixed[...], low1[...], full_out, pl.ds(0, features))
    s_out.to_core()
    dec_len = dlen_ref[p.fsdp]
    for i in range(p_pairs):
        at = 128 * i
        wide = 384 * i
        backward(
            dec_len, cut(merged, wide), cut(merged, wide + 128), cut(merged, wide + 256), cut(gmix, at), cut(mixf, at), cut(lse, at),
            cut(dmerged, wide), cut(dmerged, wide + 128), cut(dmerged, wide + 256),
        )
        weight_sum(low[...], dmerged[:, wide : wide + 384], full_in, slice(None), (i,))
        s_in[i].to_core()
        w_pair = win[i]

        def add_input(j, carry, wide=wide, w_pair=w_pair, last=i == p_pairs - 1):
            rows = pl.ds(pl.multiple_of(j * 256, 256), 256)
            total = total_in[rows, :] + nt_dot(dmerged[rows, wide : wide + 384], w_pair)
            total_in[rows, :] = total
            if last:
                gin_low[rows, :] = total.astype(BF16)
                sums[LANG_ROW : LANG_ROW + 1, :] += col_sum(total)
            return carry

        lax.fori_loop(0, tokens // 256, add_input, 0)
        for part, index in ((0, 0), (2, 1)):
            block = dmerged[:, wide + 128 * part : wide + 128 * part + 128].astype(F32)
            sums[index : index + 1, at : at + 128] = col_sum(block)
    b_in.start()
    move([s_in[3].across_x, s_in[2].along_z, s_in[1].across_y])
    small_t[...] = jnp.zeros_like(small_t)
    small_t[:16, :] = sums[...]
    place_tag = lax.broadcasted_iota(jnp.int32, (langs + 3, 1), 0) == tag_ref[p.fsdp]
    small_t[LANG_ROW : LANG_ROW + langs + 3, :] = jnp.where(place_tag, sums[LANG_ROW : LANG_ROW + 1, :], 0.0)
    columns = small_t[...].T.astype(BF16)
    full_small[:, :, :, :, :16, :] = columns.reshape(depth, 2, 2, 2, 16, 128)
    top = lax.broadcasted_iota(jnp.int32, (16, 128), 0) == 0
    for r in range(depth * 8):
        lanes = slice(128 * (r // 2), 128 * (r // 2) + 128)
        tile = jnp.where(top, fsum_in[:, lanes], 0.0)
        full_small[r // 8, (r // 4) % 2, (r // 2) % 2, r % 2, 16:32, :] = tile.astype(BF16)
    s_small.to_core()
    for i in range(2):
        r_fo[i * fo_rows : (i + 1) * fo_rows, :] = s_fo[i].result()
        r_fi[:, i * fi_cols : (i + 1) * fi_cols] = s_fi[i].result()
    r_co[...] = s_co.result()
    r_ckv[...] = s_ckv.result()
    move([s_small.across_x, s_in[3].along_z])
    r_cq[...] = s_cq.result()
    r_out[...] = s_out.result()
    move([s_in[2].across_y, s_small.along_z, s_in[3].across_y, s_small.across_y])
    for i in range(p_pairs):
        value = s_in[i].result()
        for part in range(3):
            at = part * features + 128 * i
            r_in[:, at : at + 128] = value[:, 128 * part : 128 * part + 128]
    r_small[...] = s_small.result()
    for job in (*s_fo, *s_fi, s_co, s_ckv, s_cq, s_out, *s_in, s_small, b_out, b_enc, b_in):
        job.finish()


def last_call(depth, langs, hidden, part_rows, dlen, elen, tags, sums, fsum, vecs, *arrays):
    tokens, features = arrays[4].shape
    pairs = features // 128
    groups = tokens // part_rows

    def sds(shape, dtype):
        return jax.ShapeDtypeStruct(shape, dtype)

    rows = features // (8 * depth)
    frows = hidden // (8 * depth)
    outs = [sds((groups, part_rows, features), BF16)] * 3
    outs += [
        sds((32, 128), F32), sds((rows, 3 * features), F32), sds((rows, features), F32), sds((rows, features), F32),
        sds((rows, 2 * features), F32), sds((rows, features), F32), sds((rows, hidden), F32), sds((frows, features), F32),
    ]

    def bufs(r, c, lead=()):
        return [
            pltpu.VMEM((*lead, depth, 2, 2, r, c), BF16), pltpu.VMEM((*lead, depth, 2, r, c), BF16),
            pltpu.VMEM((*lead, depth - 1, 2, r, c), BF16), pltpu.VMEM((*lead, r, c), BF16),
        ]

    def like(a):
        return pltpu.VMEM(a.shape, a.dtype)

    scratch = [like(a) for i, a in enumerate(arrays[4:]) if i not in (14, 15)]
    scratch += [
        pltpu.VMEM((tokens, features), BF16), pltpu.VMEM((tokens, 2 * features), BF16), pltpu.VMEM((tokens, features), BF16),
        pltpu.VMEM((tokens, 3 * features), BF16), pltpu.VMEM((tokens, features), BF16),
        pltpu.VMEM((tokens, features), BF16), pltpu.VMEM((tokens, features), BF16), pltpu.VMEM((16, features), F32),
        pltpu.VMEM((depth, 2, 2, frows, features), BF16), pltpu.VMEM((depth, 2, 2, rows, hidden), BF16), pltpu.VMEM((depth, 2, 2, rows, features), BF16),
        pltpu.VMEM((depth, 2, 2, 2, rows, 2 * features), BF16), pltpu.VMEM((depth, 2, 2, 2, rows, features), BF16), pltpu.VMEM((depth, 2, 2, 2, rows, features), BF16),
        pltpu.VMEM((pairs, depth, 2, 2, 2, rows, 384), BF16), pltpu.VMEM((depth, 2, 2, 2, 32, 128), BF16), pltpu.VMEM((128, features), F32),
    ]
    scratch += bufs(frows // 2, features, (2,)) + bufs(rows, hidden // 2, (2,)) + bufs(rows, features) + bufs(rows, 2 * features)
    scratch += bufs(rows, features) + bufs(rows, features) + bufs(rows, 384, (pairs,)) + bufs(32, 128)
    scratch += [
        pltpu.VMEM((tokens, 256), BF16), pltpu.VMEM((tokens, 256), BF16), pltpu.VMEM((2, 128, tokens), BF16),
        pltpu.VMEM((tokens, 128), F32), pltpu.VMEM((tokens, 128), F32),
        pltpu.SemaphoreType.DMA((pairs + 9, depth + 2)), pltpu.SemaphoreType.DMA((pairs + 9, depth + 2)),
        pltpu.SemaphoreType.DMA((3,)), pltpu.SemaphoreType.DMA((3, 3)), pltpu.SemaphoreType.DMA((3, 3)),
        pltpu.SemaphoreType.DMA((6 * pairs + 17,)),
    ]
    return pl.pallas_call(
        functools.partial(last_kernel, depth, langs),
        in_specs=[SMEM_SPEC] * 3 + [VMEM_SPEC] * 3 + [ANY_SPEC] * len(arrays),
        out_specs=[ANY_SPEC] * 3 + [VMEM_SPEC] * 8,
        out_shape=outs,
        scratch_shapes=scratch,
        compiler_params=pltpu.CompilerParams(
            vmem_limit_bytes=60 * 1024 * 1024, collective_id=2, has_side_effects=True
        ),
        name="last",
    )(dlen, elen, tags, sums, fsum, vecs, *arrays)


def finish_kernel(
    out_in, gin_in, genc_in, small_in, in_in, wout_in, cq_in, ckv_in, co_in, fi_in, fo_in,
    out, gin, genc, bias, gain, shift, table, fbias, r_in, r_out, r_cq, r_ckv, r_co, r_fi, r_fo, square,
):
    out[...] = out_in[...]
    gin[...] = gin_in[...].astype(F32)
    genc[...] = genc_in[...].astype(F32)

    @pl.when(pl.program_id(0) == 0)
    def _():
        for src, dst in (
            (in_in, r_in), (wout_in, r_out), (cq_in, r_cq), (ckv_in, r_ckv), (co_in, r_co), (fi_in, r_fi), (fo_in, r_fo),
        ):
            dst[...] = src[...]
        square[...] = jnp.zeros_like(square)
        square[:32, :] = small_in[...]
        turned = square[...].T
        bias[...] = turned[0:7, :16]
        gain[...] = turned[7:10, :16]
        shift[...] = turned[10:13, :16]
        table[...] = pltpu.roll(small_in[:16, :], 128 - LANG_ROW, 1)[:, : table.shape[1]]
        core = lax.rem(lax.axis_index(FSDP), 2)
        row = small_in[16:24, :]
        fbias[...] = jnp.where(core == 0, row, pltpu.roll(row, 64, 1))[0:1, :64]


def finish_call(langs, output, gin, genc, small, *sums):
    groups, part_rows, features = output.shape

    def block(a):
        return pl.BlockSpec((1, part_rows, features), lambda i: (i, 0, 0))

    def whole(a):
        return pl.BlockSpec(a.shape, lambda i: (0, 0))

    def sds(*shape):
        return jax.ShapeDtypeStruct(shape, F32)

    smalls = [sds(7, 16), sds(3, 16), sds(3, 16), sds(16, langs), sds(1, 64)]
    outs = [jax.ShapeDtypeStruct(output.shape, BF16), sds(*gin.shape), sds(*genc.shape), *smalls]
    outs += [sds(*a.shape) for a in sums]
    return pl.pallas_call(
        finish_kernel,
        grid=(groups,),
        in_specs=[block(a) for a in (output, gin, genc)] + [whole(a) for a in (small, *sums)],
        out_specs=[block(a) for a in (output, gin, genc)] + [whole(a) for a in (*smalls, *sums)],
        out_shape=outs,
        scratch_shapes=[pltpu.VMEM((128, 128), F32)],
        compiler_params=BIG,
        name="finish",
    )(output, gin, genc, small, *sums)


def fast_body(
    dec_input, enc_output, dec_lengths, enc_lengths, lang_tags, lang_table, self_in, self_out, cross_q, cross_kv,
    cross_out, ffn_in, ffn_out, biases, ffn_bias, norm_gains, norm_shifts, cotangent,
):
    groups, part_rows, features = dec_input.shape
    tokens = groups * part_rows
    hidden = ffn_in.shape[1]
    langs = lang_table.shape[1]
    depth = lax.axis_size(DP) // 2
    (
        w_in, w_out, w_cq, w_ckv, enc, vecs, low, merged, pair, mixed, mixed_f32, self_lse, unit1, inv1, one, cquery,
        cmixed_f32, cross_lse, output, res2, gcm, sums, fsum, g_fout, g_fin, g_co,
    ) = first_call(
        depth, dec_lengths, enc_lengths, lang_tags, biases.T, norm_gains.T, norm_shifts.T, lang_table, ffn_bias[None],
        dec_input, enc_output, cotangent, self_in, self_out, cross_q, cross_kv, cross_out, ffn_in, ffn_out,
    )
    w_in = w_in.reshape(w_in.shape[0], -1, w_in.shape[-1])
    w_out, w_cq, w_ckv = [w.reshape(-1, w.shape[-1]) for w in (w_out, w_cq, w_ckv)]
    moved = last_call(
        depth, langs, hidden, part_rows, dec_lengths, enc_lengths, lang_tags, sums, fsum, vecs,
        g_fout, g_fin, g_co, output, cquery, pair, gcm, cmixed_f32, cross_lse, res2, unit1, inv1, w_cq, w_ckv, w_out, enc, one,
        merged, mixed_f32, self_lse, mixed, low, w_in,
    )
    output, gin, genc, bias, gain, shift, table, g_fbias, *sums = finish_call(langs, *moved)
    return (output, gin, genc, table, *sums, bias.T, g_fbias.reshape(-1), gain.T, shift.T)


def solution(mesh):
    def either(*args):
        whole_sequences = mesh.shape[FSDP] == args[0].shape[0] == 4 and mesh.shape[DP] % 2 == 0
        whole_sequences = whole_sequences and args[6].shape[0] == 16
        return (fast_body if whole_sequences else body)(*args)

    return jax.shard_map(
        either,
        mesh=mesh,
        in_specs=(
            P(DP, FSDP, None),
            P(DP, FSDP, None),
            P(DP),
            P(DP),
            P(DP),
            P(AXES, None),
            P(AXES, None),
            P(AXES, None),
            P(AXES, None),
            P(AXES, None),
            P(AXES, None),
            P(AXES, None),
            P(AXES, None),
            P(AXES, None),
            P(AXES),
            P(AXES, None),
            P(AXES, None),
            P(DP, FSDP, None),
        ),
        out_specs=(
            P(DP, FSDP, None),
            P(DP, FSDP, None),
            P(DP, FSDP, None),
            P(AXES, None),
            P(AXES, None),
            P(AXES, None),
            P(AXES, None),
            P(AXES, None),
            P(AXES, None),
            P(AXES, None),
            P(AXES, None),
            P(AXES, None),
            P(AXES),
            P(AXES, None),
            P(AXES, None),
        ),
        check_vma=False,
    )
```

```python
import functools
import math

import jax
import jax.numpy as jnp
from jax import lax
from jax.experimental import pallas as pl
from jax.experimental.pallas import tpu as pltpu
from jax.sharding import PartitionSpec as P

HEADS = 8
DP, FSDP = AXES = ("dp", "fsdp")


def smooth_gelu(values):
    return (
        0.5
        * values
        * (1.0 + jnp.tanh(0.7978845608028654 * (values + 0.044715 * values * values * values)))
    )


def times_t(left, right):
    return lax.dot_general(
        left, right, (((1,), (1,)), ((), ())), preferred_element_type=jnp.float32
    )


def outer_sum(left, right):
    return lax.dot_general(
        left, right, (((0,), (0,)), ((), ())), preferred_element_type=jnp.float32
    )


def normalize_rows(residual, gain_col, shift_col):
    row_mean = jnp.mean(residual, axis=-1, keepdims=True)
    centered = residual - row_mean
    inv_dev = lax.rsqrt(jnp.mean(centered * centered, axis=-1, keepdims=True) + 1e-05)
    unit_rows = centered * inv_dev
    return (unit_rows * gain_col + shift_col, unit_rows, inv_dev)


def normalize_back(grad_above, unit_rows, inv_dev, gain_col):
    grad_unit = grad_above * gain_col
    grad_res = inv_dev * (
        grad_unit
        - jnp.mean(grad_unit, axis=-1, keepdims=True)
        - unit_rows * jnp.mean(grad_unit * unit_rows, axis=-1, keepdims=True)
    )
    return (grad_res, jnp.sum(grad_above * unit_rows, axis=0), jnp.sum(grad_above, axis=0))


def masked_scores(query_bf, key_full, lengths_here):
    groups, rows_here, features = query_bf.shape
    key_count = key_full.shape[1]
    head_size = features // HEADS
    query_heads = query_bf.reshape(groups, rows_here, HEADS, head_size)
    key_heads = key_full.reshape(groups, key_count, HEADS, head_size)
    scores = jnp.einsum(
        "sqhd,skhd->shqk", query_heads, key_heads, preferred_element_type=jnp.float32
    ) * (1.0 / math.sqrt(head_size))
    key_valid = jnp.arange(key_count)[None, :] < lengths_here[:, None]
    return jnp.where(key_valid[:, None, None, :], scores, -1000000000.0)


def attend_forward(query_bf, key_full, value_full, lengths_here):
    groups, rows_here, features = query_bf.shape
    key_count = key_full.shape[1]
    value_heads = value_full.reshape(groups, key_count, HEADS, features // HEADS)
    scores = masked_scores(query_bf, key_full, lengths_here)
    row_max = jnp.max(scores, axis=-1, keepdims=True)
    exp_scores = jnp.exp(scores - row_max)
    row_total = jnp.sum(exp_scores, axis=-1, keepdims=True)
    probs_bf = (exp_scores / row_total).astype(jnp.bfloat16)
    attn_mixed = jnp.einsum(
        "shqk,skhd->sqhd", probs_bf, value_heads, preferred_element_type=jnp.float32
    )
    return (attn_mixed.reshape(groups, rows_here, features), row_max + jnp.log(row_total))


def attend_back(grad_mixed_bf, query_bf, key_full, value_full, lengths_here, log_total):
    groups, rows_here, features = query_bf.shape
    key_count = key_full.shape[1]
    head_size = features // HEADS
    query_heads = query_bf.reshape(groups, rows_here, HEADS, head_size)
    key_heads = key_full.reshape(groups, key_count, HEADS, head_size)
    value_heads = value_full.reshape(groups, key_count, HEADS, head_size)
    grad_heads = grad_mixed_bf.reshape(groups, rows_here, HEADS, head_size)
    attn_probs = jnp.exp(masked_scores(query_bf, key_full, lengths_here) - log_total)
    probs_bf = attn_probs.astype(jnp.bfloat16)
    grad_probs = jnp.einsum(
        "sqhd,skhd->shqk", grad_heads, value_heads, preferred_element_type=jnp.float32
    )
    grad_values = jnp.einsum(
        "shqk,sqhd->skhd", probs_bf, grad_heads, preferred_element_type=jnp.float32
    )
    grad_scores = attn_probs * (
        grad_probs - jnp.sum(attn_probs * grad_probs, axis=-1, keepdims=True)
    )
    grad_scores_bf = grad_scores.astype(jnp.bfloat16)
    score_scale = 1.0 / math.sqrt(head_size)
    grad_query = (
        jnp.einsum("shqk,skhd->sqhd", grad_scores_bf, key_heads, preferred_element_type=jnp.float32)
        * score_scale
    )
    grad_keys = (
        jnp.einsum(
            "shqk,sqhd->skhd", grad_scores_bf, query_heads, preferred_element_type=jnp.float32
        )
        * score_scale
    )
    return (
        grad_query.reshape(groups, rows_here, features),
        grad_keys.reshape(groups, key_count, features),
        grad_values.reshape(groups, key_count, features),
    )


def body(
    dec_input,
    enc_output,
    dec_lengths,
    enc_lengths,
    lang_tags,
    lang_table,
    self_in,
    self_out,
    cross_q,
    cross_kv,
    cross_out,
    ffn_in,
    ffn_out,
    biases,
    ffn_bias,
    norm_gains,
    norm_shifts,
    cotangent,
):
    full_weights = (
        lax.all_gather(lang_table, AXES, axis=0, tiled=True),
        lax.all_gather(self_in, AXES, axis=0, tiled=True),
        lax.all_gather(self_out, AXES, axis=0, tiled=True),
        lax.all_gather(cross_q, AXES, axis=0, tiled=True),
        lax.all_gather(cross_kv, AXES, axis=0, tiled=True),
        lax.all_gather(cross_out, AXES, axis=0, tiled=True),
        lax.all_gather(ffn_in, AXES, axis=0, tiled=True),
        lax.all_gather(ffn_out, AXES, axis=0, tiled=True),
        lax.all_gather(biases, AXES, axis=0, tiled=True),
        lax.all_gather(ffn_bias, AXES, axis=0, tiled=True),
        lax.all_gather(norm_gains, AXES, axis=0, tiled=True),
        lax.all_gather(norm_shifts, AXES, axis=0, tiled=True),
    )
    (
        full_table,
        full_in,
        full_out,
        full_cq,
        full_ckv,
        full_co,
        full_ffn_in,
        full_ffn_out,
        full_biases,
        full_ffn_bias,
        full_gains,
        full_shifts,
    ) = full_weights
    bias_cols = full_biases.astype(jnp.float32)
    gain_cols = full_gains.astype(jnp.float32)
    shift_cols = full_shifts.astype(jnp.float32)
    groups, rows_here, features = dec_input.shape
    enc_rows = enc_output.shape[1]
    tokens = groups * rows_here
    positions = lax.axis_index(FSDP) * rows_here + jnp.arange(rows_here)
    live_rows = (positions[None, :] < dec_lengths[:, None]).astype(jnp.float32)
    live_flat = live_rows.reshape(tokens, 1)
    onehot = (lang_tags[:, None] == jnp.arange(full_table.shape[1])[None, :]).astype(jnp.float32)
    lang_rows = lax.dot_general(
        onehot,
        full_table.astype(jnp.float32),
        (((1,), (1,)), ((), ())),
        precision=lax.Precision.HIGHEST,
        preferred_element_type=jnp.float32,
    )
    flat_start = (dec_input.astype(jnp.float32) + lang_rows[:, None, :]).reshape(tokens, features)
    start_bf = flat_start.astype(jnp.bfloat16)
    zeros_row = jnp.zeros((features,), jnp.float32)
    merged = (
        jnp.dot(start_bf, full_in, preferred_element_type=jnp.float32)
        + jnp.concatenate([bias_cols[:, 0], zeros_row, bias_cols[:, 1]])[None, :]
    )
    merged_bf = merged.astype(jnp.bfloat16).reshape(groups, rows_here, 3 * features)
    query_bf = merged_bf[:, :, :features]
    key_own = merged_bf[:, :, features : 2 * features]
    value_own = merged_bf[:, :, 2 * features :]
    key_full, value_full = (
        lax.all_gather(key_own, FSDP, axis=1, tiled=True),
        lax.all_gather(value_own, FSDP, axis=1, tiled=True),
    )
    attn_mixed, self_lse = attend_forward(query_bf, key_full, value_full, dec_lengths)
    mixed_bf = attn_mixed.astype(jnp.bfloat16).reshape(tokens, features)
    branch = jnp.dot(mixed_bf, full_out, preferred_element_type=jnp.float32) + bias_cols[:, 2]
    normed_one, unit_one, inv_one = normalize_rows(
        flat_start + branch, gain_cols[:, 0], shift_cols[:, 0]
    )
    one_bf = normed_one.astype(jnp.bfloat16)
    cross_query = (
        (jnp.dot(one_bf, full_cq, preferred_element_type=jnp.float32) + bias_cols[:, 3])
        .astype(jnp.bfloat16)
        .reshape(groups, rows_here, features)
    )
    enc_flat = enc_output.reshape(groups * enc_rows, features)
    cross_pair = (
        jnp.dot(enc_flat, full_ckv, preferred_element_type=jnp.float32)
        + jnp.concatenate([zeros_row, bias_cols[:, 4]])[None, :]
    )
    pair_bf = cross_pair.astype(jnp.bfloat16).reshape(groups, enc_rows, 2 * features)
    ckey_own = pair_bf[:, :, :features]
    cvalue_own = pair_bf[:, :, features:]
    ckey_full, cvalue_full = (
        lax.all_gather(ckey_own, FSDP, axis=1, tiled=True),
        lax.all_gather(cvalue_own, FSDP, axis=1, tiled=True),
    )
    cross_mixed, cross_lse = attend_forward(cross_query, ckey_full, cvalue_full, enc_lengths)
    cmixed_bf = cross_mixed.astype(jnp.bfloat16).reshape(tokens, features)
    cross_branch = jnp.dot(cmixed_bf, full_co, preferred_element_type=jnp.float32) + bias_cols[:, 5]
    normed_two, unit_two, inv_two = normalize_rows(
        normed_one + cross_branch, gain_cols[:, 1], shift_cols[:, 1]
    )
    two_bf = normed_two.astype(jnp.bfloat16)
    hidden = jnp.dot(
        two_bf, full_ffn_in, preferred_element_type=jnp.float32
    ) + full_ffn_bias.astype(jnp.float32)
    activated, gelu_pull = jax.vjp(smooth_gelu, hidden)
    act_bf = activated.astype(jnp.bfloat16)
    ffn_branch = jnp.dot(act_bf, full_ffn_out, preferred_element_type=jnp.float32) + bias_cols[:, 6]
    normed_three, unit_three, inv_three = normalize_rows(
        normed_two + ffn_branch, gain_cols[:, 2], shift_cols[:, 2]
    )
    output = (normed_three * live_flat).astype(jnp.bfloat16).reshape(groups, rows_here, features)
    back_weights = (
        lax.all_gather(lang_table, AXES, axis=0, tiled=True),
        lax.all_gather(self_in, AXES, axis=0, tiled=True),
        lax.all_gather(self_out, AXES, axis=0, tiled=True),
        lax.all_gather(cross_q, AXES, axis=0, tiled=True),
        lax.all_gather(cross_kv, AXES, axis=0, tiled=True),
        lax.all_gather(cross_out, AXES, axis=0, tiled=True),
        lax.all_gather(ffn_in, AXES, axis=0, tiled=True),
        lax.all_gather(ffn_out, AXES, axis=0, tiled=True),
        lax.all_gather(biases, AXES, axis=0, tiled=True),
        lax.all_gather(ffn_bias, AXES, axis=0, tiled=True),
        lax.all_gather(norm_gains, AXES, axis=0, tiled=True),
        lax.all_gather(norm_shifts, AXES, axis=0, tiled=True),
    )
    back_in = back_weights[1]
    back_out = back_weights[2]
    back_cq = back_weights[3]
    back_ckv = back_weights[4]
    back_co = back_weights[5]
    back_ffn_in = back_weights[6]
    back_ffn_out = back_weights[7]
    back_gains = back_weights[10].astype(jnp.float32)
    grad_above = cotangent.reshape(tokens, features) * live_flat
    grad_res3, gain_three, shift_three = normalize_back(
        grad_above, unit_three, inv_three, back_gains[:, 2]
    )
    grad_low3 = grad_res3.astype(jnp.bfloat16)
    grad_ffn_out = outer_sum(act_bf, grad_low3)
    bias_six = jnp.sum(grad_low3.astype(jnp.float32), axis=0)
    grad_act = times_t(grad_low3, back_ffn_out)
    grad_hidden_bf = gelu_pull(grad_act)[0].astype(jnp.bfloat16)
    grad_ffn_in = outer_sum(two_bf, grad_hidden_bf)
    grad_ffn_bias = jnp.sum(grad_hidden_bf.astype(jnp.float32), axis=0)
    grad_two = grad_res3 + times_t(grad_hidden_bf, back_ffn_in)
    grad_res2, gain_two, shift_two = normalize_back(grad_two, unit_two, inv_two, back_gains[:, 1])
    grad_low2 = grad_res2.astype(jnp.bfloat16)
    grad_cross_out = outer_sum(cmixed_bf, grad_low2)
    bias_five = jnp.sum(grad_low2.astype(jnp.float32), axis=0)
    grad_cmixed = (
        times_t(grad_low2, back_co).astype(jnp.bfloat16).reshape(groups, rows_here, features)
    )
    grad_cquery, grad_ckey, grad_cvalue = attend_back(
        grad_cmixed, cross_query, ckey_full, cvalue_full, enc_lengths, cross_lse
    )
    ckey_sum, cvalue_sum = (
        lax.psum_scatter(
            grad_ckey.astype(jnp.bfloat16), FSDP, scatter_dimension=1, tiled=True
        ).astype(jnp.float32),
        lax.psum_scatter(
            grad_cvalue.astype(jnp.bfloat16), FSDP, scatter_dimension=1, tiled=True
        ).astype(jnp.float32),
    )
    grad_pair_bf = (
        jnp.concatenate([ckey_sum, cvalue_sum], axis=-1)
        .astype(jnp.bfloat16)
        .reshape(groups * enc_rows, 2 * features)
    )
    grad_cross_kv = outer_sum(enc_flat, grad_pair_bf)
    bias_four = jnp.sum(grad_pair_bf[:, features:].astype(jnp.float32), axis=0)
    grad_encoder = times_t(grad_pair_bf, back_ckv).reshape(groups, enc_rows, features)
    grad_cquery_bf = grad_cquery.astype(jnp.bfloat16).reshape(tokens, features)
    grad_cross_q = outer_sum(one_bf, grad_cquery_bf)
    bias_three = jnp.sum(grad_cquery_bf.astype(jnp.float32), axis=0)
    grad_one = grad_res2 + times_t(grad_cquery_bf, back_cq)
    grad_res1, gain_one, shift_one = normalize_back(grad_one, unit_one, inv_one, back_gains[:, 0])
    grad_low1 = grad_res1.astype(jnp.bfloat16)
    grad_self_out = outer_sum(mixed_bf, grad_low1)
    bias_two = jnp.sum(grad_low1.astype(jnp.float32), axis=0)
    grad_mixed = (
        times_t(grad_low1, back_out).astype(jnp.bfloat16).reshape(groups, rows_here, features)
    )
    grad_query, grad_key, grad_value = attend_back(
        grad_mixed, query_bf, key_full, value_full, dec_lengths, self_lse
    )
    key_sum, value_sum = (
        lax.psum_scatter(
            grad_key.astype(jnp.bfloat16), FSDP, scatter_dimension=1, tiled=True
        ).astype(jnp.float32),
        lax.psum_scatter(
            grad_value.astype(jnp.bfloat16), FSDP, scatter_dimension=1, tiled=True
        ).astype(jnp.float32),
    )
    grad_merged_bf = (
        jnp.concatenate([grad_query, key_sum, value_sum], axis=-1)
        .astype(jnp.bfloat16)
        .reshape(tokens, 3 * features)
    )
    grad_self_in = outer_sum(start_bf, grad_merged_bf)
    merged_sums = jnp.sum(grad_merged_bf.astype(jnp.float32), axis=0)
    grad_start = grad_res1 + times_t(grad_merged_bf, back_in)
    grad_input = grad_start.reshape(groups, rows_here, features)
    seq_sums = jnp.sum(grad_input, axis=1)
    grad_table = lax.dot_general(
        seq_sums,
        onehot,
        (((0,), (0,)), ((), ())),
        precision=lax.Precision.HIGHEST,
        preferred_element_type=jnp.float32,
    )
    grad_biases = jnp.stack(
        [
            merged_sums[:features],
            merged_sums[2 * features :],
            bias_two,
            bias_three,
            bias_four,
            bias_five,
            bias_six,
        ],
        axis=1,
    )
    grad_gains = jnp.stack([gain_one, gain_two, gain_three], axis=1)
    grad_shifts = jnp.stack([shift_one, shift_two, shift_three], axis=1)
    reduced = (
        lax.psum_scatter(grad_table, AXES, scatter_dimension=0, tiled=True),
        lax.psum_scatter(grad_self_in, AXES, scatter_dimension=0, tiled=True),
        lax.psum_scatter(grad_self_out, AXES, scatter_dimension=0, tiled=True),
        lax.psum_scatter(grad_cross_q, AXES, scatter_dimension=0, tiled=True),
        lax.psum_scatter(grad_cross_kv, AXES, scatter_dimension=0, tiled=True),
        lax.psum_scatter(grad_cross_out, AXES, scatter_dimension=0, tiled=True),
        lax.psum_scatter(grad_ffn_in, AXES, scatter_dimension=0, tiled=True),
        lax.psum_scatter(grad_ffn_out, AXES, scatter_dimension=0, tiled=True),
        lax.psum_scatter(grad_biases, AXES, scatter_dimension=0, tiled=True),
        lax.psum_scatter(grad_ffn_bias, AXES, scatter_dimension=0, tiled=True),
        lax.psum_scatter(grad_gains, AXES, scatter_dimension=0, tiled=True),
        lax.psum_scatter(grad_shifts, AXES, scatter_dimension=0, tiled=True),
    )
    return (
        output,
        grad_input,
        grad_encoder,
        reduced[0],
        reduced[1],
        reduced[2],
        reduced[3],
        reduced[4],
        reduced[5],
        reduced[6],
        reduced[7],
        reduced[8],
        reduced[9],
        reduced[10],
        reduced[11],
    )


F32 = jnp.float32
BF16 = jnp.bfloat16


def nt_dot(left, right):
    return lax.dot_general(left, right, (((1,), (1,)), ((), ())), preferred_element_type=F32)


def nn_dot(left, right):
    return jnp.dot(left, right, preferred_element_type=F32)


def split_three(value):
    high = value.astype(BF16)
    rest = value - high.astype(F32)
    middle = rest.astype(BF16)
    return high, middle, (rest - middle.astype(F32)).astype(BF16)


def key_extra(tokens, length):
    lane = lax.broadcasted_iota(jnp.int32, (tokens, 128), 1) % 64
    row = lax.broadcasted_iota(jnp.int32, (tokens, 128), 0)
    masked = jnp.where(row < length, 0.0, -1e30)
    return jnp.where(lane == 3, masked, jnp.where(lane < 3, 1.0, 0.0)).astype(BF16)


def row_extra(lane, head, terms, mask_lane):
    base = head * 64
    out = jnp.where(lane == base + 3, mask_lane, 0.0).astype(F32)
    for place, term in enumerate(terms):
        out = jnp.where(lane == base + place, term.astype(F32), out)
    return out.astype(BF16)


def attend_fwd_core(block, length, q_ref, k_ref, v_ref, o_ref, of_ref, lse_ref, kx_ref, va_ref, vb_ref, between):
    tokens = q_ref.shape[0]
    kx_ref[:, :128] = k_ref[...]
    kx_ref[:, 128:] = key_extra(tokens, length)
    lane_full = lax.broadcasted_iota(jnp.int32, (tokens, 128), 1)
    values = v_ref[...].astype(F32)
    va_ref[...] = jnp.where(lane_full < 64, values, 1.0).astype(BF16)
    vb_ref[...] = jnp.where(lane_full < 64, 1.0, values).astype(BF16)

    for index in range(tokens // block):
        rows = pl.ds(index * block, block)
        lane = lax.broadcasted_iota(jnp.int32, (block, 128), 1)
        query = q_ref[rows, :].astype(F32) * 0.125
        halves, tops, both = [], [], []
        for head in range(2):
            inside = (lane < 64) if head == 0 else (lane >= 64)
            own = jnp.where(inside, query, 0.0).astype(BF16)
            extra = row_extra(lane, head, (), 1.0)
            both.append(nt_dot(jnp.concatenate([own, extra], axis=1), kx_ref[...]))
        for scores, vx_ref in zip(both, (va_ref, vb_ref)):
            top = jnp.max(scores, axis=1, keepdims=True)
            probs = jnp.exp(scores - top).astype(BF16)
            halves.append(nn_dot(probs, vx_ref[...]))
            tops.append(top)
        number = jnp.where(lane < 64, halves[0], halves[1])
        total = pltpu.roll(jnp.where(lane < 64, halves[1], halves[0]), 64, 1)
        out = number / total
        o_ref[rows, :] = out.astype(BF16)
        of_ref[rows, :] = out
        lse_ref[rows, :] = jnp.where(lane < 64, tops[0], tops[1]) + jnp.log(total)
        if index + 1 < tokens // block:
            between()


def attend_bwd_core(
    chunk, length, q_ref, k_ref, v_ref, do_ref, of_ref, lse_ref, dq_ref, dk_ref, dv_ref, kx_ref, vx_ref, kt_ref, dk_acc, dv_acc, between,
):
    tokens = q_ref.shape[0]
    extra_keys = key_extra(tokens, length)
    kx_ref[:, :128] = k_ref[...]
    kx_ref[:, 128:] = extra_keys
    vx_ref[:, :128] = v_ref[...]
    vx_ref[:, 128:] = extra_keys
    turned = k_ref[...].astype(F32).T
    sub = lax.broadcasted_iota(jnp.int32, (128, tokens), 0)
    kt_ref[0] = jnp.where(sub < 64, turned, 0.0).astype(BF16)
    kt_ref[1] = jnp.where(sub < 64, 0.0, turned).astype(BF16)
    dk_acc[...] = jnp.zeros_like(dk_acc)
    dv_acc[...] = jnp.zeros_like(dv_acc)
    same = (
        lax.broadcasted_iota(jnp.int32, (128, 128), 0) // 64
        == lax.broadcasted_iota(jnp.int32, (128, 128), 1) // 64
    ).astype(F32).astype(BF16)
    lane = lax.broadcasted_iota(jnp.int32, (tokens, 128), 1)
    query = q_ref[...].astype(F32) * 0.125
    grad = do_ref[...].astype(F32)
    inner = grad * of_ref[...]
    inner_high = inner.astype(BF16)
    inner_low = (inner - inner_high.astype(F32)).astype(BF16)
    delta = nn_dot(inner_high, same) + nn_dot(inner_low, same)
    lse_terms = split_three(-lse_ref[...])
    delta_terms = split_three(-delta)
    own_q, own_g, left_q, left_g = [], [], [], []
    for head in range(2):
        inside = (lane < 64) if head == 0 else (lane >= 64)
        own_q.append(jnp.where(inside, query, 0.0).astype(BF16))
        own_g.append(jnp.where(inside, grad, 0.0).astype(BF16))
        left_q.append(jnp.concatenate([own_q[head], row_extra(lane, head, lse_terms, 1.0)], axis=1))
        left_g.append(jnp.concatenate([own_g[head], row_extra(lane, head, delta_terms, 0.0)], axis=1))
    dq_t = jnp.zeros((128, tokens), F32)

    def front(keys, head):
        return nt_dot(kx_ref[keys, :], left_q[head]), nt_dot(vx_ref[keys, :], left_g[head])

    units = [(pl.ds(start, chunk), head) for start in range(0, tokens, chunk) for head in range(2)]
    following = front(*units[0])
    for index, (keys, head) in enumerate(units):
        logits, grads = following
        if index + 1 < len(units):
            following = front(*units[index + 1])
        probs = jnp.exp(logits)
        dscore = (probs * grads).astype(BF16)
        dv_acc[keys, :] += nn_dot(probs.astype(BF16), own_g[head])
        dk_acc[keys, :] += nn_dot(dscore, own_q[head])
        dq_t = dq_t + nn_dot(kt_ref[head, :, keys], dscore)
        between()
    dq_ref[...] = (dq_t.T * 0.125).astype(BF16)
    dk_ref[...] = dk_acc[...].astype(BF16)
    dv_ref[...] = dv_acc[...].astype(BF16)


BIG = pltpu.CompilerParams(vmem_limit_bytes=56 * 1024 * 1024)
SMEM_SPEC = pl.BlockSpec(memory_space=pltpu.SMEM)


def row_stats(residual):
    mean = jnp.mean(residual, axis=1, keepdims=True)
    centered = residual - mean
    inv = lax.rsqrt(jnp.mean(centered * centered, axis=1, keepdims=True) + 1e-05)
    return centered * inv, inv


def norm_back(above, unit, inv, gain):
    scaled = above * gain
    return inv * (
        scaled
        - jnp.mean(scaled, axis=1, keepdims=True)
        - unit * jnp.mean(scaled * unit, axis=1, keepdims=True)
    )


def col_sum(value):
    return jnp.sum(value, axis=0, keepdims=True)


def vec(vec_ref, index):
    return vec_ref[pl.ds(index, 1), :]


LANG_ROW = 13


def turned_dot(left, right):
    return lax.dot_general(left, right, (((0,), (0,)), ((), ())), preferred_element_type=F32)


def ffn_rows(
    rows, live, cmixed_ref, unit_ref, cot_ref, wco_ref, win_ref, wout_ref, vec_ref, fbias_ref,
    out_ref, act_refs, low3_ref, two_ref, ghid_refs, res2_ref, low2_ref, gcm_ref, sums_ref, fsum_ref,
):
    normed_one = unit_ref[rows, :] * vec(vec_ref, 7) + vec(vec_ref, 10)
    branch = nn_dot(cmixed_ref[rows, :], flat_cols(wco_ref, EVERY)) + vec(vec_ref, 5)
    unit2, inv2 = row_stats(normed_one + branch)
    gain2 = vec(vec_ref, 8)
    normed_two = unit2 * gain2 + vec(vec_ref, 11)
    two = normed_two.astype(BF16)
    two_ref[rows, :] = two
    hidden = nn_dot(two, flat_cols(win_ref, EVERY)) + fbias_ref[...]
    square = hidden * hidden
    tanh = jnp.tanh(0.7978845608028654 * (hidden + 0.044715 * square * hidden))
    half = 0.5 * (1.0 + tanh)
    act = (hidden * half).astype(BF16)
    width = out_ref.shape[1]
    for i, ref in enumerate(act_refs):
        ref[rows, :] = act[:, i * width : (i + 1) * width]
    slope = half + (0.5 * 0.7978845608028654) * hidden * (1.0 - tanh * tanh) * (1.0 + 3 * 0.044715 * square)
    unit3, inv3 = row_stats(normed_two + nn_dot(act, flat_cols(wout_ref, EVERY)) + vec(vec_ref, 6))
    gain3 = vec(vec_ref, 9)
    out_ref[rows, :] = ((unit3 * gain3 + vec(vec_ref, 12)) * live).astype(BF16)
    above3 = cot_ref[rows, :].astype(F32) * live
    res3 = norm_back(above3, unit3, inv3, gain3)
    low3 = res3.astype(BF16)
    low3_ref[rows, :] = low3
    ghid = (nt_dot(low3, flat_cols(wout_ref, EVERY)) * slope).astype(BF16)
    for i, ref in enumerate(ghid_refs):
        ref[rows, :] = ghid[:, i * width : (i + 1) * width]
    above2 = res3 + nt_dot(ghid, flat_cols(win_ref, EVERY))
    res2 = norm_back(above2, unit2, inv2, gain2)
    res2_ref[rows, :] = res2
    low2 = res2.astype(BF16)
    low2_ref[rows, :] = low2
    gcm_ref[rows, :] = nt_dot(low2, flat_cols(wco_ref, EVERY)).astype(BF16)
    for index, value in (
        (6, low3.astype(F32)), (5, low2.astype(F32)), (9, above3 * unit3), (12, above3), (8, above2 * unit2), (11, above2),
    ):
        sums_ref[index : index + 1, :] += col_sum(value)
    fsum_ref[...] += col_sum(ghid.astype(F32))


MESH = pl.DeviceIdType.MESH
ANY_SPEC = pl.BlockSpec(memory_space=pl.ANY)
VMEM_SPEC = pl.BlockSpec(memory_space=pltpu.VMEM)
ALONG_Z, ALONG_X, ALONG_Y = 0, 1, 2
EVERY = slice(None)


class Place:
    def __init__(self, depth):
        dp, fsdp = lax.axis_index(DP), lax.axis_index(FSDP)
        self.depth = depth
        self.z, self.x = dp // 2, lax.rem(dp, 2)
        self.y, self.c = fsdp // 2, lax.rem(fsdp, 2)
        self.fsdp = fsdp

    def dev(self, z=None, x=None, y=None, c=None):
        z, x = (self.z if z is None else z), (self.x if x is None else x)
        y, c = (self.y if y is None else y), (self.c if c is None else c)
        return (2 * z + x, 2 * y + c)

    def ahead(self, d):
        return lax.rem(self.z + d, self.depth)

    def behind(self, d):
        return lax.rem(self.z + self.depth - d, self.depth)

    def greet(self):
        others = [self.dev(z=self.ahead(d)) for d in range(1, self.depth)]
        others += [self.dev(x=1 - self.x), self.dev(y=1 - self.y), self.dev(c=1 - self.c)]
        others += [self.dev(y=1 - self.y, c=1 - self.c)]
        barrier = pltpu.get_barrier_semaphore()
        for other in others:
            pl.semaphore_signal(barrier, inc=1, device_id=other, device_id_type=MESH)

    def meet(self):
        pl.semaphore_wait(pltpu.get_barrier_semaphore(), self.depth + 3)


def remote(src, dst, send, recv, device):
    return pltpu.make_async_remote_copy(
        src_ref=src, dst_ref=dst, send_sem=send, recv_sem=recv, device_id=device, device_id_type=MESH
    )


class Gather:
    def __init__(self, place, order, src, dst, local, send, recv, cols=None):
        self.place, self.order, self.src, self.dst = place, order, src, dst
        self.local, self.send, self.recv = local, send, recv
        self.cols = cols
        self.sent = []
        self.have = [place.z, place.x, place.y]

    def at(self, zxy, c):
        where = (*zxy, c)
        return self.dst.at[where] if self.cols is None else self.dst.at[(*where, EVERY, self.cols)]

    def instead(self, axis, index):
        return [index if a == axis else h for a, h in enumerate(self.have)]

    def push(self, src, dst, index, device):
        copy = remote(src, dst, self.send.at[index], self.recv.at[index], device)
        copy.start()
        self.sent.append(copy)

    def heard(self, block, index):
        remote(block, block, self.send.at[index], self.recv.at[index], self.place.dev()).wait_recv()

    def to_core(self, zxy, index):
        block = self.at(zxy, self.place.c)
        self.push(block, block, index, self.place.dev(c=1 - self.place.c))

    def start(self, stage, src=None):
        p, axis = self.place, self.order[stage]
        block = self.at(self.have, p.c)
        src = block if src is None else src
        if axis == ALONG_Z:
            for d in range(1, p.depth):
                self.push(src, block, d - 1, p.dev(z=p.ahead(d)))
        else:
            self.push(src, block, p.depth - 2 + axis, p.dev(x=1 - p.x) if axis == ALONG_X else p.dev(y=1 - p.y))

    def parts(self, stage):
        p, axis = self.place, self.order[stage]
        if axis == ALONG_Z:
            return [(self.instead(axis, p.behind(d)), d - 1) for d in range(1, p.depth)]
        other = 1 - (p.x if axis == ALONG_X else p.y)
        return [(self.instead(axis, other), p.depth - 2 + axis)]

    def arrive(self, stage):
        for zxy, index in self.parts(stage):
            self.heard(self.at(zxy, self.place.c), index)
        self.have = self.instead(self.order[stage], EVERY)

    def s0(self):
        p = self.place
        if self.src is None:
            self.start(0)
            return
        src = self.src if self.cols is None else self.src.at[:, self.cols]
        self.copy = pltpu.make_async_copy(src, self.at(self.have, p.c), self.local)
        self.copy.start()
        self.start(0, src)

    def s1(self):
        if self.src is not None:
            self.copy.wait()
        self.arrive(0)
        self.start(1)

    def s2(self):
        self.arrive(1)
        self.start(2)
        self.halfway = list(self.have)
        self.to_core(self.halfway, self.place.depth + 1)

    def s3(self):
        self.rest = [zxy for zxy, _ in self.parts(2)]
        self.arrive(2)
        for i, zxy in enumerate(self.rest):
            self.to_core(zxy, self.place.depth + 2 + i)

    def whole(self):
        p = self.place
        for i, zxy in enumerate((self.halfway, *self.rest)):
            self.heard(self.at(zxy, 1 - p.c), p.depth + 1 + i)

    def finish(self):
        for copy in self.sent:
            copy.wait_send()


class Exchange:
    def __init__(self, place, src, dst, local, send, recv):
        self.place, self.src, self.dst = place, src, dst
        self.local, self.send, self.recv = local, send, recv
        self.rows = src.shape[1]

    def block(self, owner):
        return self.dst.at[pl.ds(pl.multiple_of(owner * self.rows, self.rows), self.rows)]

    def start(self):
        me = self.place.fsdp
        self.copy = pltpu.make_async_copy(self.src.at[me], self.block(me), self.local)
        self.copy.start()
        self.sent = []
        for d in range(1, 4):
            to = lax.rem(me + d, 4)
            copy = remote(
                self.src.at[to], self.block(me), self.send.at[d - 1], self.recv.at[d - 1],
                (lax.axis_index(DP), to),
            )
            copy.start()
            self.sent.append(copy)

    def whole(self):
        self.copy.wait()
        for d in range(1, 4):
            block = self.block(lax.rem(self.place.fsdp + 4 - d, 4))
            remote(block, block, self.send.at[d - 1], self.recv.at[d - 1], self.place.dev()).wait_recv()

    def finish(self):
        for copy in self.sent:
            copy.wait_send()


def flat_cols(ref, cols):
    value = ref[:, :, :, :, :, cols]
    return value.reshape(-1, value.shape[-1])


FFN_ROW = 29


def first_kernel(
    depth,
    dlen_ref, elen_ref, tag_ref, bias_ref, gain_ref, shift_ref, table_ref, fbias_ref,
    in_ref, dec_in, enc_in, cot_in, out_in, cq_in, ckv_in, co_in, fin_in, fout_in,
    w_in, w_out, w_cq, w_ckv, enc_out, vec_out, low_out, merged_out, pair_out, mixed_out, mixf_out, lse_out, unit_out, inv_out, one_out, cq_out,
    cmixf_out, clse_out, out_out, res2_out, gcm_out, sums_out, fsum_out, gfo_out, gfi_out, gco_out,
    small_own, small, win, wkv, wout, wcq, w_co, w_fin, w_fout, cot_seq, x, enc, cot_low, vecs, fb, low, merged, pair, mixed, mixf, lse,
    unit1, inv1, one, cquery, cmixed, cmixf, clse, ghid_two, ghid_three, sums, fsum, kx, va, vb,
    wlocal, wsend, wrecv, elocal, esend, erecv, osem, csem,
):
    p = Place(depth)
    p.greet()
    tokens, features = x.shape
    langs = table_ref.shape[1]
    pairs = features // 128
    cot_loads = [
        pltpu.make_async_copy(cot_in.at[j], unit1.at[pl.ds(256 * j, 256)], csem.at[j]) for j in range(4)
    ]
    for copy in cot_loads:
        copy.start()
    tile = small_own
    tile[...] = jnp.zeros_like(tile)
    tile[0:7, :16] = bias_ref[...].astype(F32)
    tile[7:10, :16] = gain_ref[...].astype(F32)
    tile[10:13, :16] = shift_ref[...].astype(F32)
    eye = lax.broadcasted_iota(jnp.int32, (langs, langs), 0) == lax.broadcasted_iota(jnp.int32, (langs, langs), 1)
    tile[LANG_ROW : LANG_ROW + langs, :16] = nt_dot(eye.astype(F32).astype(BF16), table_ref[...])
    tile[FFN_ROW : FFN_ROW + 1, :64] = fbias_ref[...].astype(F32)
    shifted = pltpu.roll(tile[...], 16 * (4 * p.x + 2 * p.y + p.c), 1)
    ffn_row = lax.broadcasted_iota(jnp.int32, tile.shape, 0) == FFN_ROW
    small_tile = jnp.where(ffn_row, pltpu.roll(tile[...], 64 * p.c, 1), shifted).astype(BF16)
    small[p.z, p.x, p.y, p.c] = small_tile
    for i in range(pairs):
        for k in range(3):
            win[i, p.z, p.x, p.y, p.c, :, 128 * k : 128 * k + 128] = in_ref[:, features * k + 128 * i : features * k + 128 * i + 128]
    p.meet()
    jobs = []

    def gather(order, src, dst, cols=None):
        n = len(jobs)
        jobs.append(Gather(p, order, src, dst, wlocal.at[n], wsend.at[n], wrecv.at[n], cols))
        return jobs[-1]

    def part(i):
        return pl.ds(i * features, features)

    def half(i):
        return pl.ds(i * (features // 2), features // 2)

    yzx, zxy = (ALONG_Y, ALONG_Z, ALONG_X), (ALONG_Z, ALONG_X, ALONG_Y)
    dec = Exchange(p, dec_in, x, elocal.at[0], esend.at[0], erecv.at[0])
    encode = Exchange(p, enc_in, enc, elocal.at[1], esend.at[1], erecv.at[1])
    cot = Exchange(p, cot_low, cot_seq, elocal.at[2], esend.at[2], erecv.at[2])
    g_small = gather(yzx, None, small)
    g_in = [gather(yzx, None, win.at[i]) for i in range(pairs)]
    kv = [gather(yzx, ckv_in, wkv, part(i)) for i in range(2)]
    g_out, g_cq, g_co = gather(yzx, out_in, wout), gather(yzx, cq_in, wcq), gather(yzx, co_in, w_co)
    fi = [gather(yzx, fin_in, w_fin, part(i)) for i in range(4)]
    fo = [gather(order, fout_in, w_fout, half(i)) for i, order in enumerate((yzx, zxy))]

    def move(step, which):
        for job in which:
            step(job)

    writes, done = [], [0]

    def write(src, dst):
        copy = pltpu.make_async_copy(src, dst, osem.at[len(writes)])
        copy.start()
        writes.append(copy)

    def written():
        for copy in writes[done[0] :]:
            copy.wait()
        done[0] = len(writes)

    queue = [g_small, *g_in, *kv, g_out, g_cq, g_co, *fi, *fo]
    clock = [0]

    def tick(n=1):
        for _ in range(n):
            t = clock[0]
            clock[0] += 1
            for lag, step in ((4, Gather.s3), (2, Gather.s2), (0, Gather.s1)):
                if 0 <= t - lag < len(queue):
                    step(queue[t - lag])

    move(Gather.s0, queue[:7])
    dec.start()
    move(Gather.s0, queue[7:])
    tick(6)
    encode.start()
    g_small.whole()
    spread = []
    for z in range(depth):
        total = None
        for r in range(8):
            where = (z, r // 4, (r // 2) % 2, r % 2)
            tile_r = small[where].astype(F32)
            total = tile_r if total is None else total + tile_r
            at = 128 * (4 * z + r // 2)
            if r % 2 == 0:
                fb[:, at : at + 128] = tile_r[FFN_ROW : FFN_ROW + 1]
            else:
                fb[:, at : at + 128] += tile_r[FFN_ROW : FFN_ROW + 1]
        spread.append(total)
    rows_all = jnp.concatenate(spread, axis=1)
    vecs[...] = rows_all[:16]
    chosen = lax.broadcasted_iota(jnp.int32, (rows_all.shape[0], 1), 0) == tag_ref[p.fsdp] + LANG_ROW
    lang_row = col_sum(jnp.where(chosen, rows_all, 0.0))
    vecs[LANG_ROW : LANG_ROW + 1, :] = lang_row
    write(vecs, vec_out)
    dec.whole()
    low[...] = (x[...].astype(F32) + lang_row).astype(BF16)
    write(low, low_out)

    def project(source, weight, cols, bias, dest):
        def tile(i, carry):
            rows = pl.ds(pl.multiple_of(i * 512, 512), 512)
            out = nn_dot(source[rows, :], flat_cols(weight, cols))
            dest[rows, cols] = (out if bias is None else out + bias).astype(BF16)
            return carry

        lax.fori_loop(0, tokens // 512, tile, 0)

    for j in range(4):
        cot_loads[j].wait()
        cot_low[j] = unit1[256 * j : 256 * j + 256, :].astype(BF16)

    def attend(length, q, q_at, kv_ref, k_at, v_at, out, out_wide, out_lse, at, between):
        attend_fwd_core(
            512, length, q.at[:, pl.ds(q_at, 128)], kv_ref.at[:, pl.ds(k_at, 128)], kv_ref.at[:, pl.ds(v_at, 128)],
            out.at[:, pl.ds(at, 128)], out_wide.at[:, pl.ds(at, 128)], out_lse.at[:, pl.ds(at, 128)], kx, va, vb, between,
        )

    dec_len = dlen_ref[p.fsdp]
    for i in range(pairs):
        g_in[i].whole()
        at, wide = 128 * i, 384 * i

        def project_pair(j, carry, at=at, wide=wide, weight=win.at[i]):
            rows = pl.ds(pl.multiple_of(j * 512, 512), 512)
            out = nn_dot(low[rows, :], flat_cols(weight, EVERY))
            merged[rows, wide : wide + 128] = (out[:, :128] + vecs[0:1, at : at + 128]).astype(BF16)
            merged[rows, wide + 128 : wide + 256] = out[:, 128:256].astype(BF16)
            merged[rows, wide + 256 : wide + 384] = (out[:, 256:] + vecs[1:2, at : at + 128]).astype(BF16)
            return carry

        lax.fori_loop(0, tokens // 512, project_pair, 0)
        if i == 1:
            cot.start()
        attend(dec_len, merged, wide, merged, wide + 128, wide + 256, mixed, mixf, lse, at, tick)
        tick()
    for a, b in ((win, w_in), (merged, merged_out), (mixed, mixed_out), (mixf, mixf_out), (lse, lse_out)):
        write(a, b)
    encode.whole()
    write(enc, enc_out)
    kv[0].whole()
    project(enc, wkv, part(0), None, pair)
    kv[1].whole()
    project(enc, wkv, part(1), vecs[4:5, :], pair)
    write(wkv, w_ckv)
    write(pair, pair_out)
    tick()
    move(Gather.whole, (g_out, g_cq))
    write(wout, w_out)
    write(wcq, w_cq)

    def middle(i, carry):
        rows = pl.ds(pl.multiple_of(i * 256, 256), 256)
        branch = nn_dot(mixed[rows, :], flat_cols(wout, EVERY)) + vecs[2:3, :]
        unit, inv = row_stats(x[rows, :].astype(F32) + lang_row + branch)
        unit1[rows, :] = unit
        inv1[rows, :] = jnp.broadcast_to(inv, (256, 128))
        one_low = (unit * vecs[7:8, :] + vecs[10:11, :]).astype(BF16)
        one[rows, :] = one_low
        cquery[rows, :] = (nn_dot(one_low, flat_cols(wcq, EVERY)) + vecs[3:4, :]).astype(BF16)
        return carry

    lax.fori_loop(0, tokens // 256, middle, 0)
    for a, b in ((unit1, unit_out), (inv1, inv_out), (one, one_out), (cquery, cq_out)):
        write(a, b)
    enc_len = elen_ref[p.fsdp]
    tick()
    for i in range(pairs):
        at = 128 * i
        attend(enc_len, cquery, at, pair, at, features + at, cmixed, cmixf, clse, at, tick)
        tick()
    written()
    for a, b in ((cmixf, cmixf_out), (clse, clse_out)):
        write(a, b)
    low3, two, low2 = [merged.at[:, part(i)] for i in range(3)]
    gcm, output = [pair.at[:, part(i)] for i in range(2)]
    res2 = mixf
    act, ghid = (x, enc, low, mixed), (one, cquery, ghid_two, ghid_three)
    sums[...] = jnp.zeros_like(sums)
    fsum[...] = jnp.zeros_like(fsum)
    cot.whole()
    move(Gather.whole, (g_co, *fi, *fo))

    def ffn(i, carry):
        start = pl.multiple_of(i * 512, 512)
        live = (lax.broadcasted_iota(jnp.int32, (512, 1), 0) + start < dec_len).astype(F32)
        ffn_rows(
            pl.ds(start, 512), live, cmixed, unit1, cot_seq, w_co, w_fin, w_fout, vecs, fb,
            output, act, low3, two, ghid, res2, low2, gcm, sums, fsum,
        )
        return carry

    lax.fori_loop(0, tokens // 512, ffn, 0)
    for a, b in ((output, out_out), (res2, res2_out), (gcm, gcm_out), (sums, sums_out), (fsum, fsum_out)):
        write(a, b)
    for job in (*jobs, dec, encode, cot):
        job.finish()
    gco, gfi, gfo = w_co, w_fin, w_fout
    per_slab = gfo.shape[1] * gfo.shape[2] * gfo.shape[3] * gfo.shape[4]
    for i in range(len(act)):
        value = turned_dot(act[i][...], low3[...]).astype(BF16)
        for j in range(features // per_slab):
            slab = value[j * per_slab : (j + 1) * per_slab]
            gfo[i * (features // per_slab) + j] = slab.reshape(gfo.shape[1:])
    write(gfo, gfo_out)
    for i in range(len(ghid)):
        value = turned_dot(two[...], ghid[i][...]).astype(BF16)
        gfi[:, :, :, :, :, i * features : (i + 1) * features] = value.reshape(gco.shape)
    write(gfi, gfi_out)
    gco[...] = turned_dot(cmixed[...], low2[...]).astype(BF16).reshape(gco.shape)
    write(gco, gco_out)
    written()


def first_call(depth, dlen, elen, tags, biases, gains, shifts, table, fbias, dec, enc, cot, *weights):
    groups, part_rows, features = dec.shape
    tokens = groups * part_rows
    hidden = weights[5].shape[1]

    def full(shape):
        return (depth, 2, 2, 2, *shape)

    def sds(shape, dtype):
        return jax.ShapeDtypeStruct(shape, dtype)

    tf = (tokens, features)
    pairs = features // 128
    packed = (pairs, *full((weights[0].shape[0], 384)))
    full_of = [full(w.shape) for w in weights]
    outs = [sds(packed, BF16)] + [sds(s, BF16) for s in full_of[1:4]]
    outs += [sds(tf, BF16), sds((16, features), F32)]
    outs += [sds((tokens, n * features), BF16) for n in (1, 3, 2, 1)] + [sds(tf, F32)] * 2
    outs += [sds(tf, F32), sds((tokens, 128), F32), sds(tf, BF16), sds(tf, BF16), sds(tf, F32), sds(tf, F32)]
    outs += [sds(tf, BF16), sds(tf, F32), sds(tf, BF16), sds((16, features), F32), sds((1, hidden), F32)]
    outs += [sds(full_of[6], BF16), sds(full_of[5], BF16), sds(full_of[4], BF16)]
    n_jobs = 16
    dma = pltpu.SemaphoreType.DMA
    shapes = [
        ((32, 128), F32), (full((32, 128)), BF16), (packed, BF16), (full(weights[3].shape), BF16),
        (full_of[1], BF16), (full_of[2], BF16), (full_of[4], BF16), (full_of[5], BF16), (full_of[6], BF16), (tf, BF16),
        (tf, BF16), (tf, BF16), (cot.shape, BF16), ((16, features), F32), ((1, hidden), F32),
        (tf, BF16), ((tokens, 3 * features), BF16), ((tokens, 2 * features), BF16), (tf, BF16), (tf, F32), (tf, F32),
        (tf, F32), ((tokens, 128), F32), (tf, BF16), (tf, BF16), (tf, BF16), (tf, F32), (tf, F32),
        (tf, BF16), (tf, BF16),
        ((16, features), F32), ((1, hidden), F32), ((tokens, 256), BF16), ((tokens, 128), BF16), ((tokens, 128), BF16),
    ]
    return pl.pallas_call(
        functools.partial(first_kernel, depth),
        in_specs=[SMEM_SPEC] * 3 + [VMEM_SPEC] * 6 + [ANY_SPEC] * 9,
        out_specs=[ANY_SPEC] * len(outs),
        out_shape=outs,
        scratch_shapes=[pltpu.VMEM(*s) for s in shapes]
        + [dma((n_jobs,)), dma((n_jobs, depth + 5)), dma((n_jobs, depth + 5))]
        + [dma((3,)), dma((3, 3)), dma((3, 3)), dma((32,)), dma((4,))],
        compiler_params=pltpu.CompilerParams(
            vmem_limit_bytes=60 * 1024 * 1024, collective_id=1, has_side_effects=True
        ),
        name="first",
    )(dlen, elen, tags, biases, gains, shifts, table, fbias, weights[0], dec, enc, cot, *weights[1:])


class Scatter:
    def __init__(self, place, full, own, core_buf, x_buf, z_buf, y_buf, send, recv):
        self.place, self.full, self.own = place, full, own
        self.core_buf, self.x_buf, self.z_buf, self.y_buf = core_buf, x_buf, z_buf, y_buf
        self.send, self.recv = send, recv
        self.sent = []

    def push(self, src, dst, index, device):
        copy = remote(src, dst, self.send.at[index], self.recv.at[index], device)
        copy.start()
        self.sent.append(copy)

    def heard(self, block, index):
        remote(block, block, self.send.at[index], self.recv.at[index], self.place.dev()).wait_recv()

    def to_core(self):
        p = self.place
        self.push(self.full.at[:, :, :, 1 - p.c], self.core_buf, 0, p.dev(c=1 - p.c))

    def across_x(self):
        p = self.place
        self.heard(self.core_buf, 0)
        away = 1 - p.x
        for z in range(p.depth):
            total = self.core_buf[z, away].astype(F32) + self.own[z, away].astype(F32)
            self.core_buf[z, away] = total.astype(BF16)
        self.push(self.core_buf.at[:, away], self.x_buf, 1, p.dev(x=away))

    def along_z(self):
        p = self.place
        self.heard(self.x_buf, 1)
        for d in range(1, p.depth):
            z = p.ahead(d)
            total = self.x_buf[z].astype(F32) + self.core_buf[z, p.x].astype(F32) + self.own[z, p.x].astype(F32)
            self.x_buf[z] = total.astype(BF16)
            self.push(self.x_buf.at[z], self.z_buf.at[d - 1], 1 + d, p.dev(z=z))

    def here(self, y):
        p = self.place
        total = self.x_buf[p.z, y].astype(F32) + self.core_buf[p.z, p.x, y].astype(F32)
        total = total + self.own[p.z, p.x, y].astype(F32)
        for d in range(1, p.depth):
            total = total + self.z_buf[d - 1, y].astype(F32)
        return total

    def across_y(self):
        p = self.place
        for d in range(1, p.depth):
            self.heard(self.z_buf.at[d - 1], 1 + d)
        away = 1 - p.y
        self.x_buf[p.z, away] = self.here(away).astype(BF16)
        self.push(self.x_buf.at[p.z, away], self.y_buf, p.depth + 1, p.dev(y=away))

    def result(self):
        self.heard(self.y_buf, self.place.depth + 1)
        return self.here(self.place.y) + self.y_buf[...].astype(F32)

    def finish(self):
        for copy in self.sent:
            copy.wait_send()


class Return:
    def __init__(self, place, src, dst, local, send, recv):
        self.place, self.src, self.dst = place, src, dst
        self.local, self.send, self.recv = local, send, recv
        self.rows = dst.shape[1]
        self.sent = []

    def block(self, owner):
        return self.src.at[pl.ds(pl.multiple_of(owner * self.rows, self.rows), self.rows)]

    def start_one(self, d):
        me = self.place.fsdp
        if d == 0:
            self.copy = pltpu.make_async_copy(self.block(me), self.dst.at[me], self.local)
            self.copy.start()
            return
        to = lax.rem(me + d, 4)
        copy = remote(
            self.block(to), self.dst.at[me], self.send.at[d - 1], self.recv.at[d - 1], (lax.axis_index(DP), to)
        )
        copy.start()
        self.sent.append(copy)

    def start(self):
        for d in (2, 3, 1, 0):
            self.start_one(d)

    def finish(self):
        self.copy.wait()
        for d in range(1, 4):
            block = self.dst.at[lax.rem(self.place.fsdp + 4 - d, 4)]
            remote(block, block, self.send.at[d - 1], self.recv.at[d - 1], self.place.dev()).wait_recv()
        for copy in self.sent:
            copy.wait_send()


def last_kernel(
    depth, langs,
    dlen_ref, elen_ref, tag_ref, sums_in, fsum_in, vec_ref,
    gfo_in, gfi_in, gco_in, output_in, cq_in, pair_in, gcm_in, cmixf_in, clse_in,
    res2_in, unit_in, inv_in, wcq_in, wckv_in, wout_in, enc_in, one_in,
    merged_in, mixf_in, lse_in, mixed_in, low_in, win_in,
    out_ret, gin_ret, genc_ret, r_small, r_in, r_out, r_cq, r_ckv, r_co, r_fi, r_fo,
    cq, pair, gcm, cmixf, clse, res2, unit, inv, wcq, wckv, wout, enc, one, merged, mixed, low, win,
    dcq, dpair, gmix, dmerged, low1, genc_low, gin_low, sums,
    own_fo, own_fi, own_co, full_ckv, full_cq, full_out, full_in, full_small, small_t,
    c_fo, x_fo, z_fo, y_fo, c_fi, x_fi, z_fi, y_fi, c_co, x_co, z_co, y_co, c_ckv, x_ckv, z_ckv, y_ckv,
    c_cq, x_cq, z_cq, y_cq, c_out, x_out, z_out, y_out, c_in, x_in, z_in, y_in, c_sm, x_sm, z_sm, y_sm,
    kx, vx, kt, dk_acc, dv_acc,
    send, recv, rlocal, rsend, rrecv, isem,
):
    p = Place(depth)
    p.greet()
    tokens, features = cq.shape
    p_pairs = features // 128
    loads = []

    def load(src, dst):
        copy = pltpu.make_async_copy(src, dst, isem.at[len(loads)])
        copy.start()
        loads.append(copy)
        return copy

    by_pair = []
    for i in range(p_pairs):
        cols = pl.ds(128 * i, 128)
        some = [load(a.at[:, cols], b.at[:, cols]) for a, b in ((cq_in, cq), (gcm_in, gcm), (cmixf_in, cmixf), (clse_in, clse), (pair_in, pair))]
        high = pl.ds(features + 128 * i, 128)
        some.append(load(pair_in.at[:, high], pair.at[:, high]))
        by_pair.append(some)
    early = [load(gfo_in.at[:, :, :, p.c], own_fo), load(gfi_in.at[:, :, :, p.c], own_fi), load(gco_in.at[:, :, :, p.c], own_co)]
    mid = [load(a, b) for a, b in ((wcq_in, wcq), (wckv_in, wckv), (wout_in, wout), (res2_in, res2), (unit_in, unit), (inv_in, inv), (enc_in, enc), (one_in, one))]
    late = [load(a, b) for a, b in ((merged_in, merged), (mixed_in, mixed), (low_in, low), (win_in, win))]
    mixf, lse, total_in = cmixf, clse, res2

    count = [0]

    def scatter(full, own, *bufs):
        n = count[0]
        count[0] += 1
        return Scatter(p, full, own, *bufs, send.at[n], recv.at[n])

    def inner(full):
        return full.at[:, :, :, p.c]

    fo_rows, fi_cols = own_fo.shape[3] // 2, own_fi.shape[4] // 2
    s_fo = [
        scatter(gfo_in.at[:, :, :, :, rows], own_fo.at[:, :, :, rows], c_fo.at[i], x_fo.at[i], z_fo.at[i], y_fo.at[i])
        for i, rows in ((i, pl.ds(i * fo_rows, fo_rows)) for i in range(2))
    ]
    s_fi = [
        scatter(gfi_in.at[:, :, :, :, :, cols], own_fi.at[:, :, :, :, cols], c_fi.at[i], x_fi.at[i], z_fi.at[i], y_fi.at[i])
        for i, cols in ((i, pl.ds(i * fi_cols, fi_cols)) for i in range(2))
    ]
    s_co = scatter(gco_in, own_co, c_co, x_co, z_co, y_co)
    s_ckv = scatter(full_ckv, inner(full_ckv), c_ckv, x_ckv, z_ckv, y_ckv)
    s_cq = scatter(full_cq, inner(full_cq), c_cq, x_cq, z_cq, y_cq)
    s_out = scatter(full_out, inner(full_out), c_out, x_out, z_out, y_out)
    s_in = [
        scatter(full_in.at[i], inner(full_in.at[i]), c_in.at[i], x_in.at[i], z_in.at[i], y_in.at[i])
        for i in range(p_pairs)
    ]
    s_small = scatter(full_small, inner(full_small), c_sm, x_sm, z_sm, y_sm)
    b_out = Return(p, output_in, out_ret, rlocal.at[0], rsend.at[0], rrecv.at[0])
    b_enc = Return(p, genc_low, genc_ret, rlocal.at[1], rsend.at[1], rrecv.at[1])
    b_in = Return(p, gin_low, gin_ret, rlocal.at[2], rsend.at[2], rrecv.at[2])

    sums[...] = sums_in[...]

    def backward(length, q, k, v, do, of, ls, dq, dk, dv):
        attend_bwd_core(512, length, q, k, v, do, of, ls, dq, dk, dv, kx, vx, kt, dk_acc, dv_acc, between)

    def cut(ref, at):
        return ref.at[:, pl.ds(at, 128)]

    slots = [
        [], [], [], [],
        [b_out.start], [s_fo[0].across_x], [s_fi[0].across_x], [],
        [s_fo[1].across_x], [s_fi[1].across_x, s_co.across_x], [], [s_fo[0].along_z],
        [], [], [], [s_fi[0].along_z],
        [s_fo[1].along_z], [], [s_fo[0].across_y], [s_fi[0].across_y, s_fi[1].along_z],
        [], [s_out.across_x, s_co.along_z], [], [],
        [s_ckv.along_z, s_in[0].across_x], [s_cq.along_z, s_fo[1].across_y], [], [s_fi[1].across_y, s_out.along_z],
        [s_in[1].across_x, s_co.across_y], [s_in[0].along_z], [s_ckv.across_y], [s_cq.across_y],
        [s_in[2].across_x], [s_in[1].along_z], [s_out.across_y, s_in[0].across_y], [],
    ]
    slot = [0]

    def move(steps):
        for step in steps:
            step()

    def between():
        move(slots[slot[0]])
        slot[0] += 1

    enc_len = elen_ref[p.fsdp]
    for i in range(p_pairs):
        for copy in by_pair[i]:
            copy.wait()
        if i == 0:
            for copy in early:
                copy.wait()
        at = 128 * i
        backward(
            enc_len, cut(cq, at), cut(pair, at), cut(pair, features + at), cut(gcm, at), cut(cmixf, at), cut(clse, at),
            cut(dcq, at), cut(dpair, at), cut(dpair, features + at),
        )
        if i == 0:
            p.meet()
            for job in (s_fo[0], s_fi[0], s_fo[1], s_fi[1], s_co):
                job.to_core()
    late += [load(a, b) for a, b in ((mixf_in, mixf), (lse_in, lse))]
    for copy in mid:
        copy.wait()

    def weight_sum(left, right, full, cols, lead=()):
        value = turned_dot(left, right)
        shape = (depth, 2, 2, 2, value.shape[0] // (8 * depth), value.shape[1])
        full[(*lead, slice(None), slice(None), slice(None), slice(None), slice(None), cols)] = value.astype(BF16).reshape(shape)

    for part in range(2):
        cols = pl.ds(part * features, features)
        weight_sum(enc[...], dpair[:, cols], full_ckv, cols)
    s_ckv.to_core()
    weight_sum(one[...], dcq[...], full_cq, pl.ds(0, features))
    s_cq.to_core()

    for i in range(tokens // 256):
        rows = pl.ds(i * 256, 256)
        genc = nt_dot(dpair[rows, :], wckv[...])
        genc_low[rows, :] = genc.astype(BF16)
        dq = dcq[rows, :]
        above = res2[rows, :] + nt_dot(dq, wcq[...])
        units = unit[rows, :]
        res1 = norm_back(above, units, inv[rows, :1], vec(vec_ref, 7))
        total_in[rows, :] = res1
        low_one = res1.astype(BF16)
        low1[rows, :] = low_one
        gmix[rows, :] = nt_dot(low_one, wout[...]).astype(BF16)
        for index, value in (
            (2, low_one.astype(F32)), (3, dq.astype(F32)), (4, dpair[rows, features:].astype(F32)), (7, above * units), (10, above),
        ):
            sums[index : index + 1, :] += col_sum(value)
        between()
    b_enc.start()
    move([s_ckv.across_x, s_cq.across_x])
    for copy in late:
        copy.wait()
    weight_sum(mixed[...], low1[...], full_out, pl.ds(0, features))
    s_out.to_core()
    dec_len = dlen_ref[p.fsdp]
    for i in range(p_pairs):
        at = 128 * i
        wide = 384 * i
        backward(
            dec_len, cut(merged, wide), cut(merged, wide + 128), cut(merged, wide + 256), cut(gmix, at), cut(mixf, at), cut(lse, at),
            cut(dmerged, wide), cut(dmerged, wide + 128), cut(dmerged, wide + 256),
        )
        weight_sum(low[...], dmerged[:, wide : wide + 384], full_in, slice(None), (i,))
        s_in[i].to_core()

        def add_input(rows, i=i, wide=wide):
            return total_in[rows, :] + nt_dot(dmerged[rows, wide : wide + 384], win[i])

        def add_part(j, carry, add_input=add_input):
            rows = pl.ds(pl.multiple_of(j * 256, 256), 256)
            total_in[rows, :] = add_input(rows)
            return carry

        if i < p_pairs - 1:
            lax.fori_loop(0, tokens // 256, add_part, 0)
        else:
            for d in (2, 3, 1, 0):
                rows = pl.ds(pl.multiple_of(lax.rem(p.fsdp + d, 4) * b_in.rows, b_in.rows), b_in.rows)
                total = add_input(rows)
                gin_low[rows, :] = total.astype(BF16)
                b_in.start_one(d)
                sums[LANG_ROW : LANG_ROW + 1, :] += col_sum(total)
        for part, index in ((0, 0), (2, 1)):
            block = dmerged[:, wide + 128 * part : wide + 128 * part + 128].astype(F32)
            sums[index : index + 1, at : at + 128] = col_sum(block)
    move([s_in[3].across_x, s_in[2].along_z, s_in[1].across_y])
    small_t[...] = jnp.zeros_like(small_t)
    small_t[:16, :] = sums[...]
    place_tag = lax.broadcasted_iota(jnp.int32, (langs + 3, 1), 0) == tag_ref[p.fsdp]
    small_t[LANG_ROW : LANG_ROW + langs + 3, :] = jnp.where(place_tag, sums[LANG_ROW : LANG_ROW + 1, :], 0.0)
    columns = small_t[...].T.astype(BF16)
    full_small[:, :, :, :, :16, :] = columns.reshape(depth, 2, 2, 2, 16, 128)
    top = lax.broadcasted_iota(jnp.int32, (16, 128), 0) == 0
    for r in range(depth * 8):
        lanes = slice(128 * (r // 2), 128 * (r // 2) + 128)
        tile = jnp.where(top, fsum_in[:, lanes], 0.0)
        full_small[r // 8, (r // 4) % 2, (r // 2) % 2, r % 2, 16:32, :] = tile.astype(BF16)
    s_small.to_core()
    for i in range(2):
        r_fo[i * fo_rows : (i + 1) * fo_rows, :] = s_fo[i].result()
        r_fi[:, i * fi_cols : (i + 1) * fi_cols] = s_fi[i].result()
    r_co[...] = s_co.result()
    r_ckv[...] = s_ckv.result()
    move([s_small.across_x, s_in[3].along_z])
    r_cq[...] = s_cq.result()
    r_out[...] = s_out.result()
    move([s_in[2].across_y, s_small.along_z, s_in[3].across_y, s_small.across_y])
    for i in range(p_pairs):
        value = s_in[i].result()
        for part in range(3):
            at = part * features + 128 * i
            r_in[:, at : at + 128] = value[:, 128 * part : 128 * part + 128]
    r_small[...] = s_small.result()
    for job in (*s_fo, *s_fi, s_co, s_ckv, s_cq, s_out, *s_in, s_small, b_out, b_enc, b_in):
        job.finish()


def last_call(depth, langs, hidden, part_rows, dlen, elen, tags, sums, fsum, vecs, *arrays):
    tokens, features = arrays[4].shape
    pairs = features // 128
    groups = tokens // part_rows

    def sds(shape, dtype):
        return jax.ShapeDtypeStruct(shape, dtype)

    rows = features // (8 * depth)
    frows = hidden // (8 * depth)
    outs = [sds((groups, part_rows, features), BF16)] * 3
    outs += [
        sds((32, 128), F32), sds((rows, 3 * features), F32), sds((rows, features), F32), sds((rows, features), F32),
        sds((rows, 2 * features), F32), sds((rows, features), F32), sds((rows, hidden), F32), sds((frows, features), F32),
    ]

    def bufs(r, c, lead=()):
        return [
            pltpu.VMEM((*lead, depth, 2, 2, r, c), BF16), pltpu.VMEM((*lead, depth, 2, r, c), BF16),
            pltpu.VMEM((*lead, depth - 1, 2, r, c), BF16), pltpu.VMEM((*lead, r, c), BF16),
        ]

    def like(a):
        return pltpu.VMEM(a.shape, a.dtype)

    scratch = [like(a) for i, a in enumerate(arrays[4:]) if i not in (14, 15)]
    scratch += [
        pltpu.VMEM((tokens, features), BF16), pltpu.VMEM((tokens, 2 * features), BF16), pltpu.VMEM((tokens, features), BF16),
        pltpu.VMEM((tokens, 3 * features), BF16), pltpu.VMEM((tokens, features), BF16),
        pltpu.VMEM((tokens, features), BF16), pltpu.VMEM((tokens, features), BF16), pltpu.VMEM((16, features), F32),
        pltpu.VMEM((depth, 2, 2, frows, features), BF16), pltpu.VMEM((depth, 2, 2, rows, hidden), BF16), pltpu.VMEM((depth, 2, 2, rows, features), BF16),
        pltpu.VMEM((depth, 2, 2, 2, rows, 2 * features), BF16), pltpu.VMEM((depth, 2, 2, 2, rows, features), BF16), pltpu.VMEM((depth, 2, 2, 2, rows, features), BF16),
        pltpu.VMEM((pairs, depth, 2, 2, 2, rows, 384), BF16), pltpu.VMEM((depth, 2, 2, 2, 32, 128), BF16), pltpu.VMEM((128, features), F32),
    ]
    scratch += bufs(frows // 2, features, (2,)) + bufs(rows, hidden // 2, (2,)) + bufs(rows, features) + bufs(rows, 2 * features)
    scratch += bufs(rows, features) + bufs(rows, features) + bufs(rows, 384, (pairs,)) + bufs(32, 128)
    scratch += [
        pltpu.VMEM((tokens, 256), BF16), pltpu.VMEM((tokens, 256), BF16), pltpu.VMEM((2, 128, tokens), BF16),
        pltpu.VMEM((tokens, 128), F32), pltpu.VMEM((tokens, 128), F32),
        pltpu.SemaphoreType.DMA((pairs + 9, depth + 2)), pltpu.SemaphoreType.DMA((pairs + 9, depth + 2)),
        pltpu.SemaphoreType.DMA((3,)), pltpu.SemaphoreType.DMA((3, 3)), pltpu.SemaphoreType.DMA((3, 3)),
        pltpu.SemaphoreType.DMA((6 * pairs + 17,)),
    ]
    return pl.pallas_call(
        functools.partial(last_kernel, depth, langs),
        in_specs=[SMEM_SPEC] * 3 + [VMEM_SPEC] * 3 + [ANY_SPEC] * len(arrays),
        out_specs=[ANY_SPEC] * 3 + [VMEM_SPEC] * 8,
        out_shape=outs,
        scratch_shapes=scratch,
        compiler_params=pltpu.CompilerParams(
            vmem_limit_bytes=60 * 1024 * 1024, collective_id=2, has_side_effects=True
        ),
        name="last",
    )(dlen, elen, tags, sums, fsum, vecs, *arrays)


def finish_kernel(
    out_in, gin_in, genc_in, small_in, in_in, wout_in, cq_in, ckv_in, co_in, fi_in, fo_in,
    out, gin, genc, bias, gain, shift, table, fbias, r_in, r_out, r_cq, r_ckv, r_co, r_fi, r_fo, square,
):
    out[...] = out_in[...]
    gin[...] = gin_in[...].astype(F32)
    genc[...] = genc_in[...].astype(F32)

    @pl.when(pl.program_id(0) == 0)
    def _():
        for src, dst in (
            (in_in, r_in), (wout_in, r_out), (cq_in, r_cq), (ckv_in, r_ckv), (co_in, r_co), (fi_in, r_fi), (fo_in, r_fo),
        ):
            dst[...] = src[...]
        square[...] = jnp.zeros_like(square)
        square[:32, :] = small_in[...]
        turned = square[...].T
        bias[...] = turned[0:7, :16]
        gain[...] = turned[7:10, :16]
        shift[...] = turned[10:13, :16]
        table[...] = pltpu.roll(small_in[:16, :], 128 - LANG_ROW, 1)[:, : table.shape[1]]
        core = lax.rem(lax.axis_index(FSDP), 2)
        row = small_in[16:24, :]
        fbias[...] = jnp.where(core == 0, row, pltpu.roll(row, 64, 1))[0:1, :64]


def finish_call(langs, output, gin, genc, small, *sums):
    groups, part_rows, features = output.shape

    def block(a):
        return pl.BlockSpec((groups // 2, part_rows, features), lambda i: (i, 0, 0))

    def whole(a):
        return pl.BlockSpec(a.shape, lambda i: (0, 0))

    def sds(*shape):
        return jax.ShapeDtypeStruct(shape, F32)

    smalls = [sds(7, 16), sds(3, 16), sds(3, 16), sds(16, langs), sds(1, 64)]
    outs = [jax.ShapeDtypeStruct(output.shape, BF16), sds(*gin.shape), sds(*genc.shape), *smalls]
    outs += [sds(*a.shape) for a in sums]
    return pl.pallas_call(
        finish_kernel,
        grid=(2,),
        in_specs=[block(a) for a in (output, gin, genc)] + [whole(a) for a in (small, *sums)],
        out_specs=[block(a) for a in (output, gin, genc)] + [whole(a) for a in (*smalls, *sums)],
        out_shape=outs,
        scratch_shapes=[pltpu.VMEM((128, 128), F32)],
        compiler_params=BIG,
        name="finish",
    )(output, gin, genc, small, *sums)


def fast_body(
    dec_input, enc_output, dec_lengths, enc_lengths, lang_tags, lang_table, self_in, self_out, cross_q, cross_kv,
    cross_out, ffn_in, ffn_out, biases, ffn_bias, norm_gains, norm_shifts, cotangent,
):
    groups, part_rows, features = dec_input.shape
    tokens = groups * part_rows
    hidden = ffn_in.shape[1]
    langs = lang_table.shape[1]
    depth = lax.axis_size(DP) // 2
    (
        w_in, w_out, w_cq, w_ckv, enc, vecs, low, merged, pair, mixed, mixed_f32, self_lse, unit1, inv1, one, cquery,
        cmixed_f32, cross_lse, output, res2, gcm, sums, fsum, g_fout, g_fin, g_co,
    ) = first_call(
        depth, dec_lengths, enc_lengths, lang_tags, biases.T, norm_gains.T, norm_shifts.T, lang_table, ffn_bias[None],
        dec_input, enc_output, cotangent, self_in, self_out, cross_q, cross_kv, cross_out, ffn_in, ffn_out,
    )
    w_in = w_in.reshape(w_in.shape[0], -1, w_in.shape[-1])
    w_out, w_cq, w_ckv = [w.reshape(-1, w.shape[-1]) for w in (w_out, w_cq, w_ckv)]
    moved = last_call(
        depth, langs, hidden, part_rows, dec_lengths, enc_lengths, lang_tags, sums, fsum, vecs,
        g_fout, g_fin, g_co, output, cquery, pair, gcm, cmixed_f32, cross_lse, res2, unit1, inv1, w_cq, w_ckv, w_out, enc, one,
        merged, mixed_f32, self_lse, mixed, low, w_in,
    )
    output, gin, genc, bias, gain, shift, table, g_fbias, *sums = finish_call(langs, *moved)
    return (output, gin, genc, table, *sums, bias.T, g_fbias.reshape(-1), gain.T, shift.T)


def solution(mesh):
    def either(*args):
        whole_sequences = mesh.shape[FSDP] == args[0].shape[0] == 4 and mesh.shape[DP] % 2 == 0
        whole_sequences = whole_sequences and args[6].shape[0] == 16
        return (fast_body if whole_sequences else body)(*args)

    return jax.shard_map(
        either,
        mesh=mesh,
        in_specs=(
            P(DP, FSDP, None),
            P(DP, FSDP, None),
            P(DP),
            P(DP),
            P(DP),
            P(AXES, None),
            P(AXES, None),
            P(AXES, None),
            P(AXES, None),
            P(AXES, None),
            P(AXES, None),
            P(AXES, None),
            P(AXES, None),
            P(AXES, None),
            P(AXES),
            P(AXES, None),
            P(AXES, None),
            P(DP, FSDP, None),
        ),
        out_specs=(
            P(DP, FSDP, None),
            P(DP, FSDP, None),
            P(DP, FSDP, None),
            P(AXES, None),
            P(AXES, None),
            P(AXES, None),
            P(AXES, None),
            P(AXES, None),
            P(AXES, None),
            P(AXES, None),
            P(AXES, None),
            P(AXES, None),
            P(AXES),
            P(AXES, None),
            P(AXES, None),
        ),
        check_vma=False,
    )
```

```python
import functools
import math

import jax
import jax.numpy as jnp
from jax import lax
from jax.experimental import pallas as pl
from jax.experimental.pallas import tpu as pltpu
from jax.sharding import PartitionSpec as P

HEADS = 8
DP, FSDP = AXES = ("dp", "fsdp")


def smooth_gelu(values):
    return (
        0.5
        * values
        * (1.0 + jnp.tanh(0.7978845608028654 * (values + 0.044715 * values * values * values)))
    )


def times_t(left, right):
    return lax.dot_general(
        left, right, (((1,), (1,)), ((), ())), preferred_element_type=jnp.float32
    )


def outer_sum(left, right):
    return lax.dot_general(
        left, right, (((0,), (0,)), ((), ())), preferred_element_type=jnp.float32
    )


def normalize_rows(residual, gain_col, shift_col):
    row_mean = jnp.mean(residual, axis=-1, keepdims=True)
    centered = residual - row_mean
    inv_dev = lax.rsqrt(jnp.mean(centered * centered, axis=-1, keepdims=True) + 1e-05)
    unit_rows = centered * inv_dev
    return (unit_rows * gain_col + shift_col, unit_rows, inv_dev)


def normalize_back(grad_above, unit_rows, inv_dev, gain_col):
    grad_unit = grad_above * gain_col
    grad_res = inv_dev * (
        grad_unit
        - jnp.mean(grad_unit, axis=-1, keepdims=True)
        - unit_rows * jnp.mean(grad_unit * unit_rows, axis=-1, keepdims=True)
    )
    return (grad_res, jnp.sum(grad_above * unit_rows, axis=0), jnp.sum(grad_above, axis=0))


def masked_scores(query_bf, key_full, lengths_here):
    groups, rows_here, features = query_bf.shape
    key_count = key_full.shape[1]
    head_size = features // HEADS
    query_heads = query_bf.reshape(groups, rows_here, HEADS, head_size)
    key_heads = key_full.reshape(groups, key_count, HEADS, head_size)
    scores = jnp.einsum(
        "sqhd,skhd->shqk", query_heads, key_heads, preferred_element_type=jnp.float32
    ) * (1.0 / math.sqrt(head_size))
    key_valid = jnp.arange(key_count)[None, :] < lengths_here[:, None]
    return jnp.where(key_valid[:, None, None, :], scores, -1000000000.0)


def attend_forward(query_bf, key_full, value_full, lengths_here):
    groups, rows_here, features = query_bf.shape
    key_count = key_full.shape[1]
    value_heads = value_full.reshape(groups, key_count, HEADS, features // HEADS)
    scores = masked_scores(query_bf, key_full, lengths_here)
    row_max = jnp.max(scores, axis=-1, keepdims=True)
    exp_scores = jnp.exp(scores - row_max)
    row_total = jnp.sum(exp_scores, axis=-1, keepdims=True)
    probs_bf = (exp_scores / row_total).astype(jnp.bfloat16)
    attn_mixed = jnp.einsum(
        "shqk,skhd->sqhd", probs_bf, value_heads, preferred_element_type=jnp.float32
    )
    return (attn_mixed.reshape(groups, rows_here, features), row_max + jnp.log(row_total))


def attend_back(grad_mixed_bf, query_bf, key_full, value_full, lengths_here, log_total):
    groups, rows_here, features = query_bf.shape
    key_count = key_full.shape[1]
    head_size = features // HEADS
    query_heads = query_bf.reshape(groups, rows_here, HEADS, head_size)
    key_heads = key_full.reshape(groups, key_count, HEADS, head_size)
    value_heads = value_full.reshape(groups, key_count, HEADS, head_size)
    grad_heads = grad_mixed_bf.reshape(groups, rows_here, HEADS, head_size)
    attn_probs = jnp.exp(masked_scores(query_bf, key_full, lengths_here) - log_total)
    probs_bf = attn_probs.astype(jnp.bfloat16)
    grad_probs = jnp.einsum(
        "sqhd,skhd->shqk", grad_heads, value_heads, preferred_element_type=jnp.float32
    )
    grad_values = jnp.einsum(
        "shqk,sqhd->skhd", probs_bf, grad_heads, preferred_element_type=jnp.float32
    )
    grad_scores = attn_probs * (
        grad_probs - jnp.sum(attn_probs * grad_probs, axis=-1, keepdims=True)
    )
    grad_scores_bf = grad_scores.astype(jnp.bfloat16)
    score_scale = 1.0 / math.sqrt(head_size)
    grad_query = (
        jnp.einsum("shqk,skhd->sqhd", grad_scores_bf, key_heads, preferred_element_type=jnp.float32)
        * score_scale
    )
    grad_keys = (
        jnp.einsum(
            "shqk,sqhd->skhd", grad_scores_bf, query_heads, preferred_element_type=jnp.float32
        )
        * score_scale
    )
    return (
        grad_query.reshape(groups, rows_here, features),
        grad_keys.reshape(groups, key_count, features),
        grad_values.reshape(groups, key_count, features),
    )


def body(
    dec_input,
    enc_output,
    dec_lengths,
    enc_lengths,
    lang_tags,
    lang_table,
    self_in,
    self_out,
    cross_q,
    cross_kv,
    cross_out,
    ffn_in,
    ffn_out,
    biases,
    ffn_bias,
    norm_gains,
    norm_shifts,
    cotangent,
):
    full_weights = (
        lax.all_gather(lang_table, AXES, axis=0, tiled=True),
        lax.all_gather(self_in, AXES, axis=0, tiled=True),
        lax.all_gather(self_out, AXES, axis=0, tiled=True),
        lax.all_gather(cross_q, AXES, axis=0, tiled=True),
        lax.all_gather(cross_kv, AXES, axis=0, tiled=True),
        lax.all_gather(cross_out, AXES, axis=0, tiled=True),
        lax.all_gather(ffn_in, AXES, axis=0, tiled=True),
        lax.all_gather(ffn_out, AXES, axis=0, tiled=True),
        lax.all_gather(biases, AXES, axis=0, tiled=True),
        lax.all_gather(ffn_bias, AXES, axis=0, tiled=True),
        lax.all_gather(norm_gains, AXES, axis=0, tiled=True),
        lax.all_gather(norm_shifts, AXES, axis=0, tiled=True),
    )
    (
        full_table,
        full_in,
        full_out,
        full_cq,
        full_ckv,
        full_co,
        full_ffn_in,
        full_ffn_out,
        full_biases,
        full_ffn_bias,
        full_gains,
        full_shifts,
    ) = full_weights
    bias_cols = full_biases.astype(jnp.float32)
    gain_cols = full_gains.astype(jnp.float32)
    shift_cols = full_shifts.astype(jnp.float32)
    groups, rows_here, features = dec_input.shape
    enc_rows = enc_output.shape[1]
    tokens = groups * rows_here
    positions = lax.axis_index(FSDP) * rows_here + jnp.arange(rows_here)
    live_rows = (positions[None, :] < dec_lengths[:, None]).astype(jnp.float32)
    live_flat = live_rows.reshape(tokens, 1)
    onehot = (lang_tags[:, None] == jnp.arange(full_table.shape[1])[None, :]).astype(jnp.float32)
    lang_rows = lax.dot_general(
        onehot,
        full_table.astype(jnp.float32),
        (((1,), (1,)), ((), ())),
        precision=lax.Precision.HIGHEST,
        preferred_element_type=jnp.float32,
    )
    flat_start = (dec_input.astype(jnp.float32) + lang_rows[:, None, :]).reshape(tokens, features)
    start_bf = flat_start.astype(jnp.bfloat16)
    zeros_row = jnp.zeros((features,), jnp.float32)
    merged = (
        jnp.dot(start_bf, full_in, preferred_element_type=jnp.float32)
        + jnp.concatenate([bias_cols[:, 0], zeros_row, bias_cols[:, 1]])[None, :]
    )
    merged_bf = merged.astype(jnp.bfloat16).reshape(groups, rows_here, 3 * features)
    query_bf = merged_bf[:, :, :features]
    key_own = merged_bf[:, :, features : 2 * features]
    value_own = merged_bf[:, :, 2 * features :]
    key_full, value_full = (
        lax.all_gather(key_own, FSDP, axis=1, tiled=True),
        lax.all_gather(value_own, FSDP, axis=1, tiled=True),
    )
    attn_mixed, self_lse = attend_forward(query_bf, key_full, value_full, dec_lengths)
    mixed_bf = attn_mixed.astype(jnp.bfloat16).reshape(tokens, features)
    branch = jnp.dot(mixed_bf, full_out, preferred_element_type=jnp.float32) + bias_cols[:, 2]
    normed_one, unit_one, inv_one = normalize_rows(
        flat_start + branch, gain_cols[:, 0], shift_cols[:, 0]
    )
    one_bf = normed_one.astype(jnp.bfloat16)
    cross_query = (
        (jnp.dot(one_bf, full_cq, preferred_element_type=jnp.float32) + bias_cols[:, 3])
        .astype(jnp.bfloat16)
        .reshape(groups, rows_here, features)
    )
    enc_flat = enc_output.reshape(groups * enc_rows, features)
    cross_pair = (
        jnp.dot(enc_flat, full_ckv, preferred_element_type=jnp.float32)
        + jnp.concatenate([zeros_row, bias_cols[:, 4]])[None, :]
    )
    pair_bf = cross_pair.astype(jnp.bfloat16).reshape(groups, enc_rows, 2 * features)
    ckey_own = pair_bf[:, :, :features]
    cvalue_own = pair_bf[:, :, features:]
    ckey_full, cvalue_full = (
        lax.all_gather(ckey_own, FSDP, axis=1, tiled=True),
        lax.all_gather(cvalue_own, FSDP, axis=1, tiled=True),
    )
    cross_mixed, cross_lse = attend_forward(cross_query, ckey_full, cvalue_full, enc_lengths)
    cmixed_bf = cross_mixed.astype(jnp.bfloat16).reshape(tokens, features)
    cross_branch = jnp.dot(cmixed_bf, full_co, preferred_element_type=jnp.float32) + bias_cols[:, 5]
    normed_two, unit_two, inv_two = normalize_rows(
        normed_one + cross_branch, gain_cols[:, 1], shift_cols[:, 1]
    )
    two_bf = normed_two.astype(jnp.bfloat16)
    hidden = jnp.dot(
        two_bf, full_ffn_in, preferred_element_type=jnp.float32
    ) + full_ffn_bias.astype(jnp.float32)
    activated, gelu_pull = jax.vjp(smooth_gelu, hidden)
    act_bf = activated.astype(jnp.bfloat16)
    ffn_branch = jnp.dot(act_bf, full_ffn_out, preferred_element_type=jnp.float32) + bias_cols[:, 6]
    normed_three, unit_three, inv_three = normalize_rows(
        normed_two + ffn_branch, gain_cols[:, 2], shift_cols[:, 2]
    )
    output = (normed_three * live_flat).astype(jnp.bfloat16).reshape(groups, rows_here, features)
    back_weights = (
        lax.all_gather(lang_table, AXES, axis=0, tiled=True),
        lax.all_gather(self_in, AXES, axis=0, tiled=True),
        lax.all_gather(self_out, AXES, axis=0, tiled=True),
        lax.all_gather(cross_q, AXES, axis=0, tiled=True),
        lax.all_gather(cross_kv, AXES, axis=0, tiled=True),
        lax.all_gather(cross_out, AXES, axis=0, tiled=True),
        lax.all_gather(ffn_in, AXES, axis=0, tiled=True),
        lax.all_gather(ffn_out, AXES, axis=0, tiled=True),
        lax.all_gather(biases, AXES, axis=0, tiled=True),
        lax.all_gather(ffn_bias, AXES, axis=0, tiled=True),
        lax.all_gather(norm_gains, AXES, axis=0, tiled=True),
        lax.all_gather(norm_shifts, AXES, axis=0, tiled=True),
    )
    back_in = back_weights[1]
    back_out = back_weights[2]
    back_cq = back_weights[3]
    back_ckv = back_weights[4]
    back_co = back_weights[5]
    back_ffn_in = back_weights[6]
    back_ffn_out = back_weights[7]
    back_gains = back_weights[10].astype(jnp.float32)
    grad_above = cotangent.reshape(tokens, features) * live_flat
    grad_res3, gain_three, shift_three = normalize_back(
        grad_above, unit_three, inv_three, back_gains[:, 2]
    )
    grad_low3 = grad_res3.astype(jnp.bfloat16)
    grad_ffn_out = outer_sum(act_bf, grad_low3)
    bias_six = jnp.sum(grad_low3.astype(jnp.float32), axis=0)
    grad_act = times_t(grad_low3, back_ffn_out)
    grad_hidden_bf = gelu_pull(grad_act)[0].astype(jnp.bfloat16)
    grad_ffn_in = outer_sum(two_bf, grad_hidden_bf)
    grad_ffn_bias = jnp.sum(grad_hidden_bf.astype(jnp.float32), axis=0)
    grad_two = grad_res3 + times_t(grad_hidden_bf, back_ffn_in)
    grad_res2, gain_two, shift_two = normalize_back(grad_two, unit_two, inv_two, back_gains[:, 1])
    grad_low2 = grad_res2.astype(jnp.bfloat16)
    grad_cross_out = outer_sum(cmixed_bf, grad_low2)
    bias_five = jnp.sum(grad_low2.astype(jnp.float32), axis=0)
    grad_cmixed = (
        times_t(grad_low2, back_co).astype(jnp.bfloat16).reshape(groups, rows_here, features)
    )
    grad_cquery, grad_ckey, grad_cvalue = attend_back(
        grad_cmixed, cross_query, ckey_full, cvalue_full, enc_lengths, cross_lse
    )
    ckey_sum, cvalue_sum = (
        lax.psum_scatter(
            grad_ckey.astype(jnp.bfloat16), FSDP, scatter_dimension=1, tiled=True
        ).astype(jnp.float32),
        lax.psum_scatter(
            grad_cvalue.astype(jnp.bfloat16), FSDP, scatter_dimension=1, tiled=True
        ).astype(jnp.float32),
    )
    grad_pair_bf = (
        jnp.concatenate([ckey_sum, cvalue_sum], axis=-1)
        .astype(jnp.bfloat16)
        .reshape(groups * enc_rows, 2 * features)
    )
    grad_cross_kv = outer_sum(enc_flat, grad_pair_bf)
    bias_four = jnp.sum(grad_pair_bf[:, features:].astype(jnp.float32), axis=0)
    grad_encoder = times_t(grad_pair_bf, back_ckv).reshape(groups, enc_rows, features)
    grad_cquery_bf = grad_cquery.astype(jnp.bfloat16).reshape(tokens, features)
    grad_cross_q = outer_sum(one_bf, grad_cquery_bf)
    bias_three = jnp.sum(grad_cquery_bf.astype(jnp.float32), axis=0)
    grad_one = grad_res2 + times_t(grad_cquery_bf, back_cq)
    grad_res1, gain_one, shift_one = normalize_back(grad_one, unit_one, inv_one, back_gains[:, 0])
    grad_low1 = grad_res1.astype(jnp.bfloat16)
    grad_self_out = outer_sum(mixed_bf, grad_low1)
    bias_two = jnp.sum(grad_low1.astype(jnp.float32), axis=0)
    grad_mixed = (
        times_t(grad_low1, back_out).astype(jnp.bfloat16).reshape(groups, rows_here, features)
    )
    grad_query, grad_key, grad_value = attend_back(
        grad_mixed, query_bf, key_full, value_full, dec_lengths, self_lse
    )
    key_sum, value_sum = (
        lax.psum_scatter(
            grad_key.astype(jnp.bfloat16), FSDP, scatter_dimension=1, tiled=True
        ).astype(jnp.float32),
        lax.psum_scatter(
            grad_value.astype(jnp.bfloat16), FSDP, scatter_dimension=1, tiled=True
        ).astype(jnp.float32),
    )
    grad_merged_bf = (
        jnp.concatenate([grad_query, key_sum, value_sum], axis=-1)
        .astype(jnp.bfloat16)
        .reshape(tokens, 3 * features)
    )
    grad_self_in = outer_sum(start_bf, grad_merged_bf)
    merged_sums = jnp.sum(grad_merged_bf.astype(jnp.float32), axis=0)
    grad_start = grad_res1 + times_t(grad_merged_bf, back_in)
    grad_input = grad_start.reshape(groups, rows_here, features)
    seq_sums = jnp.sum(grad_input, axis=1)
    grad_table = lax.dot_general(
        seq_sums,
        onehot,
        (((0,), (0,)), ((), ())),
        precision=lax.Precision.HIGHEST,
        preferred_element_type=jnp.float32,
    )
    grad_biases = jnp.stack(
        [
            merged_sums[:features],
            merged_sums[2 * features :],
            bias_two,
            bias_three,
            bias_four,
            bias_five,
            bias_six,
        ],
        axis=1,
    )
    grad_gains = jnp.stack([gain_one, gain_two, gain_three], axis=1)
    grad_shifts = jnp.stack([shift_one, shift_two, shift_three], axis=1)
    reduced = (
        lax.psum_scatter(grad_table, AXES, scatter_dimension=0, tiled=True),
        lax.psum_scatter(grad_self_in, AXES, scatter_dimension=0, tiled=True),
        lax.psum_scatter(grad_self_out, AXES, scatter_dimension=0, tiled=True),
        lax.psum_scatter(grad_cross_q, AXES, scatter_dimension=0, tiled=True),
        lax.psum_scatter(grad_cross_kv, AXES, scatter_dimension=0, tiled=True),
        lax.psum_scatter(grad_cross_out, AXES, scatter_dimension=0, tiled=True),
        lax.psum_scatter(grad_ffn_in, AXES, scatter_dimension=0, tiled=True),
        lax.psum_scatter(grad_ffn_out, AXES, scatter_dimension=0, tiled=True),
        lax.psum_scatter(grad_biases, AXES, scatter_dimension=0, tiled=True),
        lax.psum_scatter(grad_ffn_bias, AXES, scatter_dimension=0, tiled=True),
        lax.psum_scatter(grad_gains, AXES, scatter_dimension=0, tiled=True),
        lax.psum_scatter(grad_shifts, AXES, scatter_dimension=0, tiled=True),
    )
    return (
        output,
        grad_input,
        grad_encoder,
        reduced[0],
        reduced[1],
        reduced[2],
        reduced[3],
        reduced[4],
        reduced[5],
        reduced[6],
        reduced[7],
        reduced[8],
        reduced[9],
        reduced[10],
        reduced[11],
    )


F32 = jnp.float32
BF16 = jnp.bfloat16


def nt_dot(left, right):
    return lax.dot_general(left, right, (((1,), (1,)), ((), ())), preferred_element_type=F32)


def nn_dot(left, right):
    return jnp.dot(left, right, preferred_element_type=F32)


def split_three(value):
    high = value.astype(BF16)
    rest = value - high.astype(F32)
    middle = rest.astype(BF16)
    return high, middle, (rest - middle.astype(F32)).astype(BF16)


def key_extra(tokens, length):
    lane = lax.broadcasted_iota(jnp.int32, (tokens, 128), 1) % 64
    row = lax.broadcasted_iota(jnp.int32, (tokens, 128), 0)
    masked = jnp.where(row < length, 0.0, -1e30)
    return jnp.where(lane == 3, masked, jnp.where(lane < 3, 1.0, 0.0)).astype(BF16)


def row_terms(lane, value, mask_lane):
    at = lane % 64
    high, middle, low = [term.astype(F32) for term in split_three(value)]
    rest = jnp.where(at == 3, mask_lane, 0.0)
    return jnp.where(at == 0, high, jnp.where(at == 1, middle, jnp.where(at == 2, low, rest)))


def attend_fwd_core(block, q_ref, k_ref, v_ref, o_ref, of_ref, lse_ref, kx_ref, va_ref, vb_ref, between):
    tokens = q_ref.shape[0]
    kx_ref[:, :128] = k_ref[...]
    lane_full = lax.broadcasted_iota(jnp.int32, (tokens, 128), 1)
    values = v_ref[...].astype(F32)
    va_ref[...] = jnp.where(lane_full < 64, values, 1.0).astype(BF16)
    vb_ref[...] = jnp.where(lane_full < 64, 1.0, values).astype(BF16)

    for index in range(tokens // block):
        rows = pl.ds(index * block, block)
        lane = lax.broadcasted_iota(jnp.int32, (block, 128), 1)
        query = q_ref[rows, :].astype(F32) * 0.125
        halves, tops, both = [], [], []
        for head in range(2):
            inside = (lane < 64) if head == 0 else (lane >= 64)
            own = jnp.where(inside, query, 0.0).astype(BF16)
            extra = jnp.where(lane == head * 64 + 3, 1.0, 0.0).astype(BF16)
            both.append(nt_dot(jnp.concatenate([own, extra], axis=1), kx_ref[...]))
        for scores, vx_ref in zip(both, (va_ref, vb_ref)):
            top = jnp.max(scores, axis=1, keepdims=True)
            probs = jnp.exp(scores - top).astype(BF16)
            halves.append(nn_dot(probs, vx_ref[...]))
            tops.append(top)
        number = jnp.where(lane < 64, halves[0], halves[1])
        total = pltpu.roll(jnp.where(lane < 64, halves[1], halves[0]), 64, 1)
        out = number / total
        o_ref[rows, :] = out.astype(BF16)
        of_ref[rows, :] = out
        lse_ref[rows, :] = jnp.where(lane < 64, tops[0], tops[1]) + jnp.log(total)
        if index + 1 < tokens // block:
            between()


def attend_bwd_core(
    chunk, q_ref, k_ref, v_ref, do_ref, of_ref, lse_ref, dq_ref, dk_ref, dv_ref, kx_ref, vx_ref, kt_ref, dk_acc, dv_acc, between,
):
    tokens = q_ref.shape[0]
    kx_ref[:, :128] = k_ref[...]
    vx_ref[:, :128] = v_ref[...]
    turned = k_ref[...].astype(F32).T
    sub = lax.broadcasted_iota(jnp.int32, (128, tokens), 0)
    kt_ref[0] = jnp.where(sub < 64, turned, 0.0).astype(BF16)
    kt_ref[1] = jnp.where(sub < 64, 0.0, turned).astype(BF16)
    same = (
        lax.broadcasted_iota(jnp.int32, (128, 128), 0) // 64
        == lax.broadcasted_iota(jnp.int32, (128, 128), 1) // 64
    ).astype(F32).astype(BF16)
    lane = lax.broadcasted_iota(jnp.int32, (tokens, 128), 1)
    query = q_ref[...].astype(F32) * 0.125
    grad = do_ref[...].astype(F32)
    inner = grad * of_ref[...]
    inner_high = inner.astype(BF16)
    inner_low = (inner - inner_high.astype(F32)).astype(BF16)
    delta = nn_dot(inner_high, same) + nn_dot(inner_low, same)
    lse_extra = row_terms(lane, -lse_ref[...], 1.0)
    delta_extra = row_terms(lane, -delta, 0.0)
    own_q, own_g, left_q, left_g = [], [], [], []
    for head in range(2):
        inside = (lane < 64) if head == 0 else (lane >= 64)
        own_q.append(jnp.where(inside, query, 0.0).astype(BF16))
        own_g.append(jnp.where(inside, grad, 0.0).astype(BF16))
        left_q.append(jnp.concatenate([own_q[head], jnp.where(inside, lse_extra, 0.0).astype(BF16)], axis=1))
        left_g.append(jnp.concatenate([own_g[head], jnp.where(inside, delta_extra, 0.0).astype(BF16)], axis=1))
    dq_t = jnp.zeros((128, tokens), F32)

    def front(keys, head):
        return nt_dot(kx_ref[keys, :], left_q[head]), nt_dot(vx_ref[keys, :], left_g[head])

    units = [(pl.ds(start, chunk), head) for start in range(0, tokens, chunk) for head in range(2)]
    following = front(*units[0])
    for index, (keys, head) in enumerate(units):
        logits, grads = following
        if index + 1 < len(units):
            following = front(*units[index + 1])
        probs = jnp.exp(logits)
        dscore = (probs * grads).astype(BF16)
        dv_part, dk_part = nn_dot(probs.astype(BF16), own_g[head]), nn_dot(dscore, own_q[head])
        dv_acc[keys, :] = dv_part if head == 0 else dv_acc[keys, :] + dv_part
        dk_acc[keys, :] = dk_part if head == 0 else dk_acc[keys, :] + dk_part
        dq_t = dq_t + nn_dot(kt_ref[head, :, keys], dscore)
        between()
    dq_ref[...] = (dq_t.T * 0.125).astype(BF16)
    dk_ref[...] = dk_acc[...].astype(BF16)
    dv_ref[...] = dv_acc[...].astype(BF16)


BIG = pltpu.CompilerParams(vmem_limit_bytes=56 * 1024 * 1024)
SMEM_SPEC = pl.BlockSpec(memory_space=pltpu.SMEM)


def row_stats(residual):
    mean = jnp.mean(residual, axis=1, keepdims=True)
    centered = residual - mean
    inv = lax.rsqrt(jnp.mean(centered * centered, axis=1, keepdims=True) + 1e-05)
    return centered * inv, inv


def norm_back(above, unit, inv, gain):
    scaled = above * gain
    return inv * (
        scaled
        - jnp.mean(scaled, axis=1, keepdims=True)
        - unit * jnp.mean(scaled * unit, axis=1, keepdims=True)
    )


def col_sum(value):
    return jnp.sum(value, axis=0, keepdims=True)


def vec(vec_ref, index):
    return vec_ref[pl.ds(index, 1), :]


LANG_ROW = 13


def turned_dot(left, right):
    return lax.dot_general(left, right, (((0,), (0,)), ((), ())), preferred_element_type=F32)


def ffn_rows(
    rows, live, cmixed_ref, unit_ref, cot_ref, wco_ref, win_ref, wout_ref, vec_ref, fbias_ref,
    out_ref, act_refs, low3_ref, two_ref, ghid_refs, res2_ref, low2_ref, gcm_ref, sums_ref, fsum_ref,
):
    normed_one = unit_ref[rows, :] * vec(vec_ref, 7) + vec(vec_ref, 10)
    branch = nn_dot(cmixed_ref[rows, :], flat_cols(wco_ref, EVERY)) + vec(vec_ref, 5)
    unit2, inv2 = row_stats(normed_one + branch)
    gain2 = vec(vec_ref, 8)
    normed_two = unit2 * gain2 + vec(vec_ref, 11)
    two = normed_two.astype(BF16)
    two_ref[rows, :] = two
    hidden = nn_dot(two, flat_cols(win_ref, EVERY)) + fbias_ref[...]
    square = hidden * hidden
    scale = 0.7978845608028654
    tanh = jnp.tanh(hidden * (scale + (scale * 0.044715) * square))
    half = 0.5 * (1.0 + tanh)
    act = (hidden * half).astype(BF16)
    width = out_ref.shape[1]
    for i, ref in enumerate(act_refs):
        ref[rows, :] = act[:, i * width : (i + 1) * width]
    slope = half + hidden * (1.0 - tanh * tanh) * (0.5 * scale + (1.5 * scale * 0.044715) * square)
    unit3, inv3 = row_stats(normed_two + nn_dot(act, flat_cols(wout_ref, EVERY)) + vec(vec_ref, 6))
    gain3 = vec(vec_ref, 9)
    out_ref[rows, :] = ((unit3 * gain3 + vec(vec_ref, 12)) * live).astype(BF16)
    above3 = cot_ref[rows, :].astype(F32) * live
    res3 = norm_back(above3, unit3, inv3, gain3)
    low3 = res3.astype(BF16)
    low3_ref[rows, :] = low3
    ghid = (nt_dot(low3, flat_cols(wout_ref, EVERY)) * slope).astype(BF16)
    for i, ref in enumerate(ghid_refs):
        ref[rows, :] = ghid[:, i * width : (i + 1) * width]
    above2 = res3 + nt_dot(ghid, flat_cols(win_ref, EVERY))
    res2 = norm_back(above2, unit2, inv2, gain2)
    res2_ref[rows, :] = res2
    low2 = res2.astype(BF16)
    low2_ref[rows, :] = low2
    gcm_ref[rows, :] = nt_dot(low2, flat_cols(wco_ref, EVERY)).astype(BF16)
    for index, value in (
        (6, low3.astype(F32)), (5, low2.astype(F32)), (9, above3 * unit3), (12, above3), (8, above2 * unit2), (11, above2),
    ):
        sums_ref[index : index + 1, :] += col_sum(value)
    fsum_ref[...] += col_sum(ghid.astype(F32))


MESH = pl.DeviceIdType.MESH
ANY_SPEC = pl.BlockSpec(memory_space=pl.ANY)
VMEM_SPEC = pl.BlockSpec(memory_space=pltpu.VMEM)
ALONG_Z, ALONG_X, ALONG_Y = 0, 1, 2
EVERY = slice(None)


class Place:
    def __init__(self, depth):
        dp, fsdp = lax.axis_index(DP), lax.axis_index(FSDP)
        self.depth = depth
        self.z, self.x = dp // 2, lax.rem(dp, 2)
        self.y, self.c = fsdp // 2, lax.rem(fsdp, 2)
        self.fsdp = fsdp

    def dev(self, z=None, x=None, y=None, c=None):
        z, x = (self.z if z is None else z), (self.x if x is None else x)
        y, c = (self.y if y is None else y), (self.c if c is None else c)
        return (2 * z + x, 2 * y + c)

    def ahead(self, d):
        return lax.rem(self.z + d, self.depth)

    def behind(self, d):
        return lax.rem(self.z + self.depth - d, self.depth)

    def greet(self):
        others = [self.dev(z=self.ahead(d)) for d in range(1, self.depth)]
        others += [self.dev(x=1 - self.x), self.dev(y=1 - self.y), self.dev(c=1 - self.c)]
        others += [self.dev(y=1 - self.y, c=1 - self.c)]
        barrier = pltpu.get_barrier_semaphore()
        for other in others:
            pl.semaphore_signal(barrier, inc=1, device_id=other, device_id_type=MESH)

    def meet(self):
        pl.semaphore_wait(pltpu.get_barrier_semaphore(), self.depth + 3)


def remote(src, dst, send, recv, device):
    return pltpu.make_async_remote_copy(
        src_ref=src, dst_ref=dst, send_sem=send, recv_sem=recv, device_id=device, device_id_type=MESH
    )


class Gather:
    def __init__(self, place, order, src, dst, local, send, recv, cols=None):
        self.place, self.order, self.src, self.dst = place, order, src, dst
        self.local, self.send, self.recv = local, send, recv
        self.cols = cols
        self.sent = []
        self.have = [place.z, place.x, place.y]

    def at(self, zxy, c):
        where = (*zxy, c)
        return self.dst.at[where] if self.cols is None else self.dst.at[(*where, EVERY, self.cols)]

    def instead(self, axis, index):
        return [index if a == axis else h for a, h in enumerate(self.have)]

    def push(self, src, dst, index, device):
        copy = remote(src, dst, self.send.at[index], self.recv.at[index], device)
        copy.start()
        self.sent.append(copy)

    def heard(self, block, index):
        remote(block, block, self.send.at[index], self.recv.at[index], self.place.dev()).wait_recv()

    def to_core(self, zxy, index):
        block = self.at(zxy, self.place.c)
        self.push(block, block, index, self.place.dev(c=1 - self.place.c))

    def start(self, stage, src=None):
        p, axis = self.place, self.order[stage]
        block = self.at(self.have, p.c)
        src = block if src is None else src
        if axis == ALONG_Z:
            for d in range(1, p.depth):
                self.push(src, block, d - 1, p.dev(z=p.ahead(d)))
        else:
            self.push(src, block, p.depth - 2 + axis, p.dev(x=1 - p.x) if axis == ALONG_X else p.dev(y=1 - p.y))

    def parts(self, stage):
        p, axis = self.place, self.order[stage]
        if axis == ALONG_Z:
            return [(self.instead(axis, p.behind(d)), d - 1) for d in range(1, p.depth)]
        other = 1 - (p.x if axis == ALONG_X else p.y)
        return [(self.instead(axis, other), p.depth - 2 + axis)]

    def arrive(self, stage):
        for zxy, index in self.parts(stage):
            self.heard(self.at(zxy, self.place.c), index)
        self.have = self.instead(self.order[stage], EVERY)

    def s0(self):
        p = self.place
        if self.src is None:
            self.start(0)
            return
        src = self.src if self.cols is None else self.src.at[:, self.cols]
        self.copy = pltpu.make_async_copy(src, self.at(self.have, p.c), self.local)
        self.copy.start()
        self.start(0, src)

    def s1(self):
        if self.src is not None:
            self.copy.wait()
        self.arrive(0)
        self.start(1)

    def s2(self):
        self.arrive(1)
        self.start(2)
        self.halfway = list(self.have)
        self.to_core(self.halfway, self.place.depth + 1)

    def s3(self):
        self.rest = [zxy for zxy, _ in self.parts(2)]
        self.arrive(2)
        for i, zxy in enumerate(self.rest):
            self.to_core(zxy, self.place.depth + 2 + i)

    def whole(self):
        p = self.place
        for i, zxy in enumerate((self.halfway, *self.rest)):
            self.heard(self.at(zxy, 1 - p.c), p.depth + 1 + i)

    def finish(self):
        for copy in self.sent:
            copy.wait_send()


class Exchange:
    def __init__(self, place, src, dst, local, send, recv):
        self.place, self.src, self.dst = place, src, dst
        self.local, self.send, self.recv = local, send, recv
        self.rows = src.shape[1]

    def block(self, owner):
        return self.dst.at[pl.ds(pl.multiple_of(owner * self.rows, self.rows), self.rows)]

    def start(self):
        me = self.place.fsdp
        self.copy = pltpu.make_async_copy(self.src.at[me], self.block(me), self.local)
        self.copy.start()
        self.sent = []
        for d in range(1, 4):
            to = lax.rem(me + d, 4)
            copy = remote(
                self.src.at[to], self.block(me), self.send.at[d - 1], self.recv.at[d - 1],
                (lax.axis_index(DP), to),
            )
            copy.start()
            self.sent.append(copy)

    def whole(self):
        self.copy.wait()
        for d in range(1, 4):
            block = self.block(lax.rem(self.place.fsdp + 4 - d, 4))
            remote(block, block, self.send.at[d - 1], self.recv.at[d - 1], self.place.dev()).wait_recv()

    def finish(self):
        for copy in self.sent:
            copy.wait_send()


def flat_cols(ref, cols):
    value = ref[:, :, :, :, :, cols]
    return value.reshape(-1, value.shape[-1])


FFN_ROW = 29


def first_kernel(
    depth,
    dlen_ref, elen_ref, tag_ref, bias_ref, gain_ref, shift_ref, table_ref, fbias_ref,
    in_ref, dec_in, enc_in, cot_in, out_in, cq_in, ckv_in, co_in, fin_in, fout_in,
    w_in, w_out, w_cq, w_ckv, enc_out, vec_out, low_out, merged_out, pair_out, mixed_out, mixf_out, lse_out, unit_out, inv_out, one_out, cq_out,
    cmixf_out, clse_out, out_out, res2_out, gcm_out, sums_out, fsum_out, gfo_out, gfi_out, gco_out,
    small_own, small, win, wkv, wout, wcq, w_co, w_fin, w_fout, cot_seq, x, enc, cot_low, vecs, fb, low, merged, pair, mixed, mixf, lse,
    unit1, inv1, one, cquery, cmixed, cmixf, clse, ghid_two, ghid_three, sums, fsum, kx, va, vb,
    wlocal, wsend, wrecv, elocal, esend, erecv, osem, csem,
):
    p = Place(depth)
    p.greet()
    tokens, features = x.shape
    langs = table_ref.shape[1]
    pairs = features // 128
    cot_loads = [
        pltpu.make_async_copy(cot_in.at[j], unit1.at[pl.ds(256 * j, 256)], csem.at[j]) for j in range(4)
    ]
    for copy in cot_loads:
        copy.start()
    tile = small_own
    tile[...] = jnp.zeros_like(tile)
    tile[0:7, :16] = bias_ref[...].astype(F32)
    tile[7:10, :16] = gain_ref[...].astype(F32)
    tile[10:13, :16] = shift_ref[...].astype(F32)
    eye = lax.broadcasted_iota(jnp.int32, (langs, langs), 0) == lax.broadcasted_iota(jnp.int32, (langs, langs), 1)
    tile[LANG_ROW : LANG_ROW + langs, :16] = nt_dot(eye.astype(F32).astype(BF16), table_ref[...])
    tile[FFN_ROW : FFN_ROW + 1, :64] = fbias_ref[...].astype(F32)
    shifted = pltpu.roll(tile[...], 16 * (4 * p.x + 2 * p.y + p.c), 1)
    ffn_row = lax.broadcasted_iota(jnp.int32, tile.shape, 0) == FFN_ROW
    small_tile = jnp.where(ffn_row, pltpu.roll(tile[...], 64 * p.c, 1), shifted).astype(BF16)
    small[p.z, p.x, p.y, p.c] = small_tile
    for i in range(pairs):
        for k in range(3):
            win[i, p.z, p.x, p.y, p.c, :, 128 * k : 128 * k + 128] = in_ref[:, features * k + 128 * i : features * k + 128 * i + 128]
    p.meet()
    jobs = []

    def gather(order, src, dst, cols=None):
        n = len(jobs)
        jobs.append(Gather(p, order, src, dst, wlocal.at[n], wsend.at[n], wrecv.at[n], cols))
        return jobs[-1]

    def part(i):
        return pl.ds(i * features, features)

    def half(i):
        return pl.ds(i * (features // 2), features // 2)

    yzx, zxy = (ALONG_Y, ALONG_Z, ALONG_X), (ALONG_Z, ALONG_X, ALONG_Y)
    dec = Exchange(p, dec_in, x, elocal.at[0], esend.at[0], erecv.at[0])
    encode = Exchange(p, enc_in, enc, elocal.at[1], esend.at[1], erecv.at[1])
    cot = Exchange(p, cot_low, cot_seq, elocal.at[2], esend.at[2], erecv.at[2])
    g_small = gather(yzx, None, small)
    g_in = [gather(yzx, None, win.at[i]) for i in range(pairs)]
    kv = [gather(yzx, ckv_in, wkv, part(i)) for i in range(2)]
    g_out, g_cq, g_co = gather(yzx, out_in, wout), gather(yzx, cq_in, wcq), gather(yzx, co_in, w_co)
    fi = [gather(yzx, fin_in, w_fin, part(i)) for i in range(4)]
    fo = [gather(order, fout_in, w_fout, half(i)) for i, order in enumerate((yzx, zxy))]

    def move(step, which):
        for job in which:
            step(job)

    writes, done = [], [0]

    def write(src, dst):
        copy = pltpu.make_async_copy(src, dst, osem.at[len(writes)])
        copy.start()
        writes.append(copy)

    def written():
        for copy in writes[done[0] :]:
            copy.wait()
        done[0] = len(writes)

    queue = [g_small, *g_in, *kv, g_out, g_cq, g_co, *fi, *fo]
    clock = [0]

    def tick(n=1):
        for _ in range(n):
            t = clock[0]
            clock[0] += 1
            for lag, step in ((4, Gather.s3), (2, Gather.s2), (0, Gather.s1)):
                if 0 <= t - lag < len(queue):
                    step(queue[t - lag])

    move(Gather.s0, queue[:7])
    dec.start()
    move(Gather.s0, queue[7:])
    tick(6)
    encode.start()
    g_small.whole()
    spread = []
    for z in range(depth):
        total = None
        for r in range(8):
            where = (z, r // 4, (r // 2) % 2, r % 2)
            tile_r = small[where].astype(F32)
            total = tile_r if total is None else total + tile_r
            at = 128 * (4 * z + r // 2)
            if r % 2 == 0:
                fb[:, at : at + 128] = tile_r[FFN_ROW : FFN_ROW + 1]
            else:
                fb[:, at : at + 128] += tile_r[FFN_ROW : FFN_ROW + 1]
        spread.append(total)
    rows_all = jnp.concatenate(spread, axis=1)
    vecs[...] = rows_all[:16]
    chosen = lax.broadcasted_iota(jnp.int32, (rows_all.shape[0], 1), 0) == tag_ref[p.fsdp] + LANG_ROW
    lang_row = col_sum(jnp.where(chosen, rows_all, 0.0))
    vecs[LANG_ROW : LANG_ROW + 1, :] = lang_row
    write(vecs, vec_out)
    dec.whole()
    low[...] = (x[...].astype(F32) + lang_row).astype(BF16)
    write(low, low_out)

    def project(source, weight, cols, bias, dest):
        def tile(i, carry):
            rows = pl.ds(pl.multiple_of(i * 512, 512), 512)
            out = nn_dot(source[rows, :], flat_cols(weight, cols))
            dest[rows, cols] = (out if bias is None else out + bias).astype(BF16)
            return carry

        lax.fori_loop(0, tokens // 512, tile, 0)

    for j in range(4):
        cot_loads[j].wait()
        cot_low[j] = unit1[256 * j : 256 * j + 256, :].astype(BF16)

    def attend(q, q_at, kv_ref, k_at, v_at, out, out_wide, out_lse, at, between):
        attend_fwd_core(
            512, q.at[:, pl.ds(q_at, 128)], kv_ref.at[:, pl.ds(k_at, 128)], kv_ref.at[:, pl.ds(v_at, 128)],
            out.at[:, pl.ds(at, 128)], out_wide.at[:, pl.ds(at, 128)], out_lse.at[:, pl.ds(at, 128)], kx, va, vb, between,
        )

    dec_len = dlen_ref[p.fsdp]
    kx[:, 128:] = key_extra(tokens, dec_len)
    for i in range(pairs):
        g_in[i].whole()
        at, wide = 128 * i, 384 * i

        def project_pair(j, carry, at=at, wide=wide, weight=win.at[i]):
            rows = pl.ds(pl.multiple_of(j * 512, 512), 512)
            out = nn_dot(low[rows, :], flat_cols(weight, EVERY))
            merged[rows, wide : wide + 128] = (out[:, :128] + vecs[0:1, at : at + 128]).astype(BF16)
            merged[rows, wide + 128 : wide + 256] = out[:, 128:256].astype(BF16)
            merged[rows, wide + 256 : wide + 384] = (out[:, 256:] + vecs[1:2, at : at + 128]).astype(BF16)
            return carry

        lax.fori_loop(0, tokens // 512, project_pair, 0)
        if i == 1:
            cot.start()
        attend(merged, wide, merged, wide + 128, wide + 256, mixed, mixf, lse, at, tick)
        tick()
    for a, b in ((win, w_in), (merged, merged_out), (mixed, mixed_out), (mixf, mixf_out), (lse, lse_out)):
        write(a, b)
    encode.whole()
    write(enc, enc_out)
    kv[0].whole()
    project(enc, wkv, part(0), None, pair)
    kv[1].whole()
    project(enc, wkv, part(1), vecs[4:5, :], pair)
    write(wkv, w_ckv)
    write(pair, pair_out)
    tick()
    move(Gather.whole, (g_out, g_cq))
    write(wout, w_out)
    write(wcq, w_cq)

    def middle(i, carry):
        rows = pl.ds(pl.multiple_of(i * 256, 256), 256)
        branch = nn_dot(mixed[rows, :], flat_cols(wout, EVERY)) + vecs[2:3, :]
        unit, inv = row_stats(x[rows, :].astype(F32) + lang_row + branch)
        unit1[rows, :] = unit
        inv1[rows, :] = jnp.broadcast_to(inv, (256, 128))
        one_low = (unit * vecs[7:8, :] + vecs[10:11, :]).astype(BF16)
        one[rows, :] = one_low
        cquery[rows, :] = (nn_dot(one_low, flat_cols(wcq, EVERY)) + vecs[3:4, :]).astype(BF16)
        return carry

    lax.fori_loop(0, tokens // 256, middle, 0)
    for a, b in ((unit1, unit_out), (inv1, inv_out), (one, one_out), (cquery, cq_out)):
        write(a, b)
    kx[:, 128:] = key_extra(tokens, elen_ref[p.fsdp])
    tick()
    for i in range(pairs):
        at = 128 * i
        attend(cquery, at, pair, at, features + at, cmixed, cmixf, clse, at, tick)
        tick()
    written()
    for a, b in ((cmixf, cmixf_out), (clse, clse_out)):
        write(a, b)
    low3, two, low2 = [merged.at[:, part(i)] for i in range(3)]
    gcm, output = [pair.at[:, part(i)] for i in range(2)]
    res2 = mixf
    act, ghid = (x, enc, low, mixed), (one, cquery, ghid_two, ghid_three)
    sums[...] = jnp.zeros_like(sums)
    fsum[...] = jnp.zeros_like(fsum)
    cot.whole()
    move(Gather.whole, (g_co, *fi, *fo))

    def ffn(i, carry):
        start = pl.multiple_of(i * 512, 512)
        live = (lax.broadcasted_iota(jnp.int32, (512, 1), 0) + start < dec_len).astype(F32)
        ffn_rows(
            pl.ds(start, 512), live, cmixed, unit1, cot_seq, w_co, w_fin, w_fout, vecs, fb,
            output, act, low3, two, ghid, res2, low2, gcm, sums, fsum,
        )
        return carry

    lax.fori_loop(0, tokens // 512, ffn, 0)
    for a, b in ((output, out_out), (res2, res2_out), (gcm, gcm_out), (sums, sums_out), (fsum, fsum_out)):
        write(a, b)
    for job in (*jobs, dec, encode, cot):
        job.finish()
    gco, gfi, gfo = w_co, w_fin, w_fout
    per_slab = gfo.shape[1] * gfo.shape[2] * gfo.shape[3] * gfo.shape[4]
    for i in range(len(act)):
        value = turned_dot(act[i][...], low3[...]).astype(BF16)
        for j in range(features // per_slab):
            slab = value[j * per_slab : (j + 1) * per_slab]
            gfo[i * (features // per_slab) + j] = slab.reshape(gfo.shape[1:])
    write(gfo, gfo_out)
    for i in range(len(ghid)):
        value = turned_dot(two[...], ghid[i][...]).astype(BF16)
        gfi[:, :, :, :, :, i * features : (i + 1) * features] = value.reshape(gco.shape)
    write(gfi, gfi_out)
    gco[...] = turned_dot(cmixed[...], low2[...]).astype(BF16).reshape(gco.shape)
    write(gco, gco_out)
    written()


def first_call(depth, dlen, elen, tags, biases, gains, shifts, table, fbias, dec, enc, cot, *weights):
    groups, part_rows, features = dec.shape
    tokens = groups * part_rows
    hidden = weights[5].shape[1]

    def full(shape):
        return (depth, 2, 2, 2, *shape)

    def sds(shape, dtype):
        return jax.ShapeDtypeStruct(shape, dtype)

    tf = (tokens, features)
    pairs = features // 128
    packed = (pairs, *full((weights[0].shape[0], 384)))
    full_of = [full(w.shape) for w in weights]
    outs = [sds(packed, BF16)] + [sds(s, BF16) for s in full_of[1:4]]
    outs += [sds(tf, BF16), sds((16, features), F32)]
    outs += [sds((tokens, n * features), BF16) for n in (1, 3, 2, 1)] + [sds(tf, F32)] * 2
    outs += [sds(tf, F32), sds((tokens, 128), F32), sds(tf, BF16), sds(tf, BF16), sds(tf, F32), sds(tf, F32)]
    outs += [sds(tf, BF16), sds(tf, F32), sds(tf, BF16), sds((16, features), F32), sds((1, hidden), F32)]
    outs += [sds(full_of[6], BF16), sds(full_of[5], BF16), sds(full_of[4], BF16)]
    n_jobs = 16
    dma = pltpu.SemaphoreType.DMA
    shapes = [
        ((32, 128), F32), (full((32, 128)), BF16), (packed, BF16), (full(weights[3].shape), BF16),
        (full_of[1], BF16), (full_of[2], BF16), (full_of[4], BF16), (full_of[5], BF16), (full_of[6], BF16), (tf, BF16),
        (tf, BF16), (tf, BF16), (cot.shape, BF16), ((16, features), F32), ((1, hidden), F32),
        (tf, BF16), ((tokens, 3 * features), BF16), ((tokens, 2 * features), BF16), (tf, BF16), (tf, F32), (tf, F32),
        (tf, F32), ((tokens, 128), F32), (tf, BF16), (tf, BF16), (tf, BF16), (tf, F32), (tf, F32),
        (tf, BF16), (tf, BF16),
        ((16, features), F32), ((1, hidden), F32), ((tokens, 256), BF16), ((tokens, 128), BF16), ((tokens, 128), BF16),
    ]
    return pl.pallas_call(
        functools.partial(first_kernel, depth),
        in_specs=[SMEM_SPEC] * 3 + [VMEM_SPEC] * 6 + [ANY_SPEC] * 9,
        out_specs=[ANY_SPEC] * len(outs),
        out_shape=outs,
        scratch_shapes=[pltpu.VMEM(*s) for s in shapes]
        + [dma((n_jobs,)), dma((n_jobs, depth + 5)), dma((n_jobs, depth + 5))]
        + [dma((3,)), dma((3, 3)), dma((3, 3)), dma((32,)), dma((4,))],
        compiler_params=pltpu.CompilerParams(
            vmem_limit_bytes=60 * 1024 * 1024, collective_id=1, has_side_effects=True
        ),
        name="first",
    )(dlen, elen, tags, biases, gains, shifts, table, fbias, weights[0], dec, enc, cot, *weights[1:])


class Scatter:
    def __init__(self, place, full, own, core_buf, x_buf, z_buf, y_buf, send, recv):
        self.place, self.full, self.own = place, full, own
        self.core_buf, self.x_buf, self.z_buf, self.y_buf = core_buf, x_buf, z_buf, y_buf
        self.send, self.recv = send, recv
        self.sent = []

    def push(self, src, dst, index, device):
        copy = remote(src, dst, self.send.at[index], self.recv.at[index], device)
        copy.start()
        self.sent.append(copy)

    def heard(self, block, index):
        remote(block, block, self.send.at[index], self.recv.at[index], self.place.dev()).wait_recv()

    def to_core(self):
        p = self.place
        self.push(self.full.at[:, :, :, 1 - p.c], self.core_buf, 0, p.dev(c=1 - p.c))

    def across_x(self):
        p = self.place
        self.heard(self.core_buf, 0)
        away = 1 - p.x
        for z in range(p.depth):
            total = self.core_buf[z, away].astype(F32) + self.own[z, away].astype(F32)
            self.core_buf[z, away] = total.astype(BF16)
        self.push(self.core_buf.at[:, away], self.x_buf, 1, p.dev(x=away))

    def along_z(self):
        p = self.place
        self.heard(self.x_buf, 1)
        for d in range(1, p.depth):
            z = p.ahead(d)
            total = self.x_buf[z].astype(F32) + self.core_buf[z, p.x].astype(F32) + self.own[z, p.x].astype(F32)
            self.x_buf[z] = total.astype(BF16)
            self.push(self.x_buf.at[z], self.z_buf.at[d - 1], 1 + d, p.dev(z=z))

    def here(self, y):
        p = self.place
        total = self.x_buf[p.z, y].astype(F32) + self.core_buf[p.z, p.x, y].astype(F32)
        total = total + self.own[p.z, p.x, y].astype(F32)
        for d in range(1, p.depth):
            total = total + self.z_buf[d - 1, y].astype(F32)
        return total

    def across_y(self):
        p = self.place
        for d in range(1, p.depth):
            self.heard(self.z_buf.at[d - 1], 1 + d)
        away = 1 - p.y
        self.x_buf[p.z, away] = self.here(away).astype(BF16)
        self.push(self.x_buf.at[p.z, away], self.y_buf, p.depth + 1, p.dev(y=away))

    def result(self):
        self.heard(self.y_buf, self.place.depth + 1)
        return self.here(self.place.y) + self.y_buf[...].astype(F32)

    def finish(self):
        for copy in self.sent:
            copy.wait_send()


class Return:
    def __init__(self, place, src, dst, local, send, recv):
        self.place, self.src, self.dst = place, src, dst
        self.local, self.send, self.recv = local, send, recv
        self.rows = dst.shape[1]
        self.sent = []

    def block(self, owner):
        return self.src.at[pl.ds(pl.multiple_of(owner * self.rows, self.rows), self.rows)]

    def start_one(self, d):
        me = self.place.fsdp
        if d == 0:
            self.copy = pltpu.make_async_copy(self.block(me), self.dst.at[me], self.local)
            self.copy.start()
            return
        to = lax.rem(me + d, 4)
        copy = remote(
            self.block(to), self.dst.at[me], self.send.at[d - 1], self.recv.at[d - 1], (lax.axis_index(DP), to)
        )
        copy.start()
        self.sent.append(copy)

    def start(self):
        for d in (2, 3, 1, 0):
            self.start_one(d)

    def finish(self):
        self.copy.wait()
        for d in range(1, 4):
            block = self.dst.at[lax.rem(self.place.fsdp + 4 - d, 4)]
            remote(block, block, self.send.at[d - 1], self.recv.at[d - 1], self.place.dev()).wait_recv()
        for copy in self.sent:
            copy.wait_send()


def last_kernel(
    depth, langs,
    dlen_ref, elen_ref, tag_ref, sums_in, fsum_in, vec_ref,
    gfo_in, gfi_in, gco_in, output_in, cq_in, pair_in, gcm_in, cmixf_in, clse_in,
    res2_in, unit_in, inv_in, wcq_in, wckv_in, wout_in, enc_in, one_in,
    merged_in, mixf_in, lse_in, mixed_in, low_in, win_in,
    out_ret, gin_ret, genc_ret, r_small, r_in, r_out, r_cq, r_ckv, r_co, r_fi, r_fo,
    cq, pair, gcm, cmixf, clse, res2, unit, inv, wcq, wckv, wout, enc, one, merged, mixed, low, win,
    dcq, dpair, gmix, dmerged, low1, genc_low, gin_low, sums,
    own_fo, own_fi, own_co, full_ckv, full_cq, full_out, full_in, full_small, small_t,
    c_fo, x_fo, z_fo, y_fo, c_fi, x_fi, z_fi, y_fi, c_co, x_co, z_co, y_co, c_ckv, x_ckv, z_ckv, y_ckv,
    c_cq, x_cq, z_cq, y_cq, c_out, x_out, z_out, y_out, c_in, x_in, z_in, y_in, c_sm, x_sm, z_sm, y_sm,
    kx, vx, kt, dk_acc, dv_acc,
    send, recv, rlocal, rsend, rrecv, isem,
):
    p = Place(depth)
    p.greet()
    tokens, features = cq.shape
    p_pairs = features // 128
    loads = []

    def load(src, dst):
        copy = pltpu.make_async_copy(src, dst, isem.at[len(loads)])
        copy.start()
        loads.append(copy)
        return copy

    by_pair = []
    for i in range(p_pairs):
        cols = pl.ds(128 * i, 128)
        some = [load(a.at[:, cols], b.at[:, cols]) for a, b in ((cq_in, cq), (gcm_in, gcm), (cmixf_in, cmixf), (clse_in, clse), (pair_in, pair))]
        high = pl.ds(features + 128 * i, 128)
        some.append(load(pair_in.at[:, high], pair.at[:, high]))
        by_pair.append(some)
    early = [load(gfo_in.at[:, :, :, p.c], own_fo), load(gfi_in.at[:, :, :, p.c], own_fi), load(gco_in.at[:, :, :, p.c], own_co)]
    mid = [load(a, b) for a, b in ((wcq_in, wcq), (wckv_in, wckv), (wout_in, wout), (res2_in, res2), (unit_in, unit), (inv_in, inv), (enc_in, enc), (one_in, one))]
    late = [load(a, b) for a, b in ((merged_in, merged), (mixed_in, mixed), (low_in, low), (win_in, win))]
    mixf, lse, total_in = cmixf, clse, res2

    count = [0]

    def scatter(full, own, *bufs):
        n = count[0]
        count[0] += 1
        return Scatter(p, full, own, *bufs, send.at[n], recv.at[n])

    def inner(full):
        return full.at[:, :, :, p.c]

    fo_rows, fi_cols = own_fo.shape[3] // 2, own_fi.shape[4] // 2
    s_fo = [
        scatter(gfo_in.at[:, :, :, :, rows], own_fo.at[:, :, :, rows], c_fo.at[i], x_fo.at[i], z_fo.at[i], y_fo.at[i])
        for i, rows in ((i, pl.ds(i * fo_rows, fo_rows)) for i in range(2))
    ]
    s_fi = [
        scatter(gfi_in.at[:, :, :, :, :, cols], own_fi.at[:, :, :, :, cols], c_fi.at[i], x_fi.at[i], z_fi.at[i], y_fi.at[i])
        for i, cols in ((i, pl.ds(i * fi_cols, fi_cols)) for i in range(2))
    ]
    s_co = scatter(gco_in, own_co, c_co, x_co, z_co, y_co)
    s_ckv = scatter(full_ckv, inner(full_ckv), c_ckv, x_ckv, z_ckv, y_ckv)
    s_cq = scatter(full_cq, inner(full_cq), c_cq, x_cq, z_cq, y_cq)
    s_out = scatter(full_out, inner(full_out), c_out, x_out, z_out, y_out)
    s_in = [
        scatter(full_in.at[i], inner(full_in.at[i]), c_in.at[i], x_in.at[i], z_in.at[i], y_in.at[i])
        for i in range(p_pairs)
    ]
    s_small = scatter(full_small, inner(full_small), c_sm, x_sm, z_sm, y_sm)
    b_out = Return(p, output_in, out_ret, rlocal.at[0], rsend.at[0], rrecv.at[0])
    b_enc = Return(p, genc_low, genc_ret, rlocal.at[1], rsend.at[1], rrecv.at[1])
    b_in = Return(p, gin_low, gin_ret, rlocal.at[2], rsend.at[2], rrecv.at[2])

    sums[...] = sums_in[...]

    def backward(q, k, v, do, of, ls, dq, dk, dv):
        attend_bwd_core(512, q, k, v, do, of, ls, dq, dk, dv, kx, vx, kt, dk_acc, dv_acc, between)

    def cut(ref, at):
        return ref.at[:, pl.ds(at, 128)]

    slots = [
        [], [], [], [],
        [b_out.start], [s_fo[0].across_x], [s_fi[0].across_x], [],
        [s_fo[1].across_x], [s_fi[1].across_x, s_co.across_x], [], [s_fo[0].along_z],
        [], [], [], [s_fi[0].along_z],
        [s_fo[1].along_z], [], [s_fo[0].across_y], [s_fi[0].across_y, s_fi[1].along_z],
        [], [s_out.across_x, s_co.along_z], [], [],
        [s_ckv.along_z, s_in[0].across_x], [s_cq.along_z, s_fo[1].across_y], [], [s_fi[1].across_y, s_out.along_z],
        [s_in[1].across_x, s_co.across_y], [s_in[0].along_z], [s_ckv.across_y], [s_cq.across_y],
        [s_in[2].across_x], [s_in[1].along_z], [s_out.across_y, s_in[0].across_y], [],
    ]
    slot = [0]

    def move(steps):
        for step in steps:
            step()

    def between():
        move(slots[slot[0]])
        slot[0] += 1

    def mask(length):
        extra = key_extra(tokens, length)
        kx[:, 128:] = extra
        vx[:, 128:] = extra

    mask(elen_ref[p.fsdp])
    for i in range(p_pairs):
        for copy in by_pair[i]:
            copy.wait()
        if i == 0:
            for copy in early:
                copy.wait()
        at = 128 * i
        backward(
            cut(cq, at), cut(pair, at), cut(pair, features + at), cut(gcm, at), cut(cmixf, at), cut(clse, at),
            cut(dcq, at), cut(dpair, at), cut(dpair, features + at),
        )
        if i == 0:
            p.meet()
            for job in (s_fo[0], s_fi[0], s_fo[1], s_fi[1], s_co):
                job.to_core()
    late += [load(a, b) for a, b in ((mixf_in, mixf), (lse_in, lse))]
    for copy in mid:
        copy.wait()

    def weight_sum(left, right, full, cols, lead=()):
        value = turned_dot(left, right)
        shape = (depth, 2, 2, 2, value.shape[0] // (8 * depth), value.shape[1])
        full[(*lead, slice(None), slice(None), slice(None), slice(None), slice(None), cols)] = value.astype(BF16).reshape(shape)

    for part in range(2):
        cols = pl.ds(part * features, features)
        weight_sum(enc[...], dpair[:, cols], full_ckv, cols)
    s_ckv.to_core()
    weight_sum(one[...], dcq[...], full_cq, pl.ds(0, features))
    s_cq.to_core()

    for i in range(tokens // 256):
        rows = pl.ds(i * 256, 256)
        genc = nt_dot(dpair[rows, :], wckv[...])
        genc_low[rows, :] = genc.astype(BF16)
        dq = dcq[rows, :]
        above = res2[rows, :] + nt_dot(dq, wcq[...])
        units = unit[rows, :]
        res1 = norm_back(above, units, inv[rows, :1], vec(vec_ref, 7))
        total_in[rows, :] = res1
        low_one = res1.astype(BF16)
        low1[rows, :] = low_one
        gmix[rows, :] = nt_dot(low_one, wout[...]).astype(BF16)
        for index, value in (
            (2, low_one.astype(F32)), (3, dq.astype(F32)), (4, dpair[rows, features:].astype(F32)), (7, above * units), (10, above),
        ):
            sums[index : index + 1, :] += col_sum(value)
        between()
    b_enc.start()
    move([s_ckv.across_x, s_cq.across_x])
    for copy in late:
        copy.wait()
    weight_sum(mixed[...], low1[...], full_out, pl.ds(0, features))
    s_out.to_core()
    mask(dlen_ref[p.fsdp])
    for i in range(p_pairs):
        at = 128 * i
        wide = 384 * i
        backward(
            cut(merged, wide), cut(merged, wide + 128), cut(merged, wide + 256), cut(gmix, at), cut(mixf, at), cut(lse, at),
            cut(dmerged, wide), cut(dmerged, wide + 128), cut(dmerged, wide + 256),
        )
        weight_sum(low[...], dmerged[:, wide : wide + 384], full_in, slice(None), (i,))
        s_in[i].to_core()

        def add_input(rows, i=i, wide=wide):
            return total_in[rows, :] + nt_dot(dmerged[rows, wide : wide + 384], win[i])

        def add_part(j, carry, add_input=add_input):
            rows = pl.ds(pl.multiple_of(j * 256, 256), 256)
            total_in[rows, :] = add_input(rows)
            return carry

        if i < p_pairs - 1:
            lax.fori_loop(0, tokens // 256, add_part, 0)
        else:
            for d in (2, 3, 1, 0):
                rows = pl.ds(pl.multiple_of(lax.rem(p.fsdp + d, 4) * b_in.rows, b_in.rows), b_in.rows)
                total = add_input(rows)
                gin_low[rows, :] = total.astype(BF16)
                b_in.start_one(d)
                sums[LANG_ROW : LANG_ROW + 1, :] += col_sum(total)
        for part, index in ((0, 0), (2, 1)):
            block = dmerged[:, wide + 128 * part : wide + 128 * part + 128].astype(F32)
            sums[index : index + 1, at : at + 128] = col_sum(block)
    move([s_in[3].across_x, s_in[2].along_z, s_in[1].across_y])
    small_t[...] = jnp.zeros_like(small_t)
    small_t[:16, :] = sums[...]
    place_tag = lax.broadcasted_iota(jnp.int32, (langs + 3, 1), 0) == tag_ref[p.fsdp]
    small_t[LANG_ROW : LANG_ROW + langs + 3, :] = jnp.where(place_tag, sums[LANG_ROW : LANG_ROW + 1, :], 0.0)
    columns = small_t[...].T.astype(BF16)
    full_small[:, :, :, :, :16, :] = columns.reshape(depth, 2, 2, 2, 16, 128)
    top = lax.broadcasted_iota(jnp.int32, (16, 128), 0) == 0
    for r in range(depth * 8):
        lanes = slice(128 * (r // 2), 128 * (r // 2) + 128)
        tile = jnp.where(top, fsum_in[:, lanes], 0.0)
        full_small[r // 8, (r // 4) % 2, (r // 2) % 2, r % 2, 16:32, :] = tile.astype(BF16)
    s_small.to_core()
    for i in range(2):
        r_fo[i * fo_rows : (i + 1) * fo_rows, :] = s_fo[i].result()
        r_fi[:, i * fi_cols : (i + 1) * fi_cols] = s_fi[i].result()
    r_co[...] = s_co.result()
    r_ckv[...] = s_ckv.result()
    move([s_small.across_x, s_in[3].along_z])
    r_cq[...] = s_cq.result()
    r_out[...] = s_out.result()
    move([s_in[2].across_y, s_small.along_z, s_in[3].across_y, s_small.across_y])
    for i in range(p_pairs):
        value = s_in[i].result()
        for part in range(3):
            at = part * features + 128 * i
            r_in[:, at : at + 128] = value[:, 128 * part : 128 * part + 128]
    r_small[...] = s_small.result()
    for job in (*s_fo, *s_fi, s_co, s_ckv, s_cq, s_out, *s_in, s_small, b_out, b_enc, b_in):
        job.finish()


def last_call(depth, langs, hidden, part_rows, dlen, elen, tags, sums, fsum, vecs, *arrays):
    tokens, features = arrays[4].shape
    pairs = features // 128
    groups = tokens // part_rows

    def sds(shape, dtype):
        return jax.ShapeDtypeStruct(shape, dtype)

    rows = features // (8 * depth)
    frows = hidden // (8 * depth)
    outs = [sds((groups, part_rows, features), BF16)] * 3
    outs += [
        sds((32, 128), F32), sds((rows, 3 * features), F32), sds((rows, features), F32), sds((rows, features), F32),
        sds((rows, 2 * features), F32), sds((rows, features), F32), sds((rows, hidden), F32), sds((frows, features), F32),
    ]

    def bufs(r, c, lead=()):
        return [
            pltpu.VMEM((*lead, depth, 2, 2, r, c), BF16), pltpu.VMEM((*lead, depth, 2, r, c), BF16),
            pltpu.VMEM((*lead, depth - 1, 2, r, c), BF16), pltpu.VMEM((*lead, r, c), BF16),
        ]

    def like(a):
        return pltpu.VMEM(a.shape, a.dtype)

    scratch = [like(a) for i, a in enumerate(arrays[4:]) if i not in (14, 15)]
    scratch += [
        pltpu.VMEM((tokens, features), BF16), pltpu.VMEM((tokens, 2 * features), BF16), pltpu.VMEM((tokens, features), BF16),
        pltpu.VMEM((tokens, 3 * features), BF16), pltpu.VMEM((tokens, features), BF16),
        pltpu.VMEM((tokens, features), BF16), pltpu.VMEM((tokens, features), BF16), pltpu.VMEM((16, features), F32),
        pltpu.VMEM((depth, 2, 2, frows, features), BF16), pltpu.VMEM((depth, 2, 2, rows, hidden), BF16), pltpu.VMEM((depth, 2, 2, rows, features), BF16),
        pltpu.VMEM((depth, 2, 2, 2, rows, 2 * features), BF16), pltpu.VMEM((depth, 2, 2, 2, rows, features), BF16), pltpu.VMEM((depth, 2, 2, 2, rows, features), BF16),
        pltpu.VMEM((pairs, depth, 2, 2, 2, rows, 384), BF16), pltpu.VMEM((depth, 2, 2, 2, 32, 128), BF16), pltpu.VMEM((128, features), F32),
    ]
    scratch += bufs(frows // 2, features, (2,)) + bufs(rows, hidden // 2, (2,)) + bufs(rows, features) + bufs(rows, 2 * features)
    scratch += bufs(rows, features) + bufs(rows, features) + bufs(rows, 384, (pairs,)) + bufs(32, 128)
    scratch += [
        pltpu.VMEM((tokens, 256), BF16), pltpu.VMEM((tokens, 256), BF16), pltpu.VMEM((2, 128, tokens), BF16),
        pltpu.VMEM((tokens, 128), F32), pltpu.VMEM((tokens, 128), F32),
        pltpu.SemaphoreType.DMA((pairs + 9, depth + 2)), pltpu.SemaphoreType.DMA((pairs + 9, depth + 2)),
        pltpu.SemaphoreType.DMA((3,)), pltpu.SemaphoreType.DMA((3, 3)), pltpu.SemaphoreType.DMA((3, 3)),
        pltpu.SemaphoreType.DMA((6 * pairs + 17,)),
    ]
    return pl.pallas_call(
        functools.partial(last_kernel, depth, langs),
        in_specs=[SMEM_SPEC] * 3 + [VMEM_SPEC] * 3 + [ANY_SPEC] * len(arrays),
        out_specs=[ANY_SPEC] * 3 + [VMEM_SPEC] * 8,
        out_shape=outs,
        scratch_shapes=scratch,
        compiler_params=pltpu.CompilerParams(
            vmem_limit_bytes=60 * 1024 * 1024, collective_id=2, has_side_effects=True
        ),
        name="last",
    )(dlen, elen, tags, sums, fsum, vecs, *arrays)


def finish_kernel(
    out_in, gin_in, genc_in, small_in, in_in, wout_in, cq_in, ckv_in, co_in, fi_in, fo_in,
    out, gin, genc, bias, gain, shift, table, fbias, r_in, r_out, r_cq, r_ckv, r_co, r_fi, r_fo, square,
):
    out[...] = out_in[...]
    gin[...] = gin_in[...].astype(F32)
    genc[...] = genc_in[...].astype(F32)

    @pl.when(pl.program_id(0) == 0)
    def _():
        for src, dst in (
            (in_in, r_in), (wout_in, r_out), (cq_in, r_cq), (ckv_in, r_ckv), (co_in, r_co), (fi_in, r_fi), (fo_in, r_fo),
        ):
            dst[...] = src[...]
        square[...] = jnp.zeros_like(square)
        square[:32, :] = small_in[...]
        turned = square[...].T
        bias[...] = turned[0:7, :16]
        gain[...] = turned[7:10, :16]
        shift[...] = turned[10:13, :16]
        table[...] = pltpu.roll(small_in[:16, :], 128 - LANG_ROW, 1)[:, : table.shape[1]]
        core = lax.rem(lax.axis_index(FSDP), 2)
        row = small_in[16:24, :]
        fbias[...] = jnp.where(core == 0, row, pltpu.roll(row, 64, 1))[0:1, :64]


def finish_call(langs, output, gin, genc, small, *sums):
    groups, part_rows, features = output.shape

    def block(a):
        return pl.BlockSpec((groups // 2, part_rows, features), lambda i: (i, 0, 0))

    def whole(a):
        return pl.BlockSpec(a.shape, lambda i: (0, 0))

    def sds(*shape):
        return jax.ShapeDtypeStruct(shape, F32)

    smalls = [sds(7, 16), sds(3, 16), sds(3, 16), sds(16, langs), sds(1, 64)]
    outs = [jax.ShapeDtypeStruct(output.shape, BF16), sds(*gin.shape), sds(*genc.shape), *smalls]
    outs += [sds(*a.shape) for a in sums]
    return pl.pallas_call(
        finish_kernel,
        grid=(2,),
        in_specs=[block(a) for a in (output, gin, genc)] + [whole(a) for a in (small, *sums)],
        out_specs=[block(a) for a in (output, gin, genc)] + [whole(a) for a in (*smalls, *sums)],
        out_shape=outs,
        scratch_shapes=[pltpu.VMEM((128, 128), F32)],
        compiler_params=BIG,
        name="finish",
    )(output, gin, genc, small, *sums)


def fast_body(
    dec_input, enc_output, dec_lengths, enc_lengths, lang_tags, lang_table, self_in, self_out, cross_q, cross_kv,
    cross_out, ffn_in, ffn_out, biases, ffn_bias, norm_gains, norm_shifts, cotangent,
):
    groups, part_rows, features = dec_input.shape
    tokens = groups * part_rows
    hidden = ffn_in.shape[1]
    langs = lang_table.shape[1]
    depth = lax.axis_size(DP) // 2
    (
        w_in, w_out, w_cq, w_ckv, enc, vecs, low, merged, pair, mixed, mixed_f32, self_lse, unit1, inv1, one, cquery,
        cmixed_f32, cross_lse, output, res2, gcm, sums, fsum, g_fout, g_fin, g_co,
    ) = first_call(
        depth, dec_lengths, enc_lengths, lang_tags, biases.T, norm_gains.T, norm_shifts.T, lang_table, ffn_bias[None],
        dec_input, enc_output, cotangent, self_in, self_out, cross_q, cross_kv, cross_out, ffn_in, ffn_out,
    )
    w_in = w_in.reshape(w_in.shape[0], -1, w_in.shape[-1])
    w_out, w_cq, w_ckv = [w.reshape(-1, w.shape[-1]) for w in (w_out, w_cq, w_ckv)]
    moved = last_call(
        depth, langs, hidden, part_rows, dec_lengths, enc_lengths, lang_tags, sums, fsum, vecs,
        g_fout, g_fin, g_co, output, cquery, pair, gcm, cmixed_f32, cross_lse, res2, unit1, inv1, w_cq, w_ckv, w_out, enc, one,
        merged, mixed_f32, self_lse, mixed, low, w_in,
    )
    output, gin, genc, bias, gain, shift, table, g_fbias, *sums = finish_call(langs, *moved)
    return (output, gin, genc, table, *sums, bias.T, g_fbias.reshape(-1), gain.T, shift.T)


def solution(mesh):
    def either(*args):
        whole_sequences = mesh.shape[FSDP] == args[0].shape[0] == 4 and mesh.shape[DP] % 2 == 0
        whole_sequences = whole_sequences and args[6].shape[0] == 16
        return (fast_body if whole_sequences else body)(*args)

    return jax.shard_map(
        either,
        mesh=mesh,
        in_specs=(
            P(DP, FSDP, None),
            P(DP, FSDP, None),
            P(DP),
            P(DP),
            P(DP),
            P(AXES, None),
            P(AXES, None),
            P(AXES, None),
            P(AXES, None),
            P(AXES, None),
            P(AXES, None),
            P(AXES, None),
            P(AXES, None),
            P(AXES, None),
            P(AXES),
            P(AXES, None),
            P(AXES, None),
            P(DP, FSDP, None),
        ),
        out_specs=(
            P(DP, FSDP, None),
            P(DP, FSDP, None),
            P(DP, FSDP, None),
            P(AXES, None),
            P(AXES, None),
            P(AXES, None),
            P(AXES, None),
            P(AXES, None),
            P(AXES, None),
            P(AXES, None),
            P(AXES, None),
            P(AXES, None),
            P(AXES),
            P(AXES, None),
            P(AXES, None),
        ),
        check_vma=False,
    )
```
